32 devices in a mesh: fsdp: 8 (over y, x, core), tensor: 4 (over z).
Axes of the slice: x: 2, y: 2, z: 4, core: 2. Of those that a mesh axis runs over, the one named last changes fastest.
Arguments:
- enc_in: bfloat16 [4096, 1024], P(('fsdp', 'tensor')), may hold values from -6 to 6
- dec_in: bfloat16 [4096, 1024], P(('fsdp', 'tensor')), may hold values from -6 to 6
- enc_cot: bfloat16 [4096, 1024], P(('fsdp', 'tensor')), may hold values from -6 to 6
- dec_cot: bfloat16 [4096, 1024], P(('fsdp', 'tensor')), may hold values from -6 to 6
- seq_lens: int32 [12], replicated, may hold values from 1 to 512, 4096 in all
- pic_start: int32 [12, 2], replicated, may hold values from 0 to 255
- pic_len: int32 [12, 2], replicated, may hold values from 1 to 256, as said below
- enc_attn_w: bfloat16 [4, 1024, 1024], P(None, 'fsdp', 'tensor')
- enc_attn_bias: bfloat16 [3, 1024], P(None, 'fsdp'), may hold values from -1.1953125 to 1.1953125
- enc_attn_norm: bfloat16 [2, 1024], P(None, 'fsdp')
- enc_ffn_w: bfloat16 [2, 1024, 4096], P(None, 'fsdp', 'tensor')
- enc_ffn_b1: bfloat16 [1, 4096], P(None, 'fsdp'), may hold values from -1.1953125 to 1.1953125
- enc_ffn_vec: bfloat16 [3, 1024], P(None, 'fsdp')
- self_attn_w: bfloat16 [4, 1024, 1024], P(None, 'fsdp', 'tensor')
- self_attn_bias: bfloat16 [3, 1024], P(None, 'fsdp'), may hold values from -1.1953125 to 1.1953125
- self_attn_norm: bfloat16 [2, 1024], P(None, 'fsdp')
- cross_attn_w: bfloat16 [4, 1024, 1024], P(None, 'fsdp', 'tensor')
- cross_attn_bias: bfloat16 [3, 1024], P(None, 'fsdp'), may hold values from -1.1953125 to 1.1953125
- cross_attn_norm: bfloat16 [2, 1024], P(None, 'fsdp')
- dec_ffn_w: bfloat16 [2, 1024, 4096], P(None, 'fsdp', 'tensor')
- dec_ffn_b1: bfloat16 [1, 4096], P(None, 'fsdp'), may hold values from -1.1953125 to 1.1953125
- dec_ffn_vec: bfloat16 [3, 1024], P(None, 'fsdp')
Outputs:
- enc_out: bfloat16 [4096, 1024], P(('fsdp', 'tensor'))
- dec_out: bfloat16 [4096, 1024], P(('fsdp', 'tensor'))
- enc_in_grad: float32 [4096, 1024], P(('fsdp', 'tensor'))
- dec_in_grad: float32 [4096, 1024], P(('fsdp', 'tensor'))
- enc_attn_w_grad: float32 [4, 1024, 1024], P(None, 'fsdp', 'tensor')
- enc_attn_bias_grad: float32 [3, 1024], P(None, 'fsdp')
- enc_attn_norm_grad: float32 [2, 1024], P(None, 'fsdp')
- enc_ffn_w_grad: float32 [2, 1024, 4096], P(None, 'fsdp', 'tensor')
- enc_ffn_b1_grad: float32 [1, 4096], P(None, 'fsdp')
- enc_ffn_vec_grad: float32 [3, 1024], P(None, 'fsdp')
- self_attn_w_grad: float32 [4, 1024, 1024], P(None, 'fsdp', 'tensor')
- self_attn_bias_grad: float32 [3, 1024], P(None, 'fsdp')
- self_attn_norm_grad: float32 [2, 1024], P(None, 'fsdp')
- cross_attn_w_grad: float32 [4, 1024, 1024], P(None, 'fsdp', 'tensor')
- cross_attn_bias_grad: float32 [3, 1024], P(None, 'fsdp')
- cross_attn_norm_grad: float32 [2, 1024], P(None, 'fsdp')
- dec_ffn_w_grad: float32 [2, 1024, 4096], P(None, 'fsdp', 'tensor')
- dec_ffn_b1_grad: float32 [1, 4096], P(None, 'fsdp')
- dec_ffn_vec_grad: float32 [3, 1024], P(None, 'fsdp')
The draws below stay inside these ranges and needn't reach their ends.
Inputs may be any that keep to these rules, and one draw needn't show every extreme that they name: `seq_lens`: the sequences fill the stream; the longest has exactly 512 tokens. `pic_len`: some piece has exactly 256 tokens; a piece reaching past its sequence's end covers only the tokens inside it.
All inputs are finite; a program needn't handle non-finite values.
Results may differ from the reference program's by a relative error of at most 0.03.
Values may be sent and summed in bfloat16 or wider, within the bound.
No kernel may reach another device: no remote copies, remote signals or barrier semaphores. Data moves between devices by JAX's collectives and lax.ppermute only.
A program may use at most 192 MiB of HBM per device.

```python
import math
import jax
import jax.numpy as jnp
import numpy as np
from jax import lax

D = 1024
HD = 64
FF = 4096
TOK_F = 512
PIC = 256
PICS = 2
TOKENS = 4096
N_SEQ = 12


def projections(key, out_gain):
    normal = jax.random.normal(key, (4, D, D), jnp.float32)
    factor = jnp.array([1.0, 1.0, 1.0, out_gain], jnp.float32) * D ** (-0.5)
    return (normal * factor[:, None, None]).astype(jnp.bfloat16)


def norm_pair(key):
    gain_key, shift_key = jax.random.split(key)
    gains = jax.random.uniform(gain_key, (1, D), jnp.float32, 0.7, 1.3)
    shifts = 0.2 * jax.random.normal(shift_key, (1, D), jnp.float32)
    return jnp.concatenate([gains, shifts], 0)


def feed_forward(key):
    up_key, down_key = jax.random.split(key)
    upward = jax.random.normal(up_key, (1, D, FF), jnp.float32) * D ** (-0.5)
    downward = jax.random.normal(down_key, (1, D, FF), jnp.float32) * (2.0 * FF ** (-0.5))
    return jnp.concatenate([upward, downward], 0).astype(jnp.bfloat16)


def feed_vector(key):
    bias_key, pair_key = jax.random.split(key)
    down_bias = 0.2 * jax.random.normal(bias_key, (1, D), jnp.float32)
    return jnp.concatenate([down_bias, norm_pair(pair_key)], 0).astype(jnp.bfloat16)


def draw_enc_attn_w(key, part):
    return projections(jax.random.fold_in(key, 101), 12.0)


def draw_self_attn_w(key, part):
    return projections(jax.random.fold_in(key, 102), 12.0)


def draw_cross_attn_w(key, part):
    return projections(jax.random.fold_in(key, 103), 12.0)


def draw_enc_attn_norm(key, part):
    return norm_pair(jax.random.fold_in(key, 201)).astype(jnp.bfloat16)


def draw_self_attn_norm(key, part):
    return norm_pair(jax.random.fold_in(key, 202)).astype(jnp.bfloat16)


def draw_cross_attn_norm(key, part):
    return norm_pair(jax.random.fold_in(key, 203)).astype(jnp.bfloat16)


def draw_enc_ffn_w(key, part):
    return feed_forward(jax.random.fold_in(key, 301))


def draw_dec_ffn_w(key, part):
    return feed_forward(jax.random.fold_in(key, 302))


def draw_enc_ffn_vec(key, part):
    return feed_vector(jax.random.fold_in(key, 401))


def draw_dec_ffn_vec(key, part):
    return feed_vector(jax.random.fold_in(key, 402))


def draw_pic_len(key, part):
    values = jax.random.randint(jax.random.fold_in(key, 501), (N_SEQ, PICS), 1, PIC + 1, dtype=jnp.int32)
    return values.at[0, 0].set(PIC)


def with_ends(entries, own_key, low, largest):
    longest = entries.shape.index(max(entries.shape))
    spots = []
    for shift in (0, 1):
        where = [jax.random.randint(jax.random.fold_in(own_key, axis), (), 0, length) for axis, length in enumerate(entries.shape)]
        where[longest] = (where[longest] + shift) % entries.shape[longest]
        spots.append(tuple(where))
    return entries.at[spots[0]].set(low).at[spots[1]].set(largest)


def block_scale(rng, dims, cuts, least, high):
    level = 1.0
    for axis_at, shards_of in cuts:
        draws = jax.random.uniform(jax.random.fold_in(jax.random.fold_in(rng, 6), axis_at), (shards_of,), jnp.float32, least / len(cuts), high / len(cuts))
        level = level * jnp.repeat(jnp.exp(draws), dims[axis_at] // shards_of).reshape((-1,) + (1,) * (len(dims) - 1 - axis_at))
    return level


def length_profile(count, total, reach, slope):
    portions = [(1 << 20) // math.isqrt(rank ** slope) + 1 for rank in range(2, count + 1)]
    rest, given = total - reach - (count - 1), [1] * (count - 1)
    while rest > 0:
        free = [i for i in range(count - 1) if given[i] < reach]
        whole, left = sum([portions[i] for i in free]), rest
        for i in free:
            addition = min(reach - given[i], max(1, left * portions[i] // whole), rest)
            given[i] = given[i] + addition
            rest = rest - addition
    return np.array([reach] + given)


def ragged_sizes(rng, number_of, total, most, lean):
    if number_of == 2:
        one = jax.random.randint(rng, (), max(1, total - most), min(most, total - 1) + 1)
        return jnp.stack([one, total - one])
    lengths = jnp.asarray(length_profile(number_of, total, most, lean), jnp.int32)
    couples = (number_of - 1) // 2
    giver, taker = lengths[1:1 + 2 * couples:2], lengths[2:2 + 2 * couples:2]
    room = jnp.minimum(giver - 1, most - taker)
    passed = jax.random.randint(jax.random.fold_in(rng, 1), (couples,), 0, 1 << 20) % (room + 1)
    lengths = lengths.at[1:1 + 2 * couples:2].set(giver - passed).at[2:2 + 2 * couples:2].set(taker + passed)
    return lengths[jax.random.permutation(jax.random.fold_in(rng, 2), number_of)]


def bell_draw(stream_key, dims, width, bound, cuts=(), kind=jnp.bfloat16):
    values = width * jax.random.normal(stream_key, dims, jnp.float32)
    if cuts:
        values = values * block_scale(stream_key, dims, cuts, -0.22, 0.18)
    return jnp.clip(values, -bound, bound).astype(kind)


def setup_inputs(seed: int = 0) -> dict:
    arg_keys = jax.random.split(jax.random.key(seed), 23)
    enc_in = bell_draw(arg_keys[0], (TOKENS, D), 1.0, 6.0, ((0, 32),))
    dec_in = bell_draw(arg_keys[1], (TOKENS, D), 1.0, 6.0, ((0, 32),))
    enc_cot = bell_draw(arg_keys[2], (TOKENS, D), 1.0, 6.0, ((0, 32),))
    dec_cot = bell_draw(arg_keys[3], (TOKENS, D), 1.0, 6.0, ((0, 32),))
    seq_lens = ragged_sizes(arg_keys[4], N_SEQ, TOKENS, TOK_F, 1).astype(jnp.int32)
    pic_start = with_ends(jax.random.randint(arg_keys[5], (N_SEQ, PICS), 0, TOK_F // 2), jax.random.fold_in(arg_keys[5], 1), 0, (TOK_F // 2) - 1).astype(jnp.int32)
    pic_len = draw_pic_len(jax.random.fold_in(arg_keys[22], 71), 0)
    enc_attn_w = draw_enc_attn_w(jax.random.fold_in(arg_keys[22], 71), 0)
    enc_attn_bias = bell_draw(arg_keys[8], (3, D), 0.2, 1.1953125, ((1, 8),))
    enc_attn_norm = draw_enc_attn_norm(jax.random.fold_in(arg_keys[22], 71), 0)
    enc_ffn_w = draw_enc_ffn_w(jax.random.fold_in(arg_keys[22], 71), 0)
    enc_ffn_b1 = bell_draw(arg_keys[11], (1, FF), 0.2, 1.1953125, ((1, 8),))
    enc_ffn_vec = draw_enc_ffn_vec(jax.random.fold_in(arg_keys[22], 71), 0)
    self_attn_w = draw_self_attn_w(jax.random.fold_in(arg_keys[22], 71), 0)
    self_attn_bias = bell_draw(arg_keys[14], (3, D), 0.2, 1.1953125, ((1, 8),))
    self_attn_norm = draw_self_attn_norm(jax.random.fold_in(arg_keys[22], 71), 0)
    cross_attn_w = draw_cross_attn_w(jax.random.fold_in(arg_keys[22], 71), 0)
    cross_attn_bias = bell_draw(arg_keys[17], (3, D), 0.2, 1.1953125, ((1, 8),))
    cross_attn_norm = draw_cross_attn_norm(jax.random.fold_in(arg_keys[22], 71), 0)
    dec_ffn_w = draw_dec_ffn_w(jax.random.fold_in(arg_keys[22], 71), 0)
    dec_ffn_b1 = bell_draw(arg_keys[20], (1, FF), 0.2, 1.1953125, ((1, 8),))
    dec_ffn_vec = draw_dec_ffn_vec(jax.random.fold_in(arg_keys[22], 71), 0)
    return dict(enc_in=enc_in, dec_in=dec_in, enc_cot=enc_cot, dec_cot=dec_cot, seq_lens=seq_lens, pic_start=pic_start, pic_len=pic_len, enc_attn_w=enc_attn_w, enc_attn_bias=enc_attn_bias, enc_attn_norm=enc_attn_norm, enc_ffn_w=enc_ffn_w, enc_ffn_b1=enc_ffn_b1, enc_ffn_vec=enc_ffn_vec, self_attn_w=self_attn_w, self_attn_bias=self_attn_bias, self_attn_norm=self_attn_norm, cross_attn_w=cross_attn_w, cross_attn_bias=cross_attn_bias, cross_attn_norm=cross_attn_norm, dec_ffn_w=dec_ffn_w, dec_ffn_b1=dec_ffn_b1, dec_ffn_vec=dec_ffn_vec)


@jax.custom_vjp
def low(v):
    return lax.optimization_barrier(v.astype(jnp.bfloat16)).astype(jnp.float32)

@jax.custom_vjp
def low_back(v):
    return v

def low_keep(v):
    return (low(v), None)

def low_pass(kept, grad):
    return (grad,)

def back_keep(v):
    return (v, None)

def back_low(kept, grad):
    return (low(grad),)
low.defvjp(low_keep, low_pass)
low_back.defvjp(back_keep, back_low)

def both_ways(value):
    return low(low_back(value))

def matmul(left, right):
    return jnp.dot(left, right, precision=lax.Precision.HIGHEST, preferred_element_type=jnp.float32)

def norm_rows(residual, gain_row, shift_row):
    center = residual - lax.optimization_barrier(jnp.mean(residual, -1, keepdims=True))
    spread = lax.optimization_barrier(jnp.mean(center * center, -1, keepdims=True))
    return center * lax.rsqrt(spread + 1e-05) * gain_row + shift_row

def token_info(places, seq_lens, pic_start, pic_len, limit):
    starts = (jnp.cumsum(seq_lens) - seq_lens).astype(jnp.int32)
    inside = (starts[None, :] <= places[:, None]).astype(jnp.int32)
    seq_ids = lax.optimization_barrier(jnp.sum(inside, 1)).astype(jnp.int32) - 1
    seq_ids = jnp.where(places < limit, seq_ids, -2).astype(jnp.int32)
    picked = (seq_ids[:, None] == jnp.arange(seq_lens.shape[0], dtype=jnp.int32)[None, :]).astype(jnp.int32)
    offset = (places - lax.optimization_barrier(jnp.sum(picked * starts[None, :], 1))).astype(jnp.int32)
    first_pos = lax.optimization_barrier(jnp.sum(picked[:, :, None] * pic_start[None, :, :], 1)).astype(jnp.int32)
    extent = lax.optimization_barrier(jnp.sum(picked[:, :, None] * pic_len[None, :, :], 1)).astype(jnp.int32)
    member = (offset[:, None] >= first_pos) & (offset[:, None] < first_pos + extent)
    return (places, seq_ids, member)

def visible(query_meta, key_meta, text_mask):
    allowed = query_meta[1][:, None] == key_meta[1][None, :]
    if text_mask:
        shared = key_meta[0][None, :] <= query_meta[0][:, None]
        for picture in range(query_meta[2].shape[1]):
            shared = shared | query_meta[2][:, picture][:, None] & key_meta[2][:, picture][None, :]
        allowed = allowed & shared
    return allowed

def attend(queries, key_rows, value_rows, place_info, text_mask):
    token_total = queries.shape[0]
    block_rows = min(512, TOK_F)
    margin = TOK_F
    head_count = queries.shape[1] // HD
    scaling = HD ** (-0.5)
    padded_keys = jnp.pad(key_rows, ((margin, margin), (0, 0)))
    padded_values = jnp.pad(value_rows, ((margin, margin), (0, 0)))

    def one_block(number):
        first_row = (number * block_rows).astype(jnp.int32)
        window_rows = block_rows + 2 * margin
        query_part = lax.dynamic_slice_in_dim(queries, first_row, block_rows, 0).reshape(block_rows, head_count, HD)
        key_part = lax.dynamic_slice_in_dim(padded_keys, first_row, window_rows, 0).reshape(window_rows, head_count, HD)
        value_part = lax.dynamic_slice_in_dim(padded_values, first_row, window_rows, 0).reshape(window_rows, head_count, HD)
        query_meta = tuple((lax.dynamic_slice_in_dim(member, first_row + margin, block_rows, 0) for member in place_info))
        key_meta = tuple((lax.dynamic_slice_in_dim(member, first_row, window_rows, 0) for member in place_info))
        allowed = visible(query_meta, key_meta, text_mask)
        scores = low_back(jnp.einsum('qhd,khd->hqk', query_part, key_part, precision=lax.Precision.HIGHEST) * scaling)
        scores = jnp.where(allowed[None], scores, -1e+30)
        probs = low(jax.nn.softmax(scores, axis=-1))
        mixture = jnp.einsum('hqk,khd->qhd', probs, value_part, precision=lax.Precision.HIGHEST)
        return mixture.reshape(block_rows, head_count * HD)
    result = lax.map(jax.checkpoint(one_block), jnp.arange(token_total // block_rows, dtype=jnp.int32))
    return result.reshape(token_total, head_count * HD)

def attention_layer(residual, source, projection, biases, norms, place_info, text_mask):
    flat_in = low(residual)
    if source is None:
        key_in = flat_in
    else:
        key_in = low(source)
    queries = both_ways(matmul(flat_in, projection[0]) + biases[0])
    key_rows = both_ways(matmul(key_in, projection[1]))
    value_rows = both_ways(matmul(key_in, projection[2]) + biases[1])
    mixture = both_ways(attend(queries, key_rows, value_rows, place_info, text_mask))
    branch = low_back(matmul(mixture, projection[3].T) + biases[2])
    return norm_rows(residual + branch, norms[0], norms[1])

def ffn_layer(residual, projection, first_bias, vectors):
    flat_in = low(residual)
    before = low_back(matmul(flat_in, projection[0]) + first_bias[0])
    active = low(jax.nn.gelu(before, approximate=False))
    branch = low_back(matmul(active, projection[1].T) + vectors[0])
    return norm_rows(residual + branch, vectors[1], vectors[2])

def reference(enc_in, dec_in, enc_cot, dec_cot, seq_lens, pic_start, pic_len, enc_attn_w, enc_attn_bias, enc_attn_norm, enc_ffn_w, enc_ffn_b1, enc_ffn_vec, self_attn_w, self_attn_bias, self_attn_norm, cross_attn_w, cross_attn_bias, cross_attn_norm, dec_ffn_w, dec_ffn_b1, dec_ffn_vec):
    token_total = enc_in.shape[0]
    places = jnp.arange(token_total + 2 * TOK_F, dtype=jnp.int32) - TOK_F
    place_info = token_info(places, seq_lens, pic_start, pic_len, token_total)
    params = tuple((item.astype(jnp.float32) for item in (enc_attn_w, enc_attn_bias, enc_attn_norm, enc_ffn_w, enc_ffn_b1, enc_ffn_vec, self_attn_w, self_attn_bias, self_attn_norm, cross_attn_w, cross_attn_bias, cross_attn_norm, dec_ffn_w, dec_ffn_b1, dec_ffn_vec)))

    def forward(source_in, target_in, weights):
        hidden = attention_layer(source_in, None, weights[0], weights[1], weights[2], place_info, False)
        encoded = ffn_layer(hidden, weights[3], weights[4], weights[5])
        decoded = attention_layer(target_in, None, weights[6], weights[7], weights[8], place_info, True)
        crossed = attention_layer(decoded, encoded, weights[9], weights[10], weights[11], place_info, False)
        final = ffn_layer(crossed, weights[12], weights[13], weights[14])
        return (encoded, final)
    outputs, pull = jax.vjp(forward, enc_in.astype(jnp.float32), dec_in.astype(jnp.float32), params)
    grad_source, grad_target, grads = pull((enc_cot.astype(jnp.float32), dec_cot.astype(jnp.float32)))
    return (outputs[0].astype(jnp.bfloat16), outputs[1].astype(jnp.bfloat16), grad_source, grad_target, grads[0], grads[1], grads[2], grads[3], grads[4], grads[5], grads[6], grads[7], grads[8], grads[9], grads[10], grads[11], grads[12], grads[13], grads[14])
```

```python
import functools
import jax
import jax.numpy as jnp
from jax import lax
from jax.experimental import pallas as pl
from jax.experimental.pallas import tpu as pltpu
from jax.sharding import PartitionSpec as P

HD = 64
BF = jnp.bfloat16
F32 = jnp.float32


def bits_of(axis):
    count, bit, bits = lax.axis_size(axis), 1, []
    while bit < count:
        bits.append(bit)
        bit *= 2
    return bits


def swap(value, axis, mask):
    return lax.ppermute(value, axis, [(i, i ^ mask) for i in range(lax.axis_size(axis))])


def spread(value, axis, order):
    pieces = {0: value}
    for bit in order:
        for mask in list(pieces):
            pieces[mask | bit] = swap(pieces[mask], axis, bit)
    return [pieces[mask] for mask in sorted(pieces)]


def collect(pieces, axis, order):
    held = dict(enumerate(pieces))
    for bit in order:
        for mask in list(held):
            if mask & (2 * bit - 1):
                continue
            came = swap(held.pop(mask | bit).astype(BF), axis, bit).astype(F32)
            held[mask] = held[mask].astype(F32) + came
    return held[0]


def plane_orders():
    bits = bits_of("fsdp")
    return bits[1:] + bits[:1], bits[1:][::-1] + bits[:1]


def placed(pieces, index):
    lead = pieces[0].shape[0]
    rest = pieces[0].shape[1:]
    count = len(pieces)

    def kernel(index_ref, *refs):
        ins, out, sems = refs[:count], refs[count], refs[count + 1]
        copies = []
        for mask in range(count):
            copy = pltpu.make_async_copy(
                ins[mask], out.at[:, index_ref[0] ^ mask], sems.at[mask]
            )
            copy.start()
            copies.append(copy)
        for copy in copies:
            copy.wait()

    size = lead * count
    for extent in rest:
        size *= extent
    return pl.pallas_call(
        kernel,
        out_shape=jax.ShapeDtypeStruct((lead, count) + rest, pieces[0].dtype),
        in_specs=[pl.BlockSpec(memory_space=pltpu.SMEM)]
        + [pl.BlockSpec(memory_space=pl.ANY)] * count,
        out_specs=pl.BlockSpec(memory_space=pltpu.VMEM),
        scratch_shapes=[pltpu.SemaphoreType.DMA((count,))],
        compiler_params=pltpu.CompilerParams(vmem_limit_bytes=16 * 2**20),
        cost_estimate=pl.CostEstimate(flops=0, bytes_accessed=4 * size, transcendentals=0),
        name="placed",
    )(index[None], *pieces)


def gather_plane(shard, order):
    pieces = spread(shard, "fsdp", order)
    whole = placed(pieces, lax.axis_index("fsdp"))
    return whole.reshape(shard.shape[0], -1, shard.shape[2])


def fold(value, axis, order, at):
    index = lax.axis_index(axis)
    live = bits_of(axis)[::-1]
    for bit in order:
        dim = at + live.index(bit)
        live.remove(bit)
        mine = (index // bit) % 2
        keep = lax.dynamic_index_in_dim(value, mine, dim, False)
        send = lax.dynamic_index_in_dim(value, 1 - mine, dim, False)
        came = swap(send.astype(BF), axis, bit)
        value = keep.astype(F32) + came.astype(F32)
        if live:
            value = value.astype(BF)
    return value


def fold_plane(grads, first):
    bits = bits_of("fsdp")
    order = bits[:1] + (bits[1:] if first else bits[1:][::-1])
    count = lax.axis_size("fsdp")
    rows = grads.shape[1] // count
    split = grads.reshape((grads.shape[0],) + (2,) * len(bits) + (rows, grads.shape[2]))
    return fold(split, "fsdp", order, 1)


def product(left, right):
    return jnp.dot(left, right, preferred_element_type=F32)


def contract_last(left, right):
    return lax.dot_general(left, right, (((1,), (1,)), ((), ())), preferred_element_type=F32)


def contract_first(left, right):
    return lax.dot_general(left, right, (((0,), (0,)), ((), ())), preferred_element_type=F32)


def norm_rows(residual, gain_row, shift_row):
    center = residual - jnp.mean(residual, -1, keepdims=True)
    spread_ = jnp.mean(center * center, -1, keepdims=True)
    return center * lax.rsqrt(spread_ + 1e-05) * gain_row + shift_row


def norm_back(grad, summed, gain_row):
    center = summed - jnp.mean(summed, -1, keepdims=True)
    scale = lax.rsqrt(jnp.mean(center * center, -1, keepdims=True) + 1e-05)
    unit = center * scale
    inner = grad * gain_row
    grad_sum = scale * (
        inner
        - jnp.mean(inner, -1, keepdims=True)
        - unit * jnp.mean(inner * unit, -1, keepdims=True)
    )
    low = grad_sum.astype(BF)
    sums = jnp.stack(
        [jnp.sum(low.astype(F32), 0), jnp.sum(grad * unit, 0), jnp.sum(grad, 0)]
    )
    return grad_sum, low, sums


def exact_gelu(before):
    return jax.nn.gelu(before, approximate=False)


def token_ranges(places, seq_lens, pic_start, pic_len):
    count = seq_lens.shape[0]
    index = jnp.arange(count, dtype=jnp.int32)
    starts = jnp.sum(jnp.where(index[None, :] < index[:, None], seq_lens[None, :], 0), 1)
    stops = starts + seq_lens
    picked = (starts[None, :] <= places[:, None]) & (places[:, None] < stops[None, :])

    def take(values):
        return jnp.sum(jnp.where(picked, values[None, :], 0), 1)

    start, stop = take(starts), take(stops)
    ranges = []
    for k in range(pic_start.shape[1]):
        low = starts + pic_start[:, k]
        high = jnp.minimum(low + pic_len[:, k], stops)
        low, high = take(low), take(high)
        inside = (places >= low) & (places < high)
        ranges += [jnp.where(inside, low, 0), jnp.where(inside, high, 0)]
    return start, stop, ranges


def attend_forward(queries, window, allowed):
    token_count, feature_count = queries.shape
    head_count = feature_count // HD
    scaling = HD ** (-0.5)
    key_length = window.shape[1]
    key_heads = window[0].reshape(key_length, head_count, HD)
    value_heads = window[1].reshape(key_length, head_count, HD)
    query_heads = queries.reshape(token_count, head_count, HD)
    scores = (
        jnp.einsum("qhd,khd->hqk", query_heads, key_heads, preferred_element_type=F32) * scaling
    )
    scores = jnp.where(allowed[None], scores, -1e30)
    height = jnp.max(scores, -1, keepdims=True)
    block_total = height + jnp.log(jnp.sum(jnp.exp(scores - height), -1, keepdims=True))
    weights = jnp.exp(scores - block_total).astype(BF)
    mixture = jnp.einsum("hqk,khd->qhd", weights, value_heads, preferred_element_type=F32)
    return mixture.reshape(token_count, feature_count).astype(BF), block_total


def attend_backward(queries, window, grad_mix, totals, allowed):
    token_count, feature_count = queries.shape
    head_count = feature_count // HD
    scaling = HD ** (-0.5)
    key_length = window.shape[1]
    key_heads = window[0].reshape(key_length, head_count, HD)
    value_heads = window[1].reshape(key_length, head_count, HD)
    query_heads = queries.reshape(token_count, head_count, HD)
    grad_heads = grad_mix.reshape(token_count, head_count, HD)
    scores = (
        jnp.einsum("qhd,khd->hqk", query_heads, key_heads, preferred_element_type=F32) * scaling
    )
    scores = jnp.where(allowed[None], scores, -1e30)
    weights = jnp.exp(scores - totals)
    incoming = jnp.einsum("qhd,khd->hqk", grad_heads, value_heads, preferred_element_type=F32)
    inner = jnp.sum(incoming * weights, -1, keepdims=True)
    grad_scores = (weights * (incoming - inner)).astype(BF)
    block_grad = (
        jnp.einsum("hqk,khd->qhd", grad_scores, key_heads, preferred_element_type=F32) * scaling
    )
    query_grads = block_grad.reshape(token_count, feature_count)
    key_grads = (
        jnp.einsum("hqk,qhd->khd", grad_scores, query_heads, preferred_element_type=F32) * scaling
    )
    value_grads = jnp.einsum(
        "hqk,qhd->khd", weights.astype(BF), grad_heads, preferred_element_type=F32
    )
    window_grads = jnp.stack(
        [
            key_grads.reshape(key_length, feature_count),
            value_grads.reshape(key_length, feature_count),
        ]
    )
    return query_grads.astype(BF), window_grads


def halo(pair):
    peers = lax.axis_size("fsdp")
    up = [(i, i + 1) for i in range(peers - 1)]
    down = [(j, i) for i, j in up]
    before = lax.ppermute(pair, "fsdp", up)
    after = lax.ppermute(pair, "fsdp", down)
    return jnp.concatenate([before, pair, after], 1)


def return_keys(grads, token_count):
    peers = lax.axis_size("fsdp")
    up = [(i, i + 1) for i in range(peers - 1)]
    down = [(j, i) for i, j in up]
    below = grads[:, :token_count].astype(BF)
    owned = grads[:, token_count : 2 * token_count]
    above = grads[:, 2 * token_count :].astype(BF)
    below = lax.ppermute(below, "fsdp", down)
    above = lax.ppermute(above, "fsdp", up)
    return (owned + below.astype(F32) + above.astype(F32)).astype(BF)


def per_device(
    enc_in,
    dec_in,
    enc_cot,
    dec_cot,
    seq_lens,
    pic_start,
    pic_len,
    enc_attn_w,
    enc_attn_bias,
    enc_attn_norm,
    enc_ffn_w,
    enc_ffn_b1,
    enc_ffn_vec,
    self_attn_w,
    self_attn_bias,
    self_attn_norm,
    cross_attn_w,
    cross_attn_bias,
    cross_attn_norm,
    dec_ffn_w,
    dec_ffn_b1,
    dec_ffn_vec,
):
    rows = enc_in.shape[0]
    tensor_size = lax.axis_size("tensor")
    fsdp_size = lax.axis_size("fsdp")
    t_index = lax.axis_index("tensor")
    f_index = lax.axis_index("fsdp")
    tokens = rows * tensor_size
    features = enc_attn_w.shape[2]
    hidden = enc_ffn_w.shape[2]
    t_down = bits_of("tensor")[::-1]
    t_up = bits_of("tensor")
    wide_down = t_down[:-1]
    wide_up = t_up[1:]
    t_masks = range(tensor_size)
    wide_masks = range(0, tensor_size, 2)

    small = [
        enc_attn_bias, enc_attn_norm, enc_ffn_b1, enc_ffn_vec, self_attn_bias, self_attn_norm,
        cross_attn_bias, cross_attn_norm, dec_ffn_b1, dec_ffn_vec,
    ]
    widths = [item.size for item in small]
    packed = jnp.concatenate([item.reshape(-1) for item in small])
    everything = lax.all_gather(packed, "fsdp", axis=0).astype(F32)
    vectors, begin = [], 0
    for item, width in zip(small, widths):
        part = everything[:, begin : begin + width].reshape((fsdp_size,) + item.shape)
        vectors.append(jnp.moveaxis(part, 0, 1).reshape(item.shape[0], -1))
        begin += width
    (
        enc_bias, enc_norm, enc_b1, enc_vec, self_bias, self_norm,
        cross_bias, cross_norm, dec_b1, dec_vec,
    ) = vectors

    def local(row, width, mask=0):
        return lax.dynamic_slice_in_dim(row, (t_index ^ mask) * width, width, 0)

    def rows_at(values, mask):
        return lax.dynamic_slice_in_dim(values, (t_index ^ mask) * rows, rows, 0)

    base = f_index * tokens
    places = base + jnp.arange(tokens, dtype=jnp.int32)
    start, stop, pieces = token_ranges(places, seq_lens, pic_start, pic_len)
    keys = (base - tokens + jnp.arange(3 * tokens, dtype=jnp.int32))[None, :]
    both_mask = (keys >= start[:, None]) & (keys < stop[:, None])
    text_mask = (keys >= start[:, None]) & (keys <= places[:, None])
    for k in range(len(pieces) // 2):
        text_mask = text_mask | (
            (keys >= pieces[2 * k][:, None]) & (keys < pieces[2 * k + 1][:, None])
        )

    first_order, second_order = plane_orders()

    def tensor_pieces(shard):
        return jnp.stack(spread(shard, "tensor", t_down))

    def att_weights(shard):
        qkv = gather_plane(shard[:3], first_order)
        out = gather_plane(tensor_pieces(shard[3]), second_order)
        return qkv, out

    def cross_weights(shard):
        kv_out = gather_plane(
            jnp.concatenate([shard[1:3], tensor_pieces(shard[3])]), first_order
        )
        query = gather_plane(tensor_pieces(shard[0]), second_order)
        return kv_out[:2], kv_out[2:], query

    def ffn_weights(shard):
        wide = spread(shard, "tensor", wide_down)
        wide = [jnp.concatenate([piece[k] for piece in wide], 1)[None] for k in range(2)]
        return gather_plane(wide[0], first_order)[0], gather_plane(wide[1], second_order)[0]

    def later(value, ready):
        return lax.optimization_barrier((value, ready))[0]

    enc_qkv, enc_out_w = att_weights(enc_attn_w)
    enc_up, enc_down = ffn_weights(later(enc_ffn_w, enc_qkv))
    self_qkv, self_out_w = att_weights(later(self_attn_w, enc_up))
    cross_kv, cross_out_w, cross_query = cross_weights(later(cross_attn_w, self_qkv))
    dec_up, dec_down = ffn_weights(later(dec_ffn_w, cross_kv))

    def gather_rows(low):
        pieces_ = spread(low, "tensor", t_down)
        return placed([piece[None] for piece in pieces_], t_index).reshape(tokens, -1)

    def to_rows(values):
        return [rows_at(values, 0)] + [
            swap(rows_at(values, mask), "tensor", mask) for mask in t_masks[1:]
        ]

    def to_heads(pieces_):
        came = [pieces_[0]] + [swap(pieces_[mask], "tensor", mask) for mask in t_masks[1:]]
        return placed([piece[None] for piece in came], t_index).reshape(tokens, features)

    def out_projection(mixed, weight, residual, bias, norms):
        total = residual + bias[2]
        for mask in t_masks:
            total = total + contract_last(mixed[mask], weight[mask])
        return total, norm_rows(total, norms[0], norms[1])

    def self_forward(residual, low, weights, out_w, bias, norms, allowed):
        flat = gather_rows(low)
        queries = (product(flat, weights[0]) + local(bias[0], features)).astype(BF)
        key_rows = product(flat, weights[1]).astype(BF)
        value_rows = (product(flat, weights[2]) + local(bias[1], features)).astype(BF)
        window = halo(jnp.stack([key_rows, value_rows]))
        mixture, totals = attend_forward(queries, window, allowed)
        mixed = to_rows(mixture)
        summed, out = out_projection(mixed, out_w, residual, bias, norms)
        return out, (flat, queries, window, totals, mixed, summed)

    def cross_forward(residual, low, source_low, kv_w, out_w, query_w, bias, norms, allowed):
        flat = gather_rows(source_low)
        asked = [
            (product(low, query_w[mask]) + local(bias[0], features, mask)).astype(BF)
            for mask in t_masks
        ]
        queries = to_heads(asked)
        key_rows = product(flat, kv_w[0]).astype(BF)
        value_rows = (product(flat, kv_w[1]) + local(bias[1], features)).astype(BF)
        window = halo(jnp.stack([key_rows, value_rows]))
        mixture, totals = attend_forward(queries, window, allowed)
        mixed = to_rows(mixture)
        summed, out = out_projection(mixed, out_w, residual, bias, norms)
        return out, (flat, low, queries, window, totals, mixed, summed)

    def ffn_forward(residual, low, up, down, first, vec):
        pair = jnp.concatenate([low, swap(low, "tensor", 1)], 0)
        row = jnp.concatenate([local(first[0], hidden, mask) for mask in wide_masks])
        before = product(pair, up) + row
        active = exact_gelu(before).astype(BF)
        term = contract_last(active, down)
        summed = residual + vec[0] + term[:rows] + swap(term[rows:].astype(BF), "tensor", 1)
        return norm_rows(summed, vec[1], vec[2]), (pair, before, active, summed)

    def ffn_backward(grad_out, kept, up, down, vec):
        pair, before, active, summed = kept
        grad_sum, low, sums = norm_back(grad_out, summed, vec[1])
        grad_pair = jnp.concatenate([low, swap(low, "tensor", 1)], 0)
        grad_active = product(grad_pair, down)
        unused, pull = jax.vjp(exact_gelu, before)
        grad_before = pull(grad_active)[0].astype(BF)
        term = contract_last(grad_before, up)
        grad_in = grad_sum + term[:rows] + swap(term[rows:].astype(BF), "tensor", 1)
        grad_up = contract_first(pair, grad_before).astype(BF)
        grad_down = contract_first(grad_pair, active).astype(BF)
        first_sum = jnp.sum(grad_before.astype(F32), 0)
        return grad_in, (grad_up, grad_down), first_sum, sums

    def ffn_weight_grad(pair):
        done = []
        for k in range(2):
            own = fold_plane(pair[k][None], k == 0)[0]
            parts = [
                own[:, j * hidden : (j + 1) * hidden] for j in range(len(wide_masks))
            ]
            done.append(collect_wide(parts))
        return jnp.stack(done)

    def collect_wide(parts):
        held = {2 * j: part for j, part in enumerate(parts)}
        for bit in wide_up:
            for mask in list(held):
                if mask & (2 * bit - 1):
                    continue
                came = swap(held.pop(mask | bit).astype(BF), "tensor", bit).astype(F32)
                held[mask] = held[mask] + came
        return held[0]

    def out_grads(low, mixed):
        return jnp.stack([contract_first(low, piece).astype(BF) for piece in mixed])

    def att_core_back(grad_out, kept, out_w, norms, allowed):
        queries, window, totals, mixed, summed = kept
        grad_sum, low, sums = norm_back(grad_out, summed, norms[0])
        grad_mixed = [product(low, out_w[mask]).astype(BF) for mask in t_masks]
        grad_mix = to_heads(grad_mixed)
        grad_queries, grad_window = attend_backward(queries, window, grad_mix, totals, allowed)
        returned = return_keys(grad_window, tokens)
        return grad_sum, low, sums, grad_queries, returned[0], returned[1]

    def share(terms):
        blocks = []
        for mask in t_masks:
            total = 0.0
            for left, right in terms:
                total = total + contract_last(rows_at(left, mask), right)
            blocks.append(total)
        return collect(blocks, "tensor", t_up)

    def self_backward(grad_out, kept, weights, out_w, norms, allowed):
        flat, queries, window, totals, mixed, summed = kept
        grad_sum, low, sums, dq, dk, dv = att_core_back(
            grad_out, (queries, window, totals, mixed, summed), out_w, norms, allowed
        )
        grad_in = grad_sum + share([(dq, weights[0]), (dk, weights[1]), (dv, weights[2])])
        grad_w = jnp.stack([contract_first(flat, g).astype(BF) for g in (dq, dk, dv)])
        return grad_in, grad_w, out_grads(low, mixed), (sums, dq, dv)

    def cross_backward(grad_out, kept, kv_w, out_w, query_w, norms, allowed):
        flat, low_in, queries, window, totals, mixed, summed = kept
        grad_sum, low, sums, dq, dk, dv = att_core_back(
            grad_out, (queries, window, totals, mixed, summed), out_w, norms, allowed
        )
        grad_source = share([(dk, kv_w[0]), (dv, kv_w[1])])
        asked = to_rows(dq)
        grad_in = grad_sum
        for mask in t_masks:
            grad_in = grad_in + contract_last(asked[mask], query_w[mask])
        grad_kv = jnp.stack([contract_first(flat, g).astype(BF) for g in (dk, dv)])
        grad_query = jnp.stack([contract_first(low_in, piece).astype(BF) for piece in asked])
        return grad_in, grad_source, grad_kv, out_grads(low, mixed), grad_query, (sums, dq, dv)

    def tensor_sum(parts):
        return collect([parts[mask] for mask in t_masks], "tensor", t_up)

    def att_weight_grad(grad_w, grad_o):
        own = fold_plane(grad_w, True)
        out = tensor_sum(fold_plane(grad_o, False))
        return jnp.concatenate([own, out[None]])

    def cross_weight_grad(grad_kv, grad_o, grad_q):
        first = fold_plane(jnp.concatenate([grad_kv, grad_o]), True)
        out = tensor_sum(first[2:])
        query = tensor_sum(fold_plane(grad_q, False))
        return jnp.concatenate([query[None], first[:2], out[None]])

    enc_rows = enc_in.astype(F32)
    dec_rows = dec_in.astype(F32)
    hid, kept_enc = self_forward(
        enc_rows, enc_in, enc_qkv, enc_out_w, enc_bias, enc_norm, both_mask
    )
    encoded, kept_enc_ffn = ffn_forward(hid, hid.astype(BF), enc_up, enc_down, enc_b1, enc_vec)
    encoded_low = encoded.astype(BF)
    decoded, kept_self = self_forward(
        dec_rows, dec_in, self_qkv, self_out_w, self_bias, self_norm, text_mask
    )
    crossed, kept_cross = cross_forward(
        decoded, decoded.astype(BF), encoded_low, cross_kv, cross_out_w, cross_query,
        cross_bias, cross_norm, both_mask,
    )
    final, kept_dec_ffn = ffn_forward(
        crossed, crossed.astype(BF), dec_up, dec_down, dec_b1, dec_vec
    )

    grad_crossed, dec_pair, dec_first_sum, dec_sums = ffn_backward(
        dec_cot.astype(F32), kept_dec_ffn, dec_up, dec_down, dec_vec
    )
    dec_ffn_grad = ffn_weight_grad(dec_pair)
    grad_decoded, grad_encoded, cross_kv_g, cross_o_g, cross_q_g, cross_small = cross_backward(
        grad_crossed, kept_cross, cross_kv, cross_out_w, cross_query, cross_norm, both_mask
    )
    cross_grad = cross_weight_grad(cross_kv_g, cross_o_g, cross_q_g)
    grad_target, self_g, self_o_g, self_small = self_backward(
        grad_decoded, kept_self, self_qkv, self_out_w, self_norm, text_mask
    )
    self_grad = att_weight_grad(self_g, self_o_g)
    grad_hid, enc_pair, enc_first_sum, enc_sums = ffn_backward(
        enc_cot.astype(F32) + grad_encoded, kept_enc_ffn, enc_up, enc_down, enc_vec
    )
    enc_ffn_grad = ffn_weight_grad(enc_pair)
    grad_source, enc_g, enc_o_g, enc_small = self_backward(
        grad_hid, kept_enc, enc_qkv, enc_out_w, enc_norm, both_mask
    )
    enc_grad = att_weight_grad(enc_g, enc_o_g)

    def at_own(values, width, mask, length):
        return lax.dynamic_update_slice_in_dim(
            jnp.zeros((length,), F32), values, (t_index ^ mask) * width, 0
        )

    def att_small(parts):
        sums, dq, dv = parts
        width = sums.shape[1]
        query = at_own(jnp.sum(dq.astype(F32), 0), features, 0, width)
        value = at_own(jnp.sum(dv.astype(F32), 0), features, 0, width)
        return jnp.stack([query, value, sums[0]]), sums[1:]

    def ffn_small(first_sum, sums):
        length = hidden * tensor_size
        row = jnp.zeros((length,), F32)
        for j, mask in enumerate(wide_masks):
            part = first_sum[j * hidden : (j + 1) * hidden]
            row = lax.dynamic_update_slice_in_dim(row, part, (t_index ^ mask) * hidden, 0)
        return row[None], sums

    def reduce_small(items):
        flat = jnp.concatenate(
            [
                jnp.moveaxis(item.reshape(item.shape[0], fsdp_size, -1), 1, 0).reshape(
                    fsdp_size, -1
                )
                for item in items
            ],
            1,
        )
        bits = bits_of("fsdp")
        index = f_index
        live = flat
        for bit in bits[::-1]:
            half = live.shape[0] // 2
            mine = (index // bit) % 2
            keep = lax.dynamic_slice_in_dim(live, mine * half, half, 0)
            send = lax.dynamic_slice_in_dim(live, (1 - mine) * half, half, 0)
            live = keep + swap(send, "fsdp", bit)
        live = live[0]
        for bit in t_up:
            live = live + swap(live, "tensor", bit)
        out, begin_ = [], 0
        for item in items:
            width = item.size // fsdp_size
            out.append(live[begin_ : begin_ + width].reshape(item.shape[0], -1))
            begin_ += width
        return out

    dec_small = ffn_small(dec_first_sum, dec_sums)
    enc_f_small = ffn_small(enc_first_sum, enc_sums)
    early = reduce_small(
        [*att_small(self_small), *att_small(cross_small), *dec_small, *enc_f_small]
    )
    late = reduce_small([*att_small(enc_small)])

    return (
        encoded_low,
        final.astype(BF),
        grad_source,
        grad_target,
        enc_grad,
        late[0],
        late[1],
        enc_ffn_grad,
        early[6],
        early[7],
        self_grad,
        early[0],
        early[1],
        cross_grad,
        early[2],
        early[3],
        dec_ffn_grad,
        early[4],
        early[5],
    )


def solution(mesh):
    rows = P(("fsdp", "tensor"), None)
    weight = P(None, "fsdp", "tensor")
    vector = P(None, "fsdp")
    att, ffn = (weight, vector, vector), (weight, vector, vector)
    in_specs = (rows,) * 4 + (P(),) * 3 + (att + ffn + att + att + ffn)
    out_specs = (rows,) * 4 + (att + ffn + att + att + ffn)
    return jax.shard_map(
        per_device, mesh=mesh, in_specs=in_specs, out_specs=out_specs, check_vma=False
    )
```

```python
import functools
import jax
import jax.numpy as jnp
from jax import lax
from jax.experimental import pallas as pl
from jax.experimental.pallas import tpu as pltpu
from jax.sharding import PartitionSpec as P

HD = 64
BF = jnp.bfloat16
F32 = jnp.float32
PACE = 30000000000


def bits_of(axis):
    count, bit, bits = lax.axis_size(axis), 1, []
    while bit < count:
        bits.append(bit)
        bit *= 2
    return bits


def swap(value, axis, mask):
    return lax.ppermute(value, axis, [(i, i ^ mask) for i in range(lax.axis_size(axis))])


def join(value, *ready):
    return lax.optimization_barrier((value, ready))[0] if ready else value


def spread(value, axis, order, gates=()):
    pieces = {0: value}
    for k, bit in enumerate(order):
        for mask in list(pieces):
            piece = pieces[mask]
            if mask and k < len(gates):
                piece = join(piece, *gates[k])
            pieces[mask | bit] = swap(piece, axis, bit)
    if len(gates) > len(order):
        return [pieces[0]] + [join(pieces[mask], *gates[-1]) for mask in sorted(pieces)[1:]]
    return [pieces[mask] for mask in sorted(pieces)]


def total(items):
    out = items[0].astype(F32)
    for item in items[1:]:
        out = out + item.astype(F32)
    return out


def plane_orders():
    bits = bits_of("fsdp")
    return bits[1:] + bits[:1], bits[1:][::-1] + bits[:1]


def placed(parts, index, splits):
    arrays = [array for array, masks in parts]
    total = sum(len(masks) for array, masks in parts)
    rows, cols = arrays[0].shape[2:]

    def kernel(index_ref, *refs):
        ins, outs, sems = refs[: len(parts)], refs[len(parts) : -1], refs[-1]
        copies = []
        for (array, masks), ref in zip(parts, ins):
            for at, mask in enumerate(masks):
                first = 0
                for out, width in zip(outs, splits):
                    copy = pltpu.make_async_copy(
                        ref.at[at, first : first + width],
                        out.at[:, index_ref[0] ^ mask],
                        sems.at[len(copies)],
                    )
                    copy.start()
                    copies.append(copy)
                    first += width
        for copy in copies:
            copy.wait()

    outs = pl.pallas_call(
        kernel,
        out_shape=[
            jax.ShapeDtypeStruct((width, total, rows, cols), arrays[0].dtype) for width in splits
        ],
        in_specs=[pl.BlockSpec(memory_space=pltpu.SMEM)]
        + [pl.BlockSpec(memory_space=pl.ANY)] * len(arrays),
        out_specs=[pl.BlockSpec(memory_space=pltpu.VMEM)] * len(splits),
        scratch_shapes=[pltpu.SemaphoreType.DMA((total * len(splits),))],
        compiler_params=pltpu.CompilerParams(vmem_limit_bytes=32 * 2**20),
        cost_estimate=pl.CostEstimate(flops=PACE, bytes_accessed=1, transcendentals=0),
        name="placed",
    )(index[None], *arrays)
    return [out.reshape(out.shape[0], -1, cols) for out in outs]


def gather_plane(shard, order, splits):
    return Gather(shard[None], order, splits).result()


class Gather:
    def __init__(self, held, order, splits):
        self.held, self.masks, self.order, self.splits = held, [0], list(order), splits
        self.came = None

    def take(self, gate):
        if self.came is not None:
            came = join(self.came, *gate)
            self.held = jnp.concatenate([self.held, came], 0)
            self.masks = self.masks + [mask | self.bit for mask in self.masks]

    def hop(self, *gate):
        self.take(gate)
        self.bit = self.order.pop(0)
        self.came = swap(self.held, "fsdp", self.bit)
        return self.came

    def result(self):
        while self.order:
            self.hop()
        parts = [(self.held, self.masks), (self.came, [mask | self.bit for mask in self.masks])]
        return placed(parts, lax.axis_index("fsdp"), self.splits)


class Spread:
    def __init__(self, value, axis, bits):
        self.axis, self.pieces, self.level, self.last = axis, {0: value}, 0, len(bits)
        self.masks = [m for m in range(lax.axis_size(axis)) if m & ~sum(bits) == 0]

    def hop(self, *gate):
        self.level += 1
        new = []
        for mask in self.masks[::-1]:
            if mask.bit_count() == self.level:
                low = mask & -mask
                piece = self.pieces[mask ^ low]
                if mask != low:
                    piece = join(piece, *gate)
                self.pieces[mask] = swap(piece, self.axis, low)
                new.append(self.pieces[mask])
        return new

    def result(self, *gate):
        while self.level < self.last:
            self.hop()
        return [join(self.pieces[m], *(gate if m else ())) for m in self.masks]


class Share:
    def __init__(self, pieces, axis, bits):
        self.axis, self.held, self.came, self.level = axis, dict(enumerate(pieces)), {}, len(bits)
        self.terms = [pieces[0]]

    def hop(self, *gate):
        for mask, arrays in self.came.items():
            for array in arrays:
                self.held[mask] = self.held[mask].astype(F32) + join(array, *gate).astype(F32)
        self.came = {}
        new = []
        for mask in sorted(self.held)[::-1]:
            if mask and (mask.bit_count() == self.level or mask == 1):
                low = mask & -mask
                came = swap(self.held.pop(mask).astype(BF), self.axis, low)
                if mask == low:
                    self.terms.append(came)
                else:
                    self.came.setdefault(mask ^ low, []).append(came)
                new.append(came)
        self.level -= 1
        return new

    def result(self):
        while self.level > 0:
            self.hop()
        return self.terms


class Fold:
    def __init__(self, keep, send, order, at):
        bits = bits_of("fsdp")
        self.live, self.order, self.at = bits[1:][::-1], list(order), at
        split = keep.shape[:at] + (2,) * len(self.live) + keep.shape[at + 1 :]
        self.value, self.sent, self.bit = keep.reshape(split), send.reshape(split), bits[0]

    def hop(self, *gate):
        self.came = swap(join(self.sent, *gate), "fsdp", self.bit)
        return self.came

    def next(self, *gate):
        bit = self.order.pop(0)
        dim = self.at + self.live.index(bit)
        self.live.remove(bit)
        mine = (lax.axis_index("fsdp") // bit) % 2
        value, came = self.value, join(self.came, *gate)

        def pick(which):
            return lax.dynamic_index_in_dim(value, which, dim, False).astype(
                F32
            ) + lax.dynamic_index_in_dim(came, which, dim, False).astype(F32)

        self.value, self.sent, self.bit = pick(mine).astype(BF), pick(1 - mine).astype(BF), bit
        return self.hop()

    def result(self, *gate):
        while self.order:
            self.next(*gate)
            gate = ()
        return self.value.astype(F32) + join(self.came, *gate).astype(F32)


MIB = 2**20
HEAD_SCALE = HD ** (-0.5)


def run(kernel, scalars, arrays, outs, scratch, name, flops, grid=None, in_blocks=None, out_blocks=None):
    arrays = list(arrays)
    whole = pl.BlockSpec(memory_space=pltpu.VMEM)
    in_specs = [pl.BlockSpec(memory_space=pltpu.SMEM)] * len(scalars)
    in_specs += in_blocks if in_blocks else [whole] * len(arrays)
    extra = {"grid": grid} if grid else {}
    return pl.pallas_call(
        kernel,
        out_shape=[jax.ShapeDtypeStruct(shape, kind) for shape, kind in outs],
        in_specs=in_specs,
        out_specs=out_blocks if out_blocks else [whole] * len(outs),
        scratch_shapes=scratch,
        compiler_params=pltpu.CompilerParams(vmem_limit_bytes=40 * MIB),
        cost_estimate=pl.CostEstimate(
            flops=PACE, bytes_accessed=1, transcendentals=0
        ),
        name=name,
        **extra,
    )(*scalars, *arrays)


def dot(left, right, dims):
    return lax.dot_general(left, right, ((dims[:1], dims[1:]), ((), ())), preferred_element_type=F32)


def head_mask(rows, which, level):
    lane = lax.broadcasted_iota(jnp.int32, (rows, 128), 1)
    return jnp.where(lane // HD == which, level, 0.0).astype(BF)


def tile_allowed(meta, first, size, columns, ranges):
    place = lax.broadcasted_iota(jnp.int32, (size, columns), 0) + first
    allowed = (place >= meta[0:1]) & (place < meta[1:2])
    for k in range(1, ranges):
        allowed = allowed | ((place >= meta[2 * k : 2 * k + 1]) & (place < meta[2 * k + 1 : 2 * k + 2]))
    return allowed


def multiple(value, of):
    return pl.multiple_of(value, of)


def place_rows(ref, pieces, t_index):
    rows = pieces[0].shape[0]
    for mask, piece in enumerate(pieces):
        ref[pl.ds(multiple((t_index ^ mask) * rows, rows), rows), :] = piece[...]


def attend(queries, windows, meta, bounds, t_index, count, ranges):
    tokens, width = queries.shape
    heads, rows = width // HD, tokens // count
    block = min(256, tokens)
    tiles = 3 * tokens // block

    def kernel(bounds_ref, t_ref, meta_ref, q_ref, b_ref, w_ref, a_ref, *rest):
        o_refs, (ot_ref, lse_ref, keys, v_t, held, acc, nat) = rest[:count], rest[count:]
        for j, ref in enumerate((b_ref, w_ref, a_ref)):
            keys[j * tokens : (j + 1) * tokens, :] = ref[0]
            v_t[:, j * tokens : (j + 1) * tokens] = ref[1].T
        for i in range(tokens // block):
            low, high = bounds_ref[2 * i], bounds_ref[2 * i + 1]
            span = slice(i * block, (i + 1) * block)
            info = meta_ref[:, span]
            asked = []
            for h in range(heads):
                lanes = slice(h // 2 * 128, h // 2 * 128 + 128)
                asked.append(q_ref[span, lanes] * head_mask(block, h % 2, HEAD_SCALE))

            def scores(k, tops):
                first = multiple(k * block, block)
                allowed = tile_allowed(info, first, block, block, ranges)
                out = []
                for h in range(heads):
                    lanes = slice(h // 2 * 128, h // 2 * 128 + 128)
                    s = dot(keys[pl.ds(first, block), lanes], asked[h], (1, 1))
                    s = jnp.where(allowed, s, -1e30)
                    held[h, k] = s
                    out.append(jnp.maximum(tops[h], jnp.max(s, 0, keepdims=True)))
                return tuple(out)

            tops = lax.fori_loop(
                low, high, scores, tuple(jnp.full((1, block), -1e30, F32) for h in range(heads))
            )
            acc[...] = jnp.zeros_like(acc)

            def mixes(k, sums):
                first = multiple(k * block, block)
                out = []
                for h in range(heads):
                    p = jnp.exp(held[h, k] - tops[h])
                    out.append(sums[h] + jnp.sum(p, 0, keepdims=True))
                    some = slice(h * HD, (h + 1) * HD)
                    acc[some, :] += dot(v_t[some, pl.ds(first, block)], p.astype(BF), (1, 0))
                return tuple(out)

            sums = lax.fori_loop(
                low, high, mixes, tuple(jnp.zeros((1, block), F32) for h in range(heads))
            )
            for h in range(heads):
                some = slice(h * HD, (h + 1) * HD)
                acc[some, :] = acc[some, :] / sums[h]
                lse_ref[h : h + 1, span] = tops[h] + jnp.log(sums[h])
            ot_ref[:, span] = acc[...]
            nat[span, :] = acc[...].T.astype(BF)
        for mask in range(count):
            o_refs[mask][...] = nat[pl.ds(multiple((t_ref[0] ^ mask) * rows, rows), rows), :]

    out = run(
        kernel,
        [bounds, t_index],
        [meta, queries, *windows],
        [((rows, width), BF)] * count + [((width, tokens), F32), ((heads, tokens), F32)],
        [
            pltpu.VMEM((3 * tokens, width), BF),
            pltpu.VMEM((width, 3 * tokens), BF),
            pltpu.VMEM((heads, tiles, block, block), F32),
            pltpu.VMEM((width, block), F32),
            pltpu.VMEM((tokens, width), BF),
        ],
        "attend",
        4 * tokens * 3 * tokens * width * 4,
    )
    return out[:count], out[count], out[count + 1]


def attend_back(queries, windows, grads, mixed_t, totals, meta, bounds, t_index, count, ranges):
    tokens, width = queries.shape
    heads, rows = width // HD, tokens // count
    block = min(256, tokens)

    def kernel(bounds_ref, t_ref, meta_ref, q_ref, b_ref, w_ref, a_ref, ot_ref, lse_ref, *rest):
        g_refs = rest[:count]
        dq_ref, db_ref, dw_ref, da_ref, nat, keys, values, k_t, dk, dv, acc = rest[count:]
        place_rows(nat, g_refs, t_ref[0])
        for j, ref in enumerate((b_ref, w_ref, a_ref)):
            part = slice(j * tokens, (j + 1) * tokens)
            keys[part, :] = ref[0]
            values[part, :] = ref[1]
            k_t[:, part] = ref[0].T
        dk[...] = jnp.zeros_like(dk)
        dv[...] = jnp.zeros_like(dv)
        for i in range(tokens // block):
            low, high = bounds_ref[2 * i], bounds_ref[2 * i + 1]
            span = slice(i * block, (i + 1) * block)
            info = meta_ref[:, span]
            g_t = nat[span, :].astype(F32).T
            asked, given, inner = [], [], []
            for h in range(heads):
                lanes = slice(h // 2 * 128, h // 2 * 128 + 128)
                some = slice(h * HD, (h + 1) * HD)
                asked.append(q_ref[span, lanes] * head_mask(block, h % 2, HEAD_SCALE))
                given.append(nat[span, lanes] * head_mask(block, h % 2, 1.0))
                inner.append(jnp.sum(g_t[some] * ot_ref[some, span], 0, keepdims=True))
            acc[...] = jnp.zeros_like(acc)

            def step(k, carry):
                first = multiple(k * block, block)
                at = pl.ds(first, block)
                allowed = tile_allowed(info, first, block, block, ranges)
                for h in range(heads):
                    lanes = slice(h // 2 * 128, h // 2 * 128 + 128)
                    some = slice(h * HD, (h + 1) * HD)
                    s = dot(keys[at, lanes], asked[h], (1, 1))
                    p = jnp.exp(jnp.where(allowed, s, -1e30) - lse_ref[h : h + 1, span])
                    dp = dot(values[at, lanes], given[h], (1, 1))
                    ds = (p * (dp - inner[h])).astype(BF)
                    dv[at, lanes] += dot(p.astype(BF), given[h], (1, 0))
                    dk[at, lanes] += dot(ds, asked[h], (1, 0))
                    acc[some, :] += dot(k_t[some, at], ds, (1, 0))
                return carry

            lax.fori_loop(low, high, step, 0)
            dq_ref[span, :] = (acc[...] * HEAD_SCALE).T.astype(BF)
        for j, ref in enumerate((db_ref, dw_ref, da_ref)):
            part = slice(j * tokens, (j + 1) * tokens)
            ref[0] = dk[part, :].astype(ref.dtype)
            ref[1] = dv[part, :].astype(ref.dtype)

    pair = (2, tokens, width)
    return run(
        kernel,
        [bounds, t_index],
        [meta, queries, *windows, mixed_t, totals, *grads],
        [((tokens, width), BF), (pair, BF), (pair, F32), (pair, BF)],
        [
            pltpu.VMEM((tokens, width), BF),
            pltpu.VMEM((3 * tokens, width), BF),
            pltpu.VMEM((3 * tokens, width), BF),
            pltpu.VMEM((width, 3 * tokens), BF),
            pltpu.VMEM((3 * tokens, width), F32),
            pltpu.VMEM((3 * tokens, width), F32),
            pltpu.VMEM((width, block), F32),
        ],
        "attend_back",
        10 * tokens * 3 * tokens * width * 4,
    )


def project(pieces, weights, local, lines, t_index):
    count = len(pieces)
    rows, depth = pieces[0].shape
    tokens, width = rows * count, weights.shape[2]
    outputs = weights.shape[0]

    def kernel(t_ref, w_ref, local_ref, *rest):
        x_ref = rest[count]
        place_rows(x_ref, rest[:count], t_ref[0])
        x = x_ref[...]
        done = []
        for k, line in enumerate(lines):
            value = dot(x, w_ref[k], (1, 0))
            if line is not None:
                value = value + local_ref[0, line : line + 1, :]
            done.append(value.astype(BF))
        if outputs == 3:
            rest[count + 2][...] = done[0]
        rest[count + 1][0] = done[-2]
        rest[count + 1][1] = done[-1]

    outs = [((tokens, depth), BF), ((2, tokens, width), BF)]
    if outputs == 3:
        outs.append(((tokens, width), BF))
    return run(
        kernel, [t_index], [weights, local, *pieces], outs, [], "project",
        2 * tokens * depth * width * outputs,
    )


def project_rows(low, weight, local, line):
    count, depth, width = weight.shape

    def kernel(x_ref, w_ref, local_ref, *outs):
        for mask in range(count):
            outs[mask][...] = (
                dot(x_ref[...], w_ref[mask], (1, 0)) + local_ref[mask, line : line + 1, :]
            ).astype(BF)

    return run(
        kernel, [], [low, weight, local], [((low.shape[0], width), BF)] * count, [],
        "project_rows", 2 * low.shape[0] * depth * width * count,
    )


def normed(total, gain, shift):
    center = total - jnp.mean(total, -1, keepdims=True)
    scale = lax.rsqrt(jnp.mean(center * center, -1, keepdims=True) + 1e-05)
    return center * scale * gain + shift


def out_norm(mixed, weight, residual, vectors, line):
    count, depth, width = weight.shape
    shape = residual.shape

    def kernel(w_ref, r_ref, v_ref, *rest):
        total = r_ref[...].astype(F32) + v_ref[line : line + 1, :]
        for mask in range(count):
            total = total + dot(rest[mask][...], w_ref[mask], (1, 1))
        sum_ref, out_ref, low_ref = rest[count:]
        sum_ref[...] = total
        out = normed(total, v_ref[line + 1 : line + 2, :], v_ref[line + 2 : line + 3, :])
        out_ref[...] = out
        low_ref[...] = out.astype(BF)

    return run(
        kernel, [], [weight, residual, vectors, *mixed], [(shape, F32), (shape, F32), (shape, BF)],
        [], "out_norm", 2 * shape[0] * depth * width * count,
    )


def add_norm(terms, vectors, line):
    shape = terms[0].shape

    def kernel(v_ref, *rest):
        total = v_ref[line : line + 1, :]
        for ref in rest[: len(terms)]:
            total = total + ref[...].astype(F32)
        sum_ref, low_ref = rest[len(terms) :]
        sum_ref[...] = total
        out = normed(total, v_ref[line + 1 : line + 2, :], v_ref[line + 2 : line + 3, :])
        low_ref[...] = out.astype(BF)

    return run(
        kernel, [], [vectors, *terms], [(shape, F32), (shape, BF)], [], "add_norm", 1e6
    )


def ffn_blocks(views, rows, depth, hidden):
    step = min(512 // len(views) if len(views) < 4 else 128, hidden)
    row = pl.BlockSpec((rows, depth), lambda j: (0, 0))

    def weight(index):
        return pl.BlockSpec((1, depth, step), lambda j: (index, 0, j))

    tall = pl.BlockSpec((len(views), 2 * rows, step), lambda j: (0, 0, j))
    line = pl.BlockSpec((len(views), 1, step), lambda j: (0, 0, j))
    specs, arrays = [], []
    for array, up, down in views:
        specs += [weight(up), weight(down)]
        arrays += [array, array]
    return step, row, tall, line, specs, arrays


def ffn_up_down(own, other, views, first):
    rows, depth = own.shape
    hidden, count = views[0][0].shape[2], len(views)
    step, row, tall, line, specs, arrays = ffn_blocks(views, rows, depth, hidden)

    def kernel(own_ref, other_ref, b_ref, *rest):
        weights, (act_ref, slope_ref, keep_ref, send_ref, pair, acc) = rest[:-6], rest[-6:]
        j = pl.program_id(0)

        @pl.when(j == 0)
        def _():
            pair[:rows, :] = own_ref[...]
            pair[rows:, :] = other_ref[...]

        total = None
        for v in range(count):
            u = dot(pair[...], weights[2 * v][0], (1, 0)) + b_ref[v]
            phi = 0.5 * (1.0 + lax.erf(u * 0.7071067811865476))
            act = (u * phi).astype(BF)
            act_ref[v] = act
            slope_ref[v] = (phi + u * 0.3989422804014327 * jnp.exp(-0.5 * u * u)).astype(BF)
            term = dot(act, weights[2 * v + 1][0], (1, 1))
            total = term if total is None else total + term

        @pl.when(j == 0)
        def _():
            acc[...] = total

        @pl.when(j > 0)
        def _():
            acc[...] += total

        @pl.when(j == hidden // step - 1)
        def _():
            keep_ref[...] = acc[:rows, :]
            send_ref[...] = acc[rows:, :].astype(BF)

    wide = (count, 2 * rows, hidden)
    return run(
        kernel, [], [own, other, first, *arrays],
        [(wide, BF), (wide, BF), ((rows, depth), F32), ((rows, depth), BF)],
        [pltpu.VMEM((2 * rows, depth), BF), pltpu.VMEM((2 * rows, depth), F32)],
        "ffn_up_down", 8 * rows * depth * hidden * count, (hidden // step,),
        [row, row, line] + specs, [tall, tall, row, row],
    )


def ffn_down_up(own, other, views, slope):
    rows, depth = own.shape
    hidden, count = views[0][0].shape[2], len(views)
    step, row, tall, line, specs, arrays = ffn_blocks(views, rows, depth, hidden)

    def kernel(own_ref, other_ref, slope_ref, *rest):
        weights, (du_ref, sum_ref, keep_ref, send_ref, pair, acc) = rest[:-6], rest[-6:]
        j = pl.program_id(0)

        @pl.when(j == 0)
        def _():
            pair[:rows, :] = own_ref[...]
            pair[rows:, :] = other_ref[...]

        total = None
        for v in range(count):
            du = (dot(pair[...], weights[2 * v + 1][0], (1, 0)) * slope_ref[v].astype(F32)).astype(BF)
            du_ref[v] = du
            sum_ref[v] = jnp.sum(du.astype(F32), 0, keepdims=True)
            term = dot(du, weights[2 * v][0], (1, 1))
            total = term if total is None else total + term

        @pl.when(j == 0)
        def _():
            acc[...] = total

        @pl.when(j > 0)
        def _():
            acc[...] += total

        @pl.when(j == hidden // step - 1)
        def _():
            keep_ref[...] = acc[:rows, :]
            send_ref[...] = acc[rows:, :].astype(BF)

    return run(
        kernel, [], [own, other, slope, *arrays],
        [
            ((count, 2 * rows, hidden), BF), ((count, 1, hidden), F32),
            ((rows, depth), F32), ((rows, depth), BF),
        ],
        [pltpu.VMEM((2 * rows, depth), BF), pltpu.VMEM((2 * rows, depth), F32)],
        "ffn_down_up", 8 * rows * depth * hidden * count, (hidden // step,),
        [row, row, tall] + specs, [tall, line, row, row],
    )


def split_blocks(full, keep_ref, send_ref, at, core, blocks, size):
    for p in range(blocks // 2):
        mine = multiple((2 * p + core) * size, size)
        theirs = multiple((2 * p + 1 - core) * size, size)
        keep_ref[at + (p,)] = full[pl.ds(mine, size), :]
        send_ref[at + (p,)] = full[pl.ds(theirs, size), :]


def ffn_weight_grads(x_own, x_other, e_own, e_other, du, act, core, blocks):
    rows, depth = x_own.shape
    count, _, hidden = du.shape
    step = min(512, hidden)
    per = hidden // step
    size = depth // blocks
    split = core is not None

    def kernel(core_ref, x_ref, xo_ref, e_ref, eo_ref, du_ref, act_ref, *rest):
        outs, (xs, es, full) = rest[:-3], rest[-3:]

        @pl.when(pl.program_id(0) == 0)
        def _():
            xs[:rows, :] = x_ref[...]
            xs[rows:, :] = xo_ref[...]
            es[:rows, :] = e_ref[...]
            es[rows:, :] = eo_ref[...]

        up = dot(xs[...], du_ref[0], (0, 0)).astype(BF)
        down = dot(es[...], act_ref[0], (0, 0)).astype(BF)
        if split:
            full[...] = up
            split_blocks(full, outs[0], outs[1], (), core_ref[0], blocks, size)
            full[...] = down
            split_blocks(full, outs[2], outs[3], (), core_ref[0], blocks, size)
        else:
            outs[0][0] = up
            outs[0][1] = down

    row = pl.BlockSpec((rows, depth), lambda j: (0, 0))
    tall = pl.BlockSpec((1, 2 * rows, step), lambda j: (j // per, 0, j % per))
    if split:
        part = pl.BlockSpec((blocks // 2, size, step), lambda j: (0, 0, j))
        outs, out_blocks = [((blocks // 2, size, hidden * count), BF)] * 4, [part] * 4
    else:
        outs = [((2 * count, depth, hidden), BF)]
        out_blocks = [pl.BlockSpec((2, depth, step), lambda j: (j // per, 0, j % per))]
    return run(
        kernel, [core if split else jnp.zeros((1,), jnp.int32)],
        [x_own, x_other, e_own, e_other, du, act], outs,
        [
            pltpu.VMEM((2 * rows, depth), BF),
            pltpu.VMEM((2 * rows, depth), BF),
            pltpu.VMEM((depth, step), BF),
        ],
        "ffn_weight_grads", 8 * rows * depth * hidden * count, (count * per,),
        [row, row, row, row, tall, tall], out_blocks,
    )


def weight_grads(groups, core, blocks):
    arrays, places = [], []
    for group in groups:
        for pair in group:
            spot = []
            for array in pair:
                known = [i for i, a in enumerate(arrays) if a is array]
                if not known:
                    arrays.append(array)
                    known = [len(arrays) - 1]
                spot.append(known[0])
            places.append(spot)
    depth, width = groups[0][0][0].shape[1], groups[0][0][1].shape[1]
    size = depth // blocks
    count = len(arrays)

    def kernel(core_ref, *rest):
        outs, full = rest[count:-1], rest[-1]
        number = 0
        for g, group in enumerate(groups):
            for j in range(len(group)):
                left, right = places[number]
                value = dot(rest[left][...], rest[right][...], (0, 0)).astype(BF)
                if core is None:
                    outs[g][j] = value
                else:
                    full[...] = value
                    split_blocks(
                        full, outs[2 * g], outs[2 * g + 1], (j,), core_ref[0], blocks, size
                    )
                number += 1

    outs = []
    for group in groups:
        if core is None:
            outs.append(((len(group), depth, width), BF))
        else:
            outs += [((len(group), blocks // 2, size, width), BF)] * 2
    flops = sum(2 * left.shape[0] * depth * width for group in groups for left, right in group)
    return run(
        kernel, [jnp.zeros((1,), jnp.int32) if core is None else core], arrays, outs,
        [pltpu.VMEM((depth, width), BF)], "weight_grads", flops,
    )


def norm_grad_body(terms, summed, gain, grad_ref, low_ref, sums_ref):
    grad = terms[0][...].astype(F32)
    for ref in terms[1:]:
        grad = grad + ref[...].astype(F32)
    total = summed[...]
    center = total - jnp.mean(total, -1, keepdims=True)
    scale = lax.rsqrt(jnp.mean(center * center, -1, keepdims=True) + 1e-05)
    unit = center * scale
    inner = grad * gain
    out = scale * (
        inner - jnp.mean(inner, -1, keepdims=True) - unit * jnp.mean(inner * unit, -1, keepdims=True)
    )
    low = out.astype(BF)
    grad_ref[...] = out
    low_ref[...] = low
    sums_ref[0:1, :] = jnp.sum(low.astype(F32), 0, keepdims=True)
    sums_ref[1:2, :] = jnp.sum(grad * unit, 0, keepdims=True)
    sums_ref[2:3, :] = jnp.sum(grad, 0, keepdims=True)
    return low


def norm_grad(terms, summed, gain, line):
    shape = summed.shape

    def kernel(sum_ref, gain_ref, *rest):
        norm_grad_body(rest[: len(terms)], sum_ref, gain_ref[line : line + 1, :], *rest[len(terms) :])

    return run(
        kernel, [], [summed, gain, *terms], [(shape, F32), (shape, BF), ((3, shape[1]), F32)], [],
        "norm_grad", 1e6,
    )


def norm_out_grad(terms, summed, gain, line, weight):
    shape = summed.shape
    count, depth, width = weight.shape

    def kernel(sum_ref, gain_ref, w_ref, *rest):
        outs = rest[len(terms) :]
        low = norm_grad_body(rest[: len(terms)], sum_ref, gain_ref[line : line + 1, :], *outs[:3])
        for mask in range(count):
            outs[3 + mask][...] = dot(low, w_ref[mask], (1, 0)).astype(BF)

    return run(
        kernel, [], [summed, gain, weight, *terms],
        [(shape, F32), (shape, BF), ((3, shape[1]), F32)] + [((shape[0], width), BF)] * count, [],
        "norm_out_grad", 2 * shape[0] * depth * width * count,
    )


def input_grads(dq, own, below, above, weights, t_index, count):
    tokens, width = dq.shape
    rows, depth = tokens // count, weights.shape[1]
    ahead = weights.shape[0] - 2

    def kernel(t_ref, w_ref, dq_ref, own_ref, below_ref, above_ref, dk_ref, dv_ref, sums_ref, *rest):
        full = rest[count]
        for j, ref in enumerate((dk_ref, dv_ref)):
            ref[...] = (
                own_ref[j] + below_ref[j].astype(F32) + above_ref[j].astype(F32)
            ).astype(BF)
        sums_ref[0:1, :] = jnp.sum(dq_ref[...].astype(F32), 0, keepdims=True)
        sums_ref[1:2, :] = jnp.sum(dv_ref[...].astype(F32), 0, keepdims=True)
        total = dot(dk_ref[...], w_ref[ahead], (1, 1)) + dot(dv_ref[...], w_ref[ahead + 1], (1, 1))
        if ahead:
            total = total + dot(dq_ref[...], w_ref[0], (1, 1))
        full[...] = total
        for mask in range(count):
            part = full[pl.ds(multiple((t_ref[0] ^ mask) * rows, rows), rows), :]
            rest[mask][...] = part.astype(rest[mask].dtype)

    return run(
        kernel, [t_index], [weights, dq, own, below, above],
        [((tokens, width), BF)] * 2 + [((2, width), F32), ((rows, depth), F32)]
        + [((rows, depth), BF)] * (count - 1),
        [pltpu.VMEM((tokens, depth), F32)], "input_grads",
        2 * tokens * width * depth * weights.shape[0],
    )


def asked_grad(pieces, weight):
    count, depth, width = weight.shape
    rows = pieces[0].shape[0]

    def kernel(w_ref, *rest):
        total = dot(rest[0][...], w_ref[0], (1, 1))
        for mask in range(1, count):
            total = total + dot(rest[mask][...], w_ref[mask], (1, 1))
        rest[count][...] = total

    return run(
        kernel, [], [weight, *pieces], [((rows, depth), F32)], [], "asked_grad",
        2 * rows * depth * width * count,
    )[0]


def by_mask(values, t_index, count):
    tokens, width = values.shape
    rows = tokens // count

    def kernel(t_ref, x_ref, *outs):
        for mask in range(count):
            outs[mask][...] = x_ref[pl.ds(multiple((t_ref[0] ^ mask) * rows, rows), rows), :]

    return run(kernel, [t_index], [values], [((rows, width), BF)] * count, [], "by_mask", 1000)


def in_order(pieces, t_index):
    count = len(pieces)
    rows, width = pieces[0].shape

    def kernel(t_ref, *refs):
        place_rows(refs[count], refs[:count], t_ref[0])

    return run(
        kernel, [t_index], pieces, [((rows * count, width), BF)], [], "in_order", 1000
    )[0]


LINES = 32
ENC_ATT, ENC_FFN, SELF_ATT, CROSS_ATT, DEC_FFN, ENC_FIRST, DEC_FIRST = 0, 5, 8, 13, 18, 21, 25


def pack_small(arrays, width):
    def kernel(*refs):
        lines = []
        for ref in refs[:-1]:
            value = ref[...].astype(F32)
            if value.shape[1] > width:
                value = jnp.concatenate(
                    [value[:, i : i + width] for i in range(0, value.shape[1], width)], 0
                )
            lines.append(value)
        used = sum(value.shape[0] for value in lines)
        lines.append(jnp.zeros((LINES - used, width), F32))
        refs[-1][...] = jnp.concatenate(lines, 0).astype(BF)

    blocks = [pl.BlockSpec(array.shape, lambda i: (0, 0)) for array in arrays]
    return run(
        kernel, [], arrays, [((LINES, width), BF)], [], "pack_small", 0, (1,), blocks,
        [pl.BlockSpec((LINES, width), lambda i: (0, 0))],
    )[0]


def unpack_small(parts, t_index, count, features, wide_masks):
    peers, lines, width = parts.shape
    share_ = peers // count
    quarter = 4
    hidden = share_ * quarter * width

    def kernel(t_ref, x_ref, table, local, enc_ref, dec_ref):
        for f in range(peers):
            table[:, f * width : (f + 1) * width] = x_ref[f].astype(F32)
        for mask in range(count):
            local[mask] = table[:, pl.ds(multiple((t_ref[0] ^ mask) * features, 128), features)]
        for ref, first in ((enc_ref, ENC_FIRST), (dec_ref, DEC_FIRST)):
            for v, mask in enumerate(wide_masks):
                for f in range(share_):
                    for q in range(quarter):
                        at = (f * quarter + q) * width
                        ref[v, :, at : at + width] = local[
                            mask, first + q : first + q + 1, f * width : (f + 1) * width
                        ]

    first = ((len(wide_masks), 1, hidden), F32)
    return run(
        kernel, [t_index], [parts],
        [((lines, peers * width), F32), ((count, lines, features), F32), first, first], [],
        "unpack_small", 0,
    )


def pack_grads(sums, columns, firsts, t_index, peers, wide_masks):
    depth = sums[0].shape[1]
    width = depth // peers
    features = columns[0].shape[1]
    share_ = features // width
    quarter = 4
    arrays = list(sums) + list(columns) + list(firsts)

    def kernel(t_ref, *refs):
        out, table = refs[-2:]
        table[...] = jnp.zeros_like(table)
        own = pl.ds(multiple(t_ref[0] * features, 128), features)
        att = (ENC_ATT, SELF_ATT, CROSS_ATT)
        for first, s_ref, c_ref in zip(att, refs[:3], refs[5:8]):
            table[first + 2 : first + 5, :] = s_ref[...]
            table[first : first + 2, own] = c_ref[...]
        for first, s_ref in zip((ENC_FFN, DEC_FFN), refs[3:5]):
            table[first : first + 3, :] = s_ref[...]
        for first, f_ref in zip((ENC_FIRST, DEC_FIRST), refs[8:10]):
            for v, mask in enumerate(wide_masks):
                strip = []
                for q in range(quarter):
                    pieces = []
                    for f in range(share_):
                        at = (f * quarter + q) * width
                        pieces.append(f_ref[v, :, at : at + width])
                    strip.append(jnp.concatenate(pieces, 1))
                there = pl.ds(multiple((t_ref[0] ^ mask) * features, 128), features)
                table[first : first + quarter, there] = jnp.concatenate(strip, 0)
        for f in range(peers):
            out[f] = table[:, f * width : (f + 1) * width]

    return run(
        kernel, [t_index], arrays, [((peers, LINES, width), F32)],
        [pltpu.VMEM((LINES, depth), F32)], "pack_grads", 0,
    )[0]


def unpack_grads(terms, shapes):
    def kernel(*refs):
        value = refs[0][...]
        for ref in refs[1 : len(terms)]:
            value = value + ref[...]
        width = value.shape[1]
        line = 0
        for ref in refs[len(terms) :]:
            rows, columns = ref.shape
            for r in range(rows):
                for at in range(0, columns, width):
                    ref[r : r + 1, at : at + width] = value[line : line + 1, :]
                    line += 1

    return run(kernel, [], terms, [(shape, F32) for shape in shapes], [], "unpack_grads", 0)


def token_spans(seq_lens, pic_start, pic_len, base, tokens, block):
    count, pictures = pic_start.shape
    blocks = tokens // block

    def kernel(lens, starts, extents, base_ref, both, text, both_bounds, text_bounds):
        places = lax.broadcasted_iota(jnp.int32, (1, tokens), 1) + tokens
        zero = jnp.zeros((1, tokens), jnp.int32)
        begin, end = zero, zero
        low, high = [zero] * pictures, [zero] * pictures
        edges = [
            [jnp.int32(3 * tokens), jnp.int32(0), jnp.int32(tokens + (i + 1) * block)]
            for i in range(blocks)
        ]
        start = tokens - base_ref[0]
        for s in range(count):
            stop = start + lens[s]
            inside = (places >= start) & (places < stop)
            begin = jnp.where(inside, start, begin)
            end = jnp.where(inside, stop, end)
            spans = []
            for k in range(pictures):
                first = start + starts[s, k]
                last = jnp.minimum(first + extents[s, k], stop)
                member = inside & (places >= first) & (places < last)
                low[k] = jnp.where(member, first, low[k])
                high[k] = jnp.where(member, last, high[k])
                spans.append((first, last))
            for i in range(blocks):
                from_, to = tokens + i * block, tokens + (i + 1) * block
                meets = (start < to) & (stop > from_)
                edge = edges[i]
                edge[0] = jnp.where(meets, jnp.minimum(edge[0], start), edge[0])
                edge[1] = jnp.where(meets, jnp.maximum(edge[1], stop), edge[1])
                for first, last in spans:
                    touches = (first < to) & (last > from_)
                    edge[2] = jnp.where(touches, jnp.maximum(edge[2], last), edge[2])
            start = stop
        both[...] = jnp.concatenate([begin, end] + [zero] * 6, 0)
        seen = [begin, places + 1]
        for k in range(pictures):
            seen += [low[k], high[k]]
        text[...] = jnp.concatenate(seen + [zero] * (8 - len(seen)), 0)
        for i in range(blocks):
            first = lax.div(edges[i][0], jnp.int32(block))
            both_bounds[2 * i] = first
            both_bounds[2 * i + 1] = lax.div(edges[i][1] + (block - 1), jnp.int32(block))
            text_bounds[2 * i] = first
            text_bounds[2 * i + 1] = lax.div(edges[i][2] + (block - 1), jnp.int32(block))

    whole = pl.BlockSpec(memory_space=pltpu.VMEM)
    scalars = pl.BlockSpec(memory_space=pltpu.SMEM)
    return run(
        kernel, [seq_lens, pic_start, pic_len, base], [],
        [((8, tokens), jnp.int32)] * 2 + [((2 * blocks,), jnp.int32)] * 2, [], "token_spans", 0,
        None, None, [whole, whole, scalars, scalars],
    )


def per_device(
    enc_in,
    dec_in,
    enc_cot,
    dec_cot,
    seq_lens,
    pic_start,
    pic_len,
    enc_attn_w,
    enc_attn_bias,
    enc_attn_norm,
    enc_ffn_w,
    enc_ffn_b1,
    enc_ffn_vec,
    self_attn_w,
    self_attn_bias,
    self_attn_norm,
    cross_attn_w,
    cross_attn_bias,
    cross_attn_norm,
    dec_ffn_w,
    dec_ffn_b1,
    dec_ffn_vec,
):
    rows = enc_in.shape[0]
    tensor_size = lax.axis_size("tensor")
    fsdp_size = lax.axis_size("fsdp")
    t_index = lax.axis_index("tensor")
    f_index = lax.axis_index("fsdp")
    t_ref = t_index[None].astype(jnp.int32)
    core = (f_index % 2)[None].astype(jnp.int32)
    tokens = rows * tensor_size
    features = enc_attn_w.shape[2]
    hidden = enc_ffn_w.shape[2]
    t_down = bits_of("tensor")[::-1]
    t_up = bits_of("tensor")
    wide_down = t_down[:-1]
    wide_up = t_up[1:]
    t_masks = range(tensor_size)
    wide_masks = range(0, tensor_size, 2)

    small = [
        enc_attn_bias, enc_attn_norm, enc_ffn_vec, self_attn_bias, self_attn_norm,
        cross_attn_bias, cross_attn_norm, dec_ffn_vec, enc_ffn_b1, dec_ffn_b1,
    ]
    parts = lax.all_gather(pack_small(small, enc_attn_bias.shape[1]), "fsdp", axis=0)
    table, local, enc_first, dec_first = unpack_small(
        parts, t_ref, tensor_size, features, wide_masks
    )
    block = min(256, tokens)
    base = (f_index * tokens)[None].astype(jnp.int32)
    spans = token_spans(seq_lens, pic_start, pic_len, base, tokens, block)
    both = (spans[0], spans[2], 1)
    text = (spans[1], spans[3], 1 + pic_start.shape[1])

    first_order, second_order = plane_orders()

    def later(value, ready):
        return lax.optimization_barrier((value, ready))[0]

    def ffn_gather(shards):
        stack = shards[0] if len(shards) == 1 else jnp.concatenate(shards)
        whole = lax.all_gather(stack, "fsdp", axis=1, tiled=True)
        return [(whole, 2 * i, 2 * i + 1) for i in range(len(shards))]

    def exchange(pieces_):
        return [pieces_[0]] + [swap(pieces_[mask], "tensor", mask) for mask in t_masks[1:]]

    peers = fsdp_size
    up_pairs = [(i, i + 1) for i in range(peers - 1)]
    down_pairs = [(j, i) for i, j in up_pairs]

    def halo(pair):
        before = lax.ppermute(pair, "fsdp", up_pairs)
        after = lax.ppermute(pair, "fsdp", down_pairs)
        return before, pair, after

    def attend_fg(queries, window, mode):
        return attend(queries, window, mode[0], mode[1], t_ref, tensor_size, mode[2])

    def attend_back_fg(queries, window, grads, mixed_t, totals, mode):
        return attend_back(
            queries, window, grads, mixed_t, totals, mode[0], mode[1], t_ref, tensor_size, mode[2]
        )

    pending = [[], []]

    def due(*values):
        pending[1].extend(values)

    def fg(value):
        waits = pending.pop(0)
        pending.append([])
        return join(value, *waits)

    enc_pieces = spread(enc_in, "tensor", t_down)
    (enc_qkv,) = gather_plane(enc_attn_w[:3], first_order, [3])
    enc_out_shards = jnp.stack(spread(enc_attn_w[3], "tensor", t_down))[None]
    enc_own_views = ffn_gather([join(enc_ffn_w, enc_qkv)])
    plan = Gather(enc_out_shards, second_order, [tensor_size])
    due(plan.hop())
    flat_e, pair_e, query_e = project(
        enc_pieces, fg(enc_qkv), local, (ENC_ATT, None, ENC_ATT + 1), t_ref
    )
    k1 = query_e
    window_e = halo(pair_e)
    due(plan.hop(k1))
    self_plan = Gather(join(self_attn_w[:3], k1)[None], first_order, [3])
    due(self_plan.hop())
    dec_spread = Spread(join(dec_in, k1), "tensor", t_down)
    due(*dec_spread.hop())
    self_spread = Spread(join(self_attn_w[3], k1), "tensor", t_down)
    due(*self_spread.hop())

    mixed_e, mixed_t_e, totals_e = attend_fg(fg(query_e), window_e, both)
    k2 = totals_e
    mixed_e = exchange(mixed_e)
    plan.hop(k2)
    (enc_out_w,) = plan.result()
    due(*dec_spread.hop(k2), *self_spread.hop(k2))
    due(self_plan.hop(k2))

    summed_e, hid, hid_low = out_norm(
        [fg(mixed_e[0])] + mixed_e[1:], enc_out_w, enc_in, table, ENC_ATT + 2
    )
    k3 = hid_low
    hid_other = swap(hid_low, "tensor", 1)
    self_plan.hop(k3)
    (self_qkv,) = self_plan.result()
    dec_pieces = dec_spread.result()
    self_out_plan = Gather(
        jnp.stack(self_spread.result(k3))[None], second_order, [tensor_size]
    )
    due(self_out_plan.hop())
    enc_wide = Spread(join(enc_ffn_w, k3), "tensor", wide_down)
    enc_wide.hop()
    cross_spread = Spread(
        join(jnp.stack([cross_attn_w[3], cross_attn_w[0]]), k3), "tensor", t_down
    )
    due(*cross_spread.hop())

    flat_s, pair_s, query_s = project(
        fg(dec_pieces), self_qkv, local, (SELF_ATT, None, SELF_ATT + 1), t_ref
    )
    k4 = query_s
    window_s = halo(pair_s)
    due(self_out_plan.hop(k4))
    due(*cross_spread.hop(k4))
    enc_shards = enc_wide.result(k4)

    mixed_s, mixed_t_s, totals_s = attend_fg(fg(query_s), window_s, text)
    k5 = totals_s
    mixed_s = exchange(mixed_s)
    enc_views = enc_own_views + ffn_gather(join(enc_shards[1:], k5))
    self_out_plan.hop(k5)
    (self_out_w,) = self_out_plan.result()
    cross_pieces = cross_spread.result(k5)
    cross_shards = jnp.concatenate(
        [cross_attn_w[1:3]]
        + [piece[1:2] for piece in cross_pieces]
        + [piece[0:1] for piece in cross_pieces]
    )
    cross_plan = Gather(cross_shards[None], first_order, [2, tensor_size, tensor_size])
    due(cross_plan.hop())
    dec_wide = Spread(join(dec_ffn_w, k5), "tensor", wide_down)
    dec_wide.hop()

    summed_s, decoded, decoded_low = out_norm(
        [fg(mixed_s[0])] + mixed_s[1:], self_out_w, dec_in, table, SELF_ATT + 2
    )
    k6 = decoded_low
    cross_plan.hop(k6)
    dec_views = ffn_gather(dec_wide.result(k6))

    active_e, slope_e, keep, send = ffn_up_down(
        join(hid_low, k6), hid_other, enc_views, enc_first
    )
    k7 = keep
    came = swap(send, "tensor", 1)
    cross_plan.hop(k7)
    cross_kv, cross_query, cross_out_w = cross_plan.result()
    ffn_summed_e, encoded = add_norm([hid, keep, came], table, ENC_FFN)
    enc_rows = spread(encoded, "tensor", t_down)
    asked = exchange(
        project_rows(join(decoded_low, encoded), cross_query, local, CROSS_ATT)
    )

    flat_c, pair_c = project(
        enc_rows, cross_kv, local, (None, CROSS_ATT + 1), t_ref
    )
    window_c = halo(pair_c)
    query_c = in_order(asked, t_ref)
    mixed_c, mixed_t_c, totals_c = attend_fg(query_c, window_c, both)
    mixed_c = exchange(mixed_c)
    summed_c, crossed, crossed_low = out_norm(
        mixed_c, cross_out_w, decoded, table, CROSS_ATT + 2
    )
    crossed_other = swap(crossed_low, "tensor", 1)
    active_d, slope_d, keep, send = ffn_up_down(
        crossed_low, crossed_other, dec_views, dec_first
    )
    came = swap(send, "tensor", 1)
    ffn_summed_d, final = add_norm([crossed, keep, came], table, DEC_FFN)

    grad_sum_d, low_d, dec_sums = norm_grad([dec_cot], ffn_summed_d, table, DEC_FFN + 1)
    other_d = swap(low_d, "tensor", 1)
    du_d, dec_first_sum, keep, send = ffn_down_up(low_d, other_d, dec_views, slope_d)
    came = swap(send, "tensor", 1)
    dec_grads = ffn_weight_grads(
        crossed_low, crossed_other, low_d, other_d, join(du_d, send), active_d, None, fsdp_size
    )[0]
    dec_whole = lax.psum_scatter(dec_grads, "fsdp", scatter_dimension=1, tiled=True)

    grad_sum_c, low_c, sums_c, *given = norm_out_grad(
        [grad_sum_d, join(keep, dec_grads), came], summed_c, table, CROSS_ATT + 3, cross_out_w
    )
    given = exchange(given)
    dq_c, below, own, above = attend_back_fg(
        query_c, window_c, given, mixed_t_c, totals_c, both
    )
    below = lax.ppermute(below, "fsdp", down_pairs)
    above = lax.ppermute(above, "fsdp", up_pairs)
    asked_c = exchange(by_mask(dq_c, t_ref, tensor_size))
    dk_c, dv_c, columns_c, *blocks_c = input_grads(
        dq_c, own, below, above, cross_kv, t_ref, tensor_size
    )
    source = Share(blocks_c, "tensor", t_up)
    due(*source.hop())
    from_asked = asked_grad([join(asked_c[0], dk_c)] + asked_c[1:], cross_query)

    grad_sum_s, low_s, sums_s, *given = norm_out_grad(
        [fg(grad_sum_c), from_asked], summed_s, table, SELF_ATT + 3, self_out_w
    )
    b6 = low_s
    given = exchange(given)
    due(*source.hop(b6))
    cross_grads = weight_grads(
        [
            [(flat_c, join(dk_c, b6)), (flat_c, dv_c)]
            + [(low_c, piece) for piece in mixed_c]
            + [(decoded_low, piece) for piece in asked_c]
        ],
        core, fsdp_size,
    )
    cross_fold = Fold(cross_grads[0], cross_grads[1], second_order[:-1], 1)
    due(cross_fold.hop())
    dq_s, below, own, above = attend_back_fg(
        query_s, window_s, [fg(given[0])] + given[1:], mixed_t_s, totals_s, text
    )
    b7 = dq_s
    below = lax.ppermute(below, "fsdp", down_pairs)
    above = lax.ppermute(above, "fsdp", up_pairs)
    cross_fold.next(b7)
    grad_sum_f, low_f, enc_sums = norm_grad(
        [join(enc_cot, b7)] + source.result(), ffn_summed_e, table, ENC_FFN + 1
    )
    b9 = low_f
    other_f = swap(low_f, "tensor", 1)
    dk_s, dv_s, columns_s, *blocks_s = input_grads(
        dq_s, join(own, b9), below, above, self_qkv, t_ref, tensor_size
    )
    b8 = dk_s
    target = Share(blocks_s, "tensor", t_up)
    due(*target.hop())
    due(cross_fold.came)
    du_e, enc_first_sum, keep, send = ffn_down_up(
        fg(join(low_f, b8)), other_f, enc_views, slope_e
    )
    b10 = keep
    came = swap(send, "tensor", 1)
    due(*target.hop(b10))
    due(cross_fold.next(b10))
    enc_grads = ffn_weight_grads(
        hid_low, hid_other, low_f, other_f, join(du_e, send), active_e, core, fsdp_size
    )
    self_parts = weight_grads(
        [
            [(flat_s, join(dq_s, b10)), (flat_s, dk_s), (flat_s, dv_s)]
            + [(low_s, piece) for piece in mixed_s]
        ],
        core, fsdp_size,
    )
    due(enc_grads, self_parts)

    grad_sum_e, low_e, sums_e, *given = norm_out_grad(
        [grad_sum_f, fg(keep), came], summed_e, table, ENC_ATT + 3, enc_out_w
    )
    b11 = low_e
    given = exchange(given)
    enc_folds = [
        Fold(enc_grads[2 * i], enc_grads[2 * i + 1], (first_order, second_order)[i][:-1], 0)
        for i in range(2)
    ]
    for item in enc_folds:
        due(item.hop(b11))
    self_fold = Fold(self_parts[0], self_parts[1], first_order[:-1], 1)
    due(self_fold.hop(b11))
    cross_own = cross_fold.result(b11)
    cross_pieces = cross_own[2:].reshape((2, tensor_size) + cross_own.shape[1:])
    cross_share = Share([cross_pieces[:, mask] for mask in t_masks], "tensor", t_up)
    due(*cross_share.hop())
    dq_e, below, own, above = attend_back_fg(
        query_e, window_e, [fg(given[0])] + given[1:], mixed_t_e, totals_e, both
    )
    b12 = dq_e
    below = lax.ppermute(below, "fsdp", down_pairs)
    above = lax.ppermute(above, "fsdp", up_pairs)
    for item in enc_folds:
        due(item.next(b12))
    due(*cross_share.hop(b12))
    due(self_fold.next(b12))
    dk_e, dv_e, columns_e, *blocks_e = input_grads(
        dq_e, fg(own), below, above, enc_qkv, t_ref, tensor_size
    )
    b13 = dk_e
    enc_share = Share(blocks_e, "tensor", t_up)
    enc_share.hop()
    enc_att = weight_grads(
        [
            [(flat_e, dq_e), (flat_e, join(dk_e, tuple(blocks_e))), (flat_e, dv_e)],
            [(low_e, piece) for piece in mixed_e],
        ],
        core, fsdp_size,
    )
    enc_att_folds = [
        Fold(enc_att[2 * i], enc_att[2 * i + 1], (first_order, second_order)[i][:-1], 1)
        for i in range(2)
    ]
    for item in enc_att_folds:
        item.hop()
    enc_own = [item.result(b13) for item in enc_folds]
    self_own = self_fold.result(b13)

    def tensor_sum(pieces_):
        return total(Share(pieces_, "tensor", t_up).result())

    def wide_sum(pieces_):
        held = dict(zip(wide_masks, pieces_))
        for bit in wide_up:
            for mask in sorted(held):
                if mask not in held or mask & (2 * bit - 1):
                    continue
                came_ = swap(held.pop(mask | bit).astype(BF), "tensor", bit)
                held[mask] = held[mask].astype(F32) + came_.astype(F32)
        return held[0].astype(F32)

    wide_count = len(wide_masks)
    small_grads = pack_grads(
        [sums_e, sums_s, sums_c, enc_sums, dec_sums], [columns_e, columns_s, columns_c],
        [enc_first_sum, dec_first_sum], t_ref, fsdp_size, wide_masks,
    )
    for bit in bits_of("fsdp")[::-1]:
        half = small_grads.shape[0] // 2
        mine = (f_index // bit) % 2
        kept = lax.dynamic_slice_in_dim(small_grads, mine * half, half, 0)
        sent = lax.dynamic_slice_in_dim(small_grads, (1 - mine) * half, half, 0)
        small_grads = kept + swap(sent, "fsdp", bit)
    small_grads = small_grads[0]
    for bit in t_up[:-1]:
        small_grads = small_grads + swap(small_grads, "tensor", bit)
    small_out = unpack_grads(
        [small_grads, swap(small_grads, "tensor", t_up[-1])], [item.shape for item in small]
    )

    enc_share.hop()
    dec_ffn_grad = wide_sum(
        [join(dec_whole, b12)[2 * j : 2 * j + 2] for j in range(wide_count)]
    )
    enc_pair = jnp.stack(enc_own)
    enc_ffn_grad = wide_sum(
        [enc_pair[:, :, j * hidden : (j + 1) * hidden] for j in range(wide_count)]
    )
    self_grad = jnp.concatenate(
        [self_own[:3], tensor_sum([self_own[3 + mask] for mask in t_masks])[None]]
    )
    cross_pair = total(cross_share.result())
    cross_grad = jnp.concatenate([cross_pair[1:2], cross_own[:2], cross_pair[0:1]])
    enc_att_own, enc_att_out = [item.result() for item in enc_att_folds]
    enc_grad = jnp.concatenate(
        [enc_att_own, tensor_sum([enc_att_out[mask] for mask in t_masks])[None]]
    )
    grad_source = total([grad_sum_e] + enc_share.result())
    grad_target = total([grad_sum_s] + target.result())

    (
        enc_bias_g, enc_norm_g, enc_vec_g, self_bias_g, self_norm_g,
        cross_bias_g, cross_norm_g, dec_vec_g, enc_b1_g, dec_b1_g,
    ) = small_out
    return (
        encoded,
        final,
        grad_source,
        grad_target,
        enc_grad,
        enc_bias_g,
        enc_norm_g,
        enc_ffn_grad,
        enc_b1_g,
        enc_vec_g,
        self_grad,
        self_bias_g,
        self_norm_g,
        cross_grad,
        cross_bias_g,
        cross_norm_g,
        dec_ffn_grad,
        dec_b1_g,
        dec_vec_g,
    )


def solution(mesh):
    rows = P(("fsdp", "tensor"), None)
    weight = P(None, "fsdp", "tensor")
    vector = P(None, "fsdp")
    att, ffn = (weight, vector, vector), (weight, vector, vector)
    in_specs = (rows,) * 4 + (P(),) * 3 + (att + ffn + att + att + ffn)
    out_specs = (rows,) * 4 + (att + ffn + att + att + ffn)
    return jax.shard_map(
        per_device, mesh=mesh, in_specs=in_specs, out_specs=out_specs, check_vma=False
    )
```

```python
import functools
import jax
import jax.numpy as jnp
from jax import lax
from jax.experimental import pallas as pl
from jax.experimental.pallas import tpu as pltpu
from jax.sharding import PartitionSpec as P

HD = 64
BF = jnp.bfloat16
F32 = jnp.float32
PACE = 30000000000


def bits_of(axis):
    count, bit, bits = lax.axis_size(axis), 1, []
    while bit < count:
        bits.append(bit)
        bit *= 2
    return bits


def swap(value, axis, mask):
    return lax.ppermute(value, axis, [(i, i ^ mask) for i in range(lax.axis_size(axis))])


def join(value, *ready):
    return lax.optimization_barrier((value, ready))[0] if ready else value


def spread(value, axis, order, gates=()):
    pieces = {0: value}
    for k, bit in enumerate(order):
        for mask in list(pieces):
            piece = pieces[mask]
            if mask and k < len(gates):
                piece = join(piece, *gates[k])
            pieces[mask | bit] = swap(piece, axis, bit)
    if len(gates) > len(order):
        return [pieces[0]] + [join(pieces[mask], *gates[-1]) for mask in sorted(pieces)[1:]]
    return [pieces[mask] for mask in sorted(pieces)]


def total(items):
    out = items[0].astype(F32)
    for item in items[1:]:
        out = out + item.astype(F32)
    return out


def plane_orders():
    bits = bits_of("fsdp")
    return bits[1:] + bits[:1], bits[1:][::-1] + bits[:1]


def placed(parts, index, splits):
    arrays = [array for array, masks in parts]
    total = sum(len(masks) for array, masks in parts)
    cols = arrays[0].shape[-1]
    shapes = [
        (width, total, arrays[0].shape[2], cols)
        if isinstance(width, int)
        else (width[0], total, width[1], cols)
        for width in splits
    ]
    moves_ = total * sum(1 if isinstance(width, int) else width[0] for width in splits)

    def kernel(index_ref, *refs):
        ins, outs, sems = refs[: len(parts)], refs[len(parts) : -1], refs[-1]
        copies = []
        for (array, masks), ref in zip(parts, ins):
            for at, mask in enumerate(masks):
                first = 0
                for out, width in zip(outs, splits):
                    if isinstance(width, int):
                        moves = [(ref.at[at, first : first + width], out.at[:, index_ref[0] ^ mask])]
                        first += width
                    else:
                        moves = []
                        for line in range(width[0]):
                            moves.append(
                                (ref.at[at, first : first + width[1]], out.at[line, index_ref[0] ^ mask])
                            )
                            first += width[1]
                    for source, target in moves:
                        copy = pltpu.make_async_copy(source, target, sems.at[len(copies)])
                        copy.start()
                        copies.append(copy)
        for copy in copies:
            copy.wait()

    outs = pl.pallas_call(
        kernel,
        out_shape=[jax.ShapeDtypeStruct(shape, arrays[0].dtype) for shape in shapes],
        in_specs=[pl.BlockSpec(memory_space=pltpu.SMEM)]
        + [pl.BlockSpec(memory_space=pl.ANY)] * len(arrays),
        out_specs=[pl.BlockSpec(memory_space=pltpu.VMEM)] * len(splits),
        scratch_shapes=[pltpu.SemaphoreType.DMA((moves_,))],
        compiler_params=pltpu.CompilerParams(vmem_limit_bytes=32 * 2**20),
        cost_estimate=pl.CostEstimate(flops=PACE, bytes_accessed=1, transcendentals=0),
        name="placed",
    )(index[None], *arrays)
    return [out.reshape(out.shape[0], -1, cols) for out in outs]


def gather_plane(shard, order, splits):
    return Gather(shard[None], order, splits).result()


def reach(value, axis, masks):
    pieces = {0: value}
    for mask in masks:
        pieces[mask] = swap(value, axis, mask)
    return [pieces[mask] for mask in sorted(pieces)]


class Gather:
    def __init__(self, held, order, splits):
        self.held, self.masks, self.order, self.splits = held, [0], list(order), splits
        self.came = None

    def take(self, gate):
        if self.came is not None:
            came = join(self.came, *gate)
            self.held = jnp.concatenate([self.held, came], 0)
            self.masks = self.masks + [mask | self.bit for mask in self.masks]

    def hop(self, *gate):
        self.take(gate)
        self.bit = self.order.pop(0)
        self.came = swap(self.held, "fsdp", self.bit)
        return self.came

    def result(self):
        while self.order:
            self.hop()
        parts = [(self.held, self.masks), (self.came, [mask | self.bit for mask in self.masks])]
        return placed(parts, lax.axis_index("fsdp"), self.splits)


class Spread:
    def __init__(self, value, axis, bits):
        self.axis, self.pieces, self.level, self.last = axis, {0: value}, 0, len(bits)
        self.masks = [m for m in range(lax.axis_size(axis)) if m & ~sum(bits) == 0]

    def hop(self, *gate):
        self.level += 1
        new = []
        for mask in self.masks[::-1]:
            if mask.bit_count() == self.level:
                low = mask & -mask
                piece = self.pieces[mask ^ low]
                if mask != low:
                    piece = join(piece, *gate)
                self.pieces[mask] = swap(piece, self.axis, low)
                new.append(self.pieces[mask])
        return new

    def result(self, *gate):
        while self.level < self.last:
            self.hop()
        return [join(self.pieces[m], *(gate if m else ())) for m in self.masks]


class Share:
    def __init__(self, pieces, axis, bits):
        self.axis, self.held, self.bits = axis, dict(enumerate(pieces)), list(bits)
        self.came, self.terms = None, [pieces[0]]

    def hop(self, *gate):
        if self.came is not None:
            came = join(self.came, *gate)
            for at, mask in enumerate(self.kept):
                if mask == 0:
                    self.terms.append(came[at])
                else:
                    self.held[mask] = self.held[mask].astype(F32) + came[at].astype(F32)
            self.came = None
        if self.bits:
            bit = self.bits.pop(0)
            sent = [mask for mask in sorted(self.held) if mask & bit]
            self.kept = [mask ^ bit for mask in sent]
            stack = jnp.stack([self.held.pop(mask).astype(BF) for mask in sent])
            self.came = swap(stack, self.axis, bit)
        return self.came

    def result(self):
        while self.bits or self.came is not None:
            self.hop()
        return self.terms


class Fold:
    def __init__(self, keep, send, order, at):
        bits = bits_of("fsdp")
        self.live, self.order, self.at = bits[1:][::-1], list(order), at
        split = keep.shape[:at] + (2,) * len(self.live) + keep.shape[at + 1 :]
        self.value, self.sent, self.bit = keep.reshape(split), send.reshape(split), bits[0]

    def hop(self, *gate):
        self.came = swap(join(self.sent, *gate), "fsdp", self.bit)
        return self.came

    def next(self, *gate):
        bit = self.order.pop(0)
        dim = self.at + self.live.index(bit)
        self.live.remove(bit)
        mine = (lax.axis_index("fsdp") // bit) % 2
        value, came = self.value, join(self.came, *gate)

        def pick(which):
            return lax.dynamic_index_in_dim(value, which, dim, False).astype(
                F32
            ) + lax.dynamic_index_in_dim(came, which, dim, False).astype(F32)

        self.value, self.sent, self.bit = pick(mine).astype(BF), pick(1 - mine).astype(BF), bit
        return self.hop()

    def result(self, *gate):
        while self.order:
            self.next(*gate)
            gate = ()
        return self.value.astype(F32) + join(self.came, *gate).astype(F32)


MIB = 2**20
HEAD_SCALE = HD ** (-0.5)


def run(kernel, scalars, arrays, outs, scratch, name, flops, grid=None, in_blocks=None, out_blocks=None):
    arrays = list(arrays)
    whole = pl.BlockSpec(memory_space=pltpu.VMEM)
    in_specs = [pl.BlockSpec(memory_space=pltpu.SMEM)] * len(scalars)
    in_specs += in_blocks if in_blocks else [whole] * len(arrays)
    extra = {"grid": grid} if grid else {}
    return pl.pallas_call(
        kernel,
        out_shape=[jax.ShapeDtypeStruct(shape, kind) for shape, kind in outs],
        in_specs=in_specs,
        out_specs=out_blocks if out_blocks else [whole] * len(outs),
        scratch_shapes=scratch,
        compiler_params=pltpu.CompilerParams(vmem_limit_bytes=40 * MIB),
        cost_estimate=pl.CostEstimate(
            flops=PACE, bytes_accessed=1, transcendentals=0
        ),
        name=name,
        **extra,
    )(*scalars, *arrays)


def dot(left, right, dims):
    return lax.dot_general(left, right, ((dims[:1], dims[1:]), ((), ())), preferred_element_type=F32)


def head_mask(rows, which, level):
    lane = lax.broadcasted_iota(jnp.int32, (rows, 128), 1)
    return jnp.where(lane // HD == which, level, 0.0).astype(BF)


def tile_allowed(meta, first, size, columns, ranges):
    place = lax.broadcasted_iota(jnp.int32, (size, columns), 0) + first
    allowed = (place >= meta[0:1]) & (place < meta[1:2])
    for k in range(1, ranges):
        allowed = allowed | ((place >= meta[2 * k : 2 * k + 1]) & (place < meta[2 * k + 1 : 2 * k + 2]))
    return allowed


def multiple(value, of):
    return pl.multiple_of(value, of)


def place_rows(ref, pieces, t_index):
    rows = pieces[0].shape[0]
    for mask, piece in enumerate(pieces):
        ref[pl.ds(multiple((t_index ^ mask) * rows, rows), rows), :] = piece[:, : ref.shape[1]]


def attend(queries, windows, meta, bounds, t_index, count, ranges):
    tokens, width = queries.shape
    heads, rows = width // HD, tokens // count
    block = min(256, tokens)
    tiles = 3 * tokens // block

    def kernel(bounds_ref, t_ref, meta_ref, q_ref, b_ref, w_ref, a_ref, *rest):
        o_refs, (ot_ref, lse_ref, keys, v_t, held, acc, nat) = rest[:count], rest[count:]
        for j, ref in enumerate((b_ref, w_ref, a_ref)):
            keys[j * tokens : (j + 1) * tokens, :] = ref[0]
            v_t[:, j * tokens : (j + 1) * tokens] = ref[1].T
        for i in range(tokens // block):
            low, high = bounds_ref[2 * i], bounds_ref[2 * i + 1]
            span = slice(i * block, (i + 1) * block)
            info = meta_ref[:, span]
            asked = []
            for h in range(heads):
                lanes = slice(h // 2 * 128, h // 2 * 128 + 128)
                asked.append(q_ref[span, lanes] * head_mask(block, h % 2, HEAD_SCALE))

            def scores(k, tops):
                first = multiple(k * block, block)
                allowed = tile_allowed(info, first, block, block, ranges)
                out = []
                for h in range(heads):
                    lanes = slice(h // 2 * 128, h // 2 * 128 + 128)
                    s = dot(keys[pl.ds(first, block), lanes], asked[h], (1, 1))
                    s = jnp.where(allowed, s, -1e30)
                    held[h, k] = s
                    out.append(jnp.maximum(tops[h], jnp.max(s, 0, keepdims=True)))
                return tuple(out)

            tops = lax.fori_loop(
                low, high, scores, tuple(jnp.full((1, block), -1e30, F32) for h in range(heads))
            )
            acc[...] = jnp.zeros_like(acc)

            def mixes(k, sums):
                first = multiple(k * block, block)
                out = []
                for h in range(heads):
                    p = jnp.exp(held[h, k] - tops[h])
                    out.append(sums[h] + jnp.sum(p, 0, keepdims=True))
                    some = slice(h * HD, (h + 1) * HD)
                    acc[some, :] += dot(v_t[some, pl.ds(first, block)], p.astype(BF), (1, 0))
                return tuple(out)

            sums = lax.fori_loop(
                low, high, mixes, tuple(jnp.zeros((1, block), F32) for h in range(heads))
            )
            for h in range(heads):
                some = slice(h * HD, (h + 1) * HD)
                acc[some, :] = acc[some, :] / sums[h]
                lse_ref[h : h + 1, span] = tops[h] + jnp.log(sums[h])
            ot_ref[:, span] = acc[...]
            nat[span, :] = acc[...].T.astype(BF)
        for mask in range(count):
            o_refs[mask][...] = nat[pl.ds(multiple((t_ref[0] ^ mask) * rows, rows), rows), :]

    out = run(
        kernel,
        [bounds, t_index],
        [meta, queries, *windows],
        [((rows, width), BF)] * count + [((width, tokens), F32), ((heads, tokens), F32)],
        [
            pltpu.VMEM((3 * tokens, width), BF),
            pltpu.VMEM((width, 3 * tokens), BF),
            pltpu.VMEM((heads, tiles, block, block), F32),
            pltpu.VMEM((width, block), F32),
            pltpu.VMEM((tokens, width), BF),
        ],
        "attend",
        4 * tokens * 3 * tokens * width * 4,
    )
    return out[:count], out[count], out[count + 1]


def attend_back(queries, windows, grads, mixed_t, totals, meta, bounds, t_index, count, ranges):
    tokens, width = queries.shape
    heads, rows = width // HD, tokens // count
    block = min(256, tokens)

    def kernel(bounds_ref, t_ref, meta_ref, q_ref, b_ref, w_ref, a_ref, ot_ref, lse_ref, *rest):
        g_refs = rest[:count]
        dq_ref, db_ref, dw_ref, da_ref, nat, keys, values, k_t, dk, dv, acc = rest[count:]
        place_rows(nat, g_refs, t_ref[0])
        for j, ref in enumerate((b_ref, w_ref, a_ref)):
            part = slice(j * tokens, (j + 1) * tokens)
            keys[part, :] = ref[0]
            values[part, :] = ref[1]
            k_t[:, part] = ref[0].T
        dk[...] = jnp.zeros_like(dk)
        dv[...] = jnp.zeros_like(dv)
        for i in range(tokens // block):
            low, high = bounds_ref[2 * i], bounds_ref[2 * i + 1]
            span = slice(i * block, (i + 1) * block)
            info = meta_ref[:, span]
            g_t = nat[span, :].astype(F32).T
            asked, given, inner = [], [], []
            for h in range(heads):
                lanes = slice(h // 2 * 128, h // 2 * 128 + 128)
                some = slice(h * HD, (h + 1) * HD)
                asked.append(q_ref[span, lanes] * head_mask(block, h % 2, HEAD_SCALE))
                given.append(nat[span, lanes] * head_mask(block, h % 2, 1.0))
                inner.append(jnp.sum(g_t[some] * ot_ref[some, span], 0, keepdims=True))
            acc[...] = jnp.zeros_like(acc)

            def step(k, carry):
                first = multiple(k * block, block)
                at = pl.ds(first, block)
                allowed = tile_allowed(info, first, block, block, ranges)
                for h in range(heads):
                    lanes = slice(h // 2 * 128, h // 2 * 128 + 128)
                    some = slice(h * HD, (h + 1) * HD)
                    s = dot(keys[at, lanes], asked[h], (1, 1))
                    p = jnp.exp(jnp.where(allowed, s, -1e30) - lse_ref[h : h + 1, span])
                    dp = dot(values[at, lanes], given[h], (1, 1))
                    ds = (p * (dp - inner[h])).astype(BF)
                    dv[at, lanes] += dot(p.astype(BF), given[h], (1, 0))
                    dk[at, lanes] += dot(ds, asked[h], (1, 0))
                    acc[some, :] += dot(k_t[some, at], ds, (1, 0))
                return carry

            lax.fori_loop(low, high, step, 0)
            dq_ref[span, :] = (acc[...] * HEAD_SCALE).T.astype(BF)
        for j, ref in enumerate((db_ref, dw_ref, da_ref)):
            part = slice(j * tokens, (j + 1) * tokens)
            ref[0] = dk[part, :].astype(ref.dtype)
            ref[1] = dv[part, :].astype(ref.dtype)

    pair = (2, tokens, width)
    return run(
        kernel,
        [bounds, t_index],
        [meta, queries, *windows, mixed_t, totals, *grads],
        [((tokens, width), BF), (pair, BF), (pair, F32), (pair, BF)],
        [
            pltpu.VMEM((tokens, width), BF),
            pltpu.VMEM((3 * tokens, width), BF),
            pltpu.VMEM((3 * tokens, width), BF),
            pltpu.VMEM((width, 3 * tokens), BF),
            pltpu.VMEM((3 * tokens, width), F32),
            pltpu.VMEM((3 * tokens, width), F32),
            pltpu.VMEM((width, block), F32),
        ],
        "attend_back",
        10 * tokens * 3 * tokens * width * 4,
    )


def project(pieces, weights, local, lines, t_index):
    count = len(pieces)
    rows, depth = pieces[0].shape[0], weights.shape[1]
    tokens, width = rows * count, weights.shape[2]
    outputs = weights.shape[0]

    def kernel(t_ref, w_ref, local_ref, *rest):
        x_ref = rest[count]
        place_rows(x_ref, rest[:count], t_ref[0])
        x = x_ref[...]
        done = []
        for k, line in enumerate(lines):
            value = dot(x, w_ref[k], (1, 0))
            if line is not None:
                value = value + local_ref[0, line : line + 1, :]
            done.append(value.astype(BF))
        if outputs == 3:
            rest[count + 2][...] = done[0]
        rest[count + 1][0] = done[-2]
        rest[count + 1][1] = done[-1]

    outs = [((tokens, depth), BF), ((2, tokens, width), BF)]
    if outputs == 3:
        outs.append(((tokens, width), BF))
    return run(
        kernel, [t_index], [weights, local, *pieces], outs, [], "project",
        2 * tokens * depth * width * outputs,
    )


def project_rows(low, weight, local, line):
    count, depth, width = weight.shape

    def kernel(x_ref, w_ref, local_ref, *outs):
        for mask in range(count):
            outs[mask][...] = (
                dot(x_ref[...], w_ref[mask], (1, 0)) + local_ref[mask, line : line + 1, :]
            ).astype(BF)

    return run(
        kernel, [], [low, weight, local], [((low.shape[0], width), BF)] * count, [],
        "project_rows", 2 * low.shape[0] * depth * width * count,
    )


def normed(total, gain, shift):
    center = total - jnp.mean(total, -1, keepdims=True)
    scale = lax.rsqrt(jnp.mean(center * center, -1, keepdims=True) + 1e-05)
    return center * scale * gain + shift


def out_norm(mixed, weight, residual, vectors, line):
    count, depth, width = weight.shape
    shape = residual.shape

    def kernel(w_ref, r_ref, v_ref, *rest):
        total = r_ref[...].astype(F32) + v_ref[line : line + 1, :]
        for mask in range(count):
            total = total + dot(rest[mask][...], w_ref[mask], (1, 1))
        sum_ref, out_ref, low_ref = rest[count:]
        sum_ref[...] = total
        out = normed(total, v_ref[line + 1 : line + 2, :], v_ref[line + 2 : line + 3, :])
        out_ref[...] = out
        low_ref[...] = out.astype(BF)

    return run(
        kernel, [], [weight, residual, vectors, *mixed], [(shape, F32), (shape, F32), (shape, BF)],
        [], "out_norm", 2 * shape[0] * depth * width * count,
    )


def add_norm(terms, vectors, line):
    shape = terms[0].shape

    def kernel(v_ref, *rest):
        total = v_ref[line : line + 1, :]
        for ref in rest[: len(terms)]:
            total = total + ref[...].astype(F32)
        sum_ref, low_ref = rest[len(terms) :]
        sum_ref[...] = total
        out = normed(total, v_ref[line + 1 : line + 2, :], v_ref[line + 2 : line + 3, :])
        low_ref[...] = out.astype(BF)

    return run(
        kernel, [], [vectors, *terms], [(shape, F32), (shape, BF)], [], "add_norm", 1e6
    )


def ffn_blocks(views, rows, depth, hidden):
    step = views[0][0].shape[2]
    row = pl.BlockSpec((rows, depth), lambda j: (0, 0))

    def weight(first):
        return pl.BlockSpec((1, depth, step), lambda j: (first + j, 0, 0))

    tall = pl.BlockSpec((len(views), 2 * rows, step), lambda j: (0, 0, j))
    line = pl.BlockSpec((len(views), 1, step), lambda j: (0, 0, j))
    specs, arrays = [], []
    for up, up_first, down, down_first in views:
        specs += [weight(up_first), weight(down_first)]
        arrays += [up, down]
    return step, row, tall, line, specs, arrays


def ffn_up_down(own, other, views, first):
    rows, depth = own.shape
    hidden = first.shape[2]
    count = len(views)
    step, row, tall, line, specs, arrays = ffn_blocks(views, rows, depth, hidden)

    def kernel(own_ref, other_ref, b_ref, *rest):
        weights, (act_ref, slope_ref, keep_ref, send_ref, pair, acc) = rest[:-6], rest[-6:]
        j = pl.program_id(0)

        @pl.when(j == 0)
        def _():
            pair[:rows, :] = own_ref[...]
            pair[rows:, :] = other_ref[...]

        total = None
        for v in range(count):
            u = dot(pair[...], weights[2 * v][0], (1, 0)) + b_ref[v]
            phi = 0.5 * (1.0 + lax.erf(u * 0.7071067811865476))
            act = (u * phi).astype(BF)
            act_ref[v] = act
            slope_ref[v] = (phi + u * 0.3989422804014327 * jnp.exp(-0.5 * u * u)).astype(BF)
            term = dot(act, weights[2 * v + 1][0], (1, 1))
            total = term if total is None else total + term

        @pl.when(j == 0)
        def _():
            acc[...] = total

        @pl.when(j > 0)
        def _():
            acc[...] += total

        @pl.when(j == hidden // step - 1)
        def _():
            keep_ref[...] = acc[:rows, :]
            send_ref[...] = acc[rows:, :].astype(BF)

    wide = (count, 2 * rows, hidden)
    return run(
        kernel, [], [own, other, first, *arrays],
        [(wide, BF), (wide, BF), ((rows, depth), F32), ((rows, depth), BF)],
        [pltpu.VMEM((2 * rows, depth), BF), pltpu.VMEM((2 * rows, depth), F32)],
        "ffn_up_down", 8 * rows * depth * hidden * count, (hidden // step,),
        [row, row, line] + specs, [tall, tall, row, row],
    )


def ffn_down_up(own, other, views, slope):
    rows, depth = own.shape
    hidden = slope.shape[2]
    count = len(views)
    step, row, tall, line, specs, arrays = ffn_blocks(views, rows, depth, hidden)

    def kernel(own_ref, other_ref, slope_ref, *rest):
        weights, (du_ref, sum_ref, keep_ref, send_ref, pair, acc) = rest[:-6], rest[-6:]
        j = pl.program_id(0)

        @pl.when(j == 0)
        def _():
            pair[:rows, :] = own_ref[...]
            pair[rows:, :] = other_ref[...]

        total = None
        for v in range(count):
            du = (dot(pair[...], weights[2 * v + 1][0], (1, 0)) * slope_ref[v].astype(F32)).astype(BF)
            du_ref[v] = du
            sum_ref[v] = jnp.sum(du.astype(F32), 0, keepdims=True)
            term = dot(du, weights[2 * v][0], (1, 1))
            total = term if total is None else total + term

        @pl.when(j == 0)
        def _():
            acc[...] = total

        @pl.when(j > 0)
        def _():
            acc[...] += total

        @pl.when(j == hidden // step - 1)
        def _():
            keep_ref[...] = acc[:rows, :]
            send_ref[...] = acc[rows:, :].astype(BF)

    return run(
        kernel, [], [own, other, slope, *arrays],
        [
            ((count, 2 * rows, hidden), BF), ((count, 1, hidden), F32),
            ((rows, depth), F32), ((rows, depth), BF),
        ],
        [pltpu.VMEM((2 * rows, depth), BF), pltpu.VMEM((2 * rows, depth), F32)],
        "ffn_down_up", 8 * rows * depth * hidden * count, (hidden // step,),
        [row, row, tall] + specs, [tall, line, row, row],
    )


def split_blocks(full, keep_ref, send_ref, at, core, blocks, size):
    for p in range(blocks // 2):
        mine = multiple((2 * p + core) * size, size)
        theirs = multiple((2 * p + 1 - core) * size, size)
        keep_ref[at + (p,)] = full[pl.ds(mine, size), :]
        send_ref[at + (p,)] = full[pl.ds(theirs, size), :]


def ffn_weight_grads(x_own, x_other, e_own, e_other, du, act, core, blocks):
    rows, depth = x_own.shape
    count, _, hidden = du.shape
    step = min(512, hidden)
    per = hidden // step
    size = depth // blocks
    split = core is not None

    def kernel(core_ref, x_ref, xo_ref, e_ref, eo_ref, du_ref, act_ref, *rest):
        outs, (xs, es, full) = rest[:-3], rest[-3:]

        @pl.when(pl.program_id(0) == 0)
        def _():
            xs[:rows, :] = x_ref[...]
            xs[rows:, :] = xo_ref[...]
            es[:rows, :] = e_ref[...]
            es[rows:, :] = eo_ref[...]

        up = dot(xs[...], du_ref[0], (0, 0)).astype(BF)
        down = dot(es[...], act_ref[0], (0, 0)).astype(BF)
        if split:
            full[...] = up
            split_blocks(full, outs[0], outs[1], (), core_ref[0], blocks, size)
            full[...] = down
            split_blocks(full, outs[2], outs[3], (), core_ref[0], blocks, size)
        else:
            outs[0][0] = up
            outs[0][1] = down

    row = pl.BlockSpec((rows, depth), lambda j: (0, 0))
    tall = pl.BlockSpec((1, 2 * rows, step), lambda j: (j // per, 0, j % per))
    if split:
        part = pl.BlockSpec((blocks // 2, size, step), lambda j: (0, 0, j))
        outs, out_blocks = [((blocks // 2, size, hidden * count), BF)] * 4, [part] * 4
    else:
        outs = [((2 * count, depth, hidden), BF)]
        out_blocks = [pl.BlockSpec((2, depth, step), lambda j: (j // per, 0, j % per))]
    return run(
        kernel, [core if split else jnp.zeros((1,), jnp.int32)],
        [x_own, x_other, e_own, e_other, du, act], outs,
        [
            pltpu.VMEM((2 * rows, depth), BF),
            pltpu.VMEM((2 * rows, depth), BF),
            pltpu.VMEM((depth, step), BF),
        ],
        "ffn_weight_grads", 8 * rows * depth * hidden * count, (count * per,),
        [row, row, row, row, tall, tall], out_blocks,
    )


def weight_grads(groups, core, blocks):
    arrays, places = [], []
    for group in groups:
        for pair in group:
            spot = []
            for array in pair:
                known = [i for i, a in enumerate(arrays) if a is array]
                if not known:
                    arrays.append(array)
                    known = [len(arrays) - 1]
                spot.append(known[0])
            places.append(spot)
    depth, width = groups[0][0][0].shape[1], groups[0][0][1].shape[1]
    size = depth // blocks
    count = len(arrays)

    def kernel(core_ref, *rest):
        outs, full = rest[count:-1], rest[-1]
        number = 0
        for g, group in enumerate(groups):
            for j in range(len(group)):
                left, right = places[number]
                value = dot(rest[left][...], rest[right][...], (0, 0)).astype(BF)
                if core is None:
                    outs[g][j] = value
                else:
                    full[...] = value
                    split_blocks(
                        full, outs[2 * g], outs[2 * g + 1], (j,), core_ref[0], blocks, size
                    )
                number += 1

    outs = []
    for group in groups:
        if core is None:
            outs.append(((len(group), depth, width), BF))
        else:
            outs += [((len(group), blocks // 2, size, width), BF)] * 2
    flops = sum(2 * left.shape[0] * depth * width for group in groups for left, right in group)
    return run(
        kernel, [jnp.zeros((1,), jnp.int32) if core is None else core], arrays, outs,
        [pltpu.VMEM((depth, width), BF)], "weight_grads", flops,
    )


def norm_grad_body(terms, summed, gain, grad_ref, low_ref, sums_ref):
    grad = terms[0][...].astype(F32)
    for ref in terms[1:]:
        grad = grad + ref[...].astype(F32)
    total = summed[...]
    center = total - jnp.mean(total, -1, keepdims=True)
    scale = lax.rsqrt(jnp.mean(center * center, -1, keepdims=True) + 1e-05)
    unit = center * scale
    inner = grad * gain
    out = scale * (
        inner - jnp.mean(inner, -1, keepdims=True) - unit * jnp.mean(inner * unit, -1, keepdims=True)
    )
    low = out.astype(BF)
    grad_ref[...] = out
    low_ref[...] = low
    sums_ref[0:1, :] = jnp.sum(low.astype(F32), 0, keepdims=True)
    sums_ref[1:2, :] = jnp.sum(grad * unit, 0, keepdims=True)
    sums_ref[2:3, :] = jnp.sum(grad, 0, keepdims=True)
    return low


def norm_grad(terms, summed, gain, line):
    shape = summed.shape

    def kernel(sum_ref, gain_ref, *rest):
        norm_grad_body(rest[: len(terms)], sum_ref, gain_ref[line : line + 1, :], *rest[len(terms) :])

    return run(
        kernel, [], [summed, gain, *terms], [(shape, F32), (shape, BF), ((3, shape[1]), F32)], [],
        "norm_grad", 1e6,
    )


def norm_out_grad(terms, summed, gain, line, weight):
    shape = summed.shape
    count, depth, width = weight.shape

    def kernel(sum_ref, gain_ref, w_ref, *rest):
        outs = rest[len(terms) :]
        low = norm_grad_body(rest[: len(terms)], sum_ref, gain_ref[line : line + 1, :], *outs[:3])
        for mask in range(count):
            outs[3 + mask][...] = dot(low, w_ref[mask], (1, 0)).astype(BF)

    return run(
        kernel, [], [summed, gain, weight, *terms],
        [(shape, F32), (shape, BF), ((3, shape[1]), F32)] + [((shape[0], width), BF)] * count, [],
        "norm_out_grad", 2 * shape[0] * depth * width * count,
    )


def input_grads(dq, own, below, above, weights, t_index, count):
    tokens, width = dq.shape
    rows, depth = tokens // count, weights.shape[1]
    ahead = weights.shape[0] - 2

    def kernel(t_ref, w_ref, dq_ref, own_ref, below_ref, above_ref, dk_ref, dv_ref, sums_ref, *rest):
        full = rest[count]
        for j, ref in enumerate((dk_ref, dv_ref)):
            ref[...] = (
                own_ref[j] + below_ref[j].astype(F32) + above_ref[j].astype(F32)
            ).astype(BF)
        sums_ref[0:1, :] = jnp.sum(dq_ref[...].astype(F32), 0, keepdims=True)
        sums_ref[1:2, :] = jnp.sum(dv_ref[...].astype(F32), 0, keepdims=True)
        total = dot(dk_ref[...], w_ref[ahead], (1, 1)) + dot(dv_ref[...], w_ref[ahead + 1], (1, 1))
        if ahead:
            total = total + dot(dq_ref[...], w_ref[0], (1, 1))
        full[...] = total
        for mask in range(count):
            part = full[pl.ds(multiple((t_ref[0] ^ mask) * rows, rows), rows), :]
            rest[mask][...] = part.astype(rest[mask].dtype)

    return run(
        kernel, [t_index], [weights, dq, own, below, above],
        [((tokens, width), BF)] * 2 + [((2, width), F32), ((rows, depth), F32)]
        + [((rows, depth), BF)] * (count - 1),
        [pltpu.VMEM((tokens, depth), F32)], "input_grads",
        2 * tokens * width * depth * weights.shape[0],
    )


def asked_grad(pieces, weight):
    count, depth, width = weight.shape
    rows = pieces[0].shape[0]

    def kernel(w_ref, *rest):
        total = dot(rest[0][...], w_ref[0], (1, 1))
        for mask in range(1, count):
            total = total + dot(rest[mask][...], w_ref[mask], (1, 1))
        rest[count][...] = total

    return run(
        kernel, [], [weight, *pieces], [((rows, depth), F32)], [], "asked_grad",
        2 * rows * depth * width * count,
    )[0]


def by_mask(values, t_index, count):
    tokens, width = values.shape
    rows = tokens // count

    def kernel(t_ref, x_ref, *outs):
        for mask in range(count):
            outs[mask][...] = x_ref[pl.ds(multiple((t_ref[0] ^ mask) * rows, rows), rows), :]

    return run(kernel, [t_index], [values], [((rows, width), BF)] * count, [], "by_mask", 1000)


def in_order(pieces, t_index):
    count = len(pieces)
    rows, width = pieces[0].shape

    def kernel(t_ref, *refs):
        place_rows(refs[count], refs[:count], t_ref[0])

    return run(
        kernel, [t_index], pieces, [((rows * count, width), BF)], [], "in_order", 1000
    )[0]


LINES = 32
ENC_ATT, ENC_FFN, SELF_ATT, CROSS_ATT, DEC_FFN, ENC_FIRST, DEC_FIRST = 0, 5, 8, 13, 18, 21, 25


def pack_small(arrays, width):
    def kernel(*refs):
        lines = []
        for ref in refs[:-1]:
            value = ref[...].astype(F32)
            if value.shape[1] > width:
                value = jnp.concatenate(
                    [value[:, i : i + width] for i in range(0, value.shape[1], width)], 0
                )
            lines.append(value)
        used = sum(value.shape[0] for value in lines)
        lines.append(jnp.zeros((LINES - used, width), F32))
        whole = jnp.concatenate(lines, 0)
        refs[-1][...] = jnp.concatenate([whole[: LINES // 2], whole[LINES // 2 :]], 1).astype(BF)

    blocks = [pl.BlockSpec(array.shape, lambda i: (0, 0)) for array in arrays]
    shape = (LINES // 2, 2 * width)
    return run(
        kernel, [], arrays, [(shape, BF)], [], "pack_small", 0, (1,), blocks,
        [pl.BlockSpec(shape, lambda i: (0, 0))],
    )[0]


def unpack_small(parts, t_index, count, features, wide_masks):
    peers, lines, width = parts.shape[0], LINES, parts.shape[2] // 2
    share_ = peers // count
    quarter = 4
    hidden = share_ * quarter * width

    def kernel(t_ref, x_ref, table, local, enc_ref, dec_ref):
        for f in range(peers):
            value = x_ref[f].astype(F32)
            span = slice(f * width, (f + 1) * width)
            table[: lines // 2, span] = value[:, :width]
            table[lines // 2 :, span] = value[:, width:]
        for mask in range(count):
            local[mask] = table[:, pl.ds(multiple((t_ref[0] ^ mask) * features, 128), features)]
        for ref, first in ((enc_ref, ENC_FIRST), (dec_ref, DEC_FIRST)):
            for v, mask in enumerate(wide_masks):
                for f in range(share_):
                    for q in range(quarter):
                        at = (f * quarter + q) * width
                        ref[v, :, at : at + width] = local[
                            mask, first + q : first + q + 1, f * width : (f + 1) * width
                        ]

    first = ((len(wide_masks), 1, hidden), F32)
    return run(
        kernel, [t_index], [parts],
        [((lines, peers * width), F32), ((count, lines, features), F32), first, first], [],
        "unpack_small", 0,
    )


def pack_grads(sums, columns, firsts, t_index, peers, wide_masks):
    depth = sums[0].shape[1]
    width = depth // peers
    features = columns[0].shape[1]
    share_ = features // width
    quarter = 4
    arrays = list(sums) + list(columns) + list(firsts)

    def kernel(t_ref, *refs):
        out, table = refs[-2:]
        table[...] = jnp.zeros_like(table)
        own = pl.ds(multiple(t_ref[0] * features, 128), features)
        att = (ENC_ATT, SELF_ATT, CROSS_ATT)
        for first, s_ref, c_ref in zip(att, refs[:3], refs[5:8]):
            table[first + 2 : first + 5, :] = s_ref[...]
            table[first : first + 2, own] = c_ref[...]
        for first, s_ref in zip((ENC_FFN, DEC_FFN), refs[3:5]):
            table[first : first + 3, :] = s_ref[...]
        for first, f_ref in zip((ENC_FIRST, DEC_FIRST), refs[8:10]):
            for v, mask in enumerate(wide_masks):
                strip = []
                for q in range(quarter):
                    pieces = []
                    for f in range(share_):
                        at = (f * quarter + q) * width
                        pieces.append(f_ref[v, :, at : at + width])
                    strip.append(jnp.concatenate(pieces, 1))
                there = pl.ds(multiple((t_ref[0] ^ mask) * features, 128), features)
                table[first : first + quarter, there] = jnp.concatenate(strip, 0)
        for f in range(peers):
            out[f] = table[:, f * width : (f + 1) * width]

    return run(
        kernel, [t_index], arrays, [((peers, LINES, width), F32)],
        [pltpu.VMEM((LINES, depth), F32)], "pack_grads", 0,
    )[0]


def unpack_grads(terms, shapes):
    def kernel(*refs):
        value = refs[0][...]
        for ref in refs[1 : len(terms)]:
            value = value + ref[...]
        width = value.shape[1]
        line = 0
        for ref in refs[len(terms) :]:
            rows, columns = ref.shape
            for r in range(rows):
                for at in range(0, columns, width):
                    ref[r : r + 1, at : at + width] = value[line : line + 1, :]
                    line += 1

    return run(kernel, [], terms, [(shape, F32) for shape in shapes], [], "unpack_grads", 0)


def token_spans(seq_lens, pic_start, pic_len, base, tokens, block):
    count, pictures = pic_start.shape
    blocks = tokens // block

    def kernel(lens, starts, extents, base_ref, both, text, both_bounds, text_bounds):
        places = lax.broadcasted_iota(jnp.int32, (1, tokens), 1) + tokens
        zero = jnp.zeros((1, tokens), jnp.int32)
        begin, end = zero, zero
        low, high = [zero] * pictures, [zero] * pictures
        edges = [
            [jnp.int32(3 * tokens), jnp.int32(0), jnp.int32(tokens + (i + 1) * block)]
            for i in range(blocks)
        ]
        start = tokens - base_ref[0]
        for s in range(count):
            stop = start + lens[s]
            inside = (places >= start) & (places < stop)
            begin = jnp.where(inside, start, begin)
            end = jnp.where(inside, stop, end)
            spans = []
            for k in range(pictures):
                first = start + starts[s, k]
                last = jnp.minimum(first + extents[s, k], stop)
                member = inside & (places >= first) & (places < last)
                low[k] = jnp.where(member, first, low[k])
                high[k] = jnp.where(member, last, high[k])
                spans.append((first, last))
            for i in range(blocks):
                from_, to = tokens + i * block, tokens + (i + 1) * block
                meets = (start < to) & (stop > from_)
                edge = edges[i]
                edge[0] = jnp.where(meets, jnp.minimum(edge[0], start), edge[0])
                edge[1] = jnp.where(meets, jnp.maximum(edge[1], stop), edge[1])
                for first, last in spans:
                    touches = (first < to) & (last > from_)
                    edge[2] = jnp.where(touches, jnp.maximum(edge[2], last), edge[2])
            start = stop
        both[...] = jnp.concatenate([begin, end] + [zero] * 6, 0)
        seen = [begin, places + 1]
        for k in range(pictures):
            seen += [low[k], high[k]]
        text[...] = jnp.concatenate(seen + [zero] * (8 - len(seen)), 0)
        for i in range(blocks):
            first = lax.div(edges[i][0], jnp.int32(block))
            both_bounds[2 * i] = first
            both_bounds[2 * i + 1] = lax.div(edges[i][1] + (block - 1), jnp.int32(block))
            text_bounds[2 * i] = first
            text_bounds[2 * i + 1] = lax.div(edges[i][2] + (block - 1), jnp.int32(block))

    whole = pl.BlockSpec(memory_space=pltpu.VMEM)
    scalars = pl.BlockSpec(memory_space=pltpu.SMEM)
    return run(
        kernel, [seq_lens, pic_start, pic_len, base], [],
        [((8, tokens), jnp.int32)] * 2 + [((2 * blocks,), jnp.int32)] * 2, [], "token_spans", 0,
        None, None, [whole, whole, scalars, scalars],
    )


def per_device(
    enc_in,
    dec_in,
    enc_cot,
    dec_cot,
    seq_lens,
    pic_start,
    pic_len,
    enc_attn_w,
    enc_attn_bias,
    enc_attn_norm,
    enc_ffn_w,
    enc_ffn_b1,
    enc_ffn_vec,
    self_attn_w,
    self_attn_bias,
    self_attn_norm,
    cross_attn_w,
    cross_attn_bias,
    cross_attn_norm,
    dec_ffn_w,
    dec_ffn_b1,
    dec_ffn_vec,
):
    rows = enc_in.shape[0]
    tensor_size = lax.axis_size("tensor")
    fsdp_size = lax.axis_size("fsdp")
    t_index = lax.axis_index("tensor")
    f_index = lax.axis_index("fsdp")
    t_ref = t_index[None].astype(jnp.int32)
    core = (f_index % 2)[None].astype(jnp.int32)
    tokens = rows * tensor_size
    features = enc_attn_w.shape[2]
    hidden = enc_ffn_w.shape[2]
    t_down = bits_of("tensor")[::-1]
    t_up = bits_of("tensor")
    wide_down = t_down[:-1]
    wide_up = t_up[1:]
    t_masks = range(tensor_size)
    wide_masks = range(0, tensor_size, 2)
    wide_count = len(wide_masks)

    small = [
        enc_attn_bias, enc_attn_norm, enc_ffn_vec, self_attn_bias, self_attn_norm,
        cross_attn_bias, cross_attn_norm, dec_ffn_vec, enc_ffn_b1, dec_ffn_b1,
    ]
    block = min(256, tokens)
    base = (f_index * tokens)[None].astype(jnp.int32)
    spans = token_spans(seq_lens, pic_start, pic_len, base, tokens, block)
    both = (spans[0], spans[2], 1)
    text = (spans[1], spans[3], 1 + pic_start.shape[1])

    first_order, second_order = plane_orders()

    def later(value, ready):
        return lax.optimization_barrier((value, ready))[0]

    class Pair:
        def __init__(self, halves, splits):
            self.plans = [
                Gather(half[None], order, split)
                for half, order, split in zip(halves, (first_order, second_order), splits)
            ]

        def hop(self, *gate):
            if self.plans[0].came is not None:
                came_ = join([plan.came for plan in self.plans], *gate)
                for plan, value in zip(self.plans, came_):
                    plan.came = value
                gate = ()
            return [plan.hop(*gate) for plan in self.plans]

        def result(self):
            return [plan.result() for plan in self.plans]

    slices = hidden // features

    def ffn_slices(shard):
        cut = shard.reshape(2, rows, slices, features)
        return jnp.moveaxis(cut, 2, 1).reshape(2 * slices, rows, features)

    def ffn_halves(shards):
        cut = [ffn_slices(shard) for shard in shards]
        half = (wide_count + 1) // 2
        return cut[:half], cut[half:]

    def ffn_views(low, high):
        views = []
        for array in (low, high):
            for at in range(0, array.shape[0], 2 * slices):
                views.append((array, at, array, at + slices))
        return views

    def exchange(pieces_):
        held = dict(enumerate(pieces_))
        for bit in t_up:
            moved = [mask for mask in t_masks if mask & bit]
            came_ = swap(jnp.stack([held[mask] for mask in moved]), "tensor", bit)
            for at, mask in enumerate(moved):
                held[mask] = came_[at]
        return [held[mask] for mask in t_masks]

    def doubled(value):
        held = {0: value}
        for bit in t_down:
            known = sorted(held)
            came_ = swap(jnp.stack([held[mask] for mask in known]), "tensor", bit)
            gate = yield came_
            came_ = join(came_, *(gate or ()))
            for at, mask in enumerate(known):
                held[mask | bit] = came_[at]
        yield [held[mask] for mask in t_masks]

    peers = fsdp_size
    up_pairs = [(i, i + 1) for i in range(peers - 1)]
    down_pairs = [(j, i) for i, j in up_pairs]

    def halo(pair):
        before = lax.ppermute(pair, "fsdp", up_pairs)
        after = lax.ppermute(pair, "fsdp", down_pairs)
        return before, pair, after

    def attend_fg(queries, window, mode):
        return attend(queries, window, mode[0], mode[1], t_ref, tensor_size, mode[2])

    def attend_back_fg(queries, window, grads, mixed_t, totals, mode):
        return attend_back(
            queries, window, grads, mixed_t, totals, mode[0], mode[1], t_ref, tensor_size, mode[2]
        )

    class Folds:
        def __init__(self, parts_, at):
            self.folds = [
                Fold(parts_[2 * k], parts_[2 * k + 1], order[:-1], at)
                for k, order in enumerate((first_order, second_order))
            ]

        def hop(self, *gate):
            return [fold.hop(*gate) for fold in self.folds]

        def next(self, *gate):
            came_ = join([fold.came for fold in self.folds], *gate)
            for fold, value in zip(self.folds, came_):
                fold.came = value
            return [fold.next() for fold in self.folds]

        def result(self, *gate):
            return [fold.result(*gate) for fold in self.folds]

    class SmallSum:
        def __init__(self, value):
            self.value, self.came = value, None
            self.bits = [("fsdp", bit) for bit in bits_of("fsdp")[::-1]]
            self.bits += [("tensor", bit) for bit in t_up]

        def hop(self):
            if self.came is not None:
                self.value = self.value + self.came
            axis, bit = self.bits.pop(0)
            sent = self.value
            if axis == "fsdp":
                half = self.value.shape[0] // 2
                mine = (f_index // bit) % 2
                sent = lax.dynamic_slice_in_dim(self.value, (1 - mine) * half, half, 0)
                self.value = lax.dynamic_slice_in_dim(self.value, mine * half, half, 0)
            self.came = swap(sent, axis, bit)

        def result(self):
            while self.bits:
                self.hop()
            return [self.value[0], self.came[0]]

    class WideShare:
        def __init__(self, halves):
            self.held = {
                mask: halves[:, :, j * hidden : (j + 1) * hidden]
                for j, mask in enumerate(wide_masks)
            }
            self.bits = list(wide_up)

        def hop(self):
            bit = self.bits.pop(0)
            new = []
            for mask in sorted(self.held):
                if mask not in self.held or mask & (2 * bit - 1):
                    continue
                came_ = swap(self.held.pop(mask | bit).astype(BF), "tensor", bit)
                self.held[mask] = self.held[mask] + came_.astype(F32)
                new.append(came_)
            self.came = new
            return new

        def result(self):
            while self.bits:
                self.hop()
            return self.held[0]

    pending = [[], []]

    def due(*values):
        pending[1].extend(values)

    def fg(value):
        waits = pending.pop(0)
        pending.append([])
        return join(value, *waits)

    packed = pack_small(small, enc_attn_bias.shape[1])
    depth = enc_in.shape[1]
    enc_pieces = reach(
        jnp.concatenate([enc_in, enc_attn_w[3]], 1), "tensor", t_masks[:0:-1]
    )
    first_shard = jnp.concatenate([enc_attn_w[:3].reshape(-1, features), packed])
    qkv_plan = Gather(first_shard[None], first_order, [(3, rows), (1, packed.shape[0])])
    qkv_plan.hop()
    enc_qkv, parts = qkv_plan.result()
    table, local, enc_first, dec_first = unpack_small(
        parts.reshape(fsdp_size, -1, features), t_ref, tensor_size, features, wide_masks
    )
    plan1 = Pair(
        (self_attn_w[:3], jnp.stack([piece[:, depth:] for piece in enc_pieces])),
        ([3], [tensor_size]),
    )
    due(plan1.hop())
    dec_steps = doubled(
        join(
            jnp.concatenate([dec_in, self_attn_w[3], cross_attn_w[3], cross_attn_w[0]], 1),
            *enc_pieces[1:],
        )
    )
    due(next(dec_steps))

    flat_e, pair_e, query_e = project(
        fg(enc_pieces), enc_qkv, local, (ENC_ATT, None, ENC_ATT + 1), t_ref
    )
    window_e = halo(pair_e)
    r1 = (window_e[0], window_e[2])
    plan1.hop(*r1)
    dec_pieces = dec_steps.send(r1)

    mixed_e, mixed_t_e, totals_e = attend_fg(fg(query_e), window_e, both)
    mixed_e = exchange(mixed_e)
    r2 = tuple(mixed_e[1:])
    plan1.hop(*r2)
    (self_qkv,), (enc_out_w,) = plan1.result()
    enc_wide = Spread(join(enc_ffn_w, *r2), "tensor", wide_down)
    enc_wide.hop()
    for step in range(len(t_down) - 1):
        dec_pieces = dec_steps.send(r2)

    summed_e, hid, hid_low = out_norm(
        fg(mixed_e), enc_out_w, enc_in, table, ENC_ATT + 2
    )
    hid_other = swap(hid_low, "tensor", 1)
    r3 = (hid_other,)
    flat_s, pair_s, query_s = project(
        fg(join(dec_pieces, hid_low)), self_qkv, local, (SELF_ATT, None, SELF_ATT + 1), t_ref
    )
    spare = [join(piece, *r3)[:, depth:] for piece in dec_pieces]

    def spare_part(which):
        return [piece[None, :, which * features : (which + 1) * features] for piece in spare]

    low_shards, high_shards = ffn_halves(enc_wide.result(*r3))
    low_count, high_count = len(low_shards) * 2 * slices, len(high_shards) * 2 * slices
    plan2 = Pair(
        (
            jnp.concatenate(low_shards + spare_part(0) + [cross_attn_w[1:3]]),
            jnp.concatenate(high_shards + spare_part(1) + spare_part(2)),
        ),
        ([low_count, tensor_size, 2], [high_count, tensor_size, tensor_size]),
    )
    plan2.hop()
    window_s = halo(pair_s)
    r4 = (window_s[0], window_s[2])
    mixed_s, mixed_t_s, totals_s = attend_fg(fg(query_s), window_s, text)
    mixed_s = exchange(mixed_s)
    r5 = tuple(mixed_s[1:])
    plan2.hop(*r5)
    dec_wide = Spread(join(dec_ffn_w, *r5), "tensor", wide_down)
    dec_wide.hop()
    plan2.hop(*r5)
    (low_views, self_out_w, cross_kv), (high_views, cross_out_w, cross_query) = plan2.result()
    enc_views = ffn_views(low_views, high_views)
    active_e, slope_e, keep, send = ffn_up_down(hid_low, hid_other, enc_views, enc_first)
    came = swap(send, "tensor", 1)
    r7 = (came,)
    low_shards, high_shards = ffn_halves(dec_wide.result(send))
    plan4 = Pair(
        (jnp.concatenate(low_shards), jnp.concatenate(high_shards)), ([low_count], [high_count])
    )
    plan4.hop()

    summed_s, decoded, decoded_low = out_norm(
        join(mixed_s, send), self_out_w, dec_in, table, SELF_ATT + 2
    )
    ffn_summed_e, encoded = add_norm(
        [hid, join(keep, decoded_low), came], table, ENC_FFN
    )
    enc_rows = spread(encoded, "tensor", t_down)
    plan4.hop(encoded)
    asked = exchange(project_rows(join(decoded_low, encoded), cross_query, local, CROSS_ATT))
    query_c = in_order(asked, t_ref)

    flat_c, pair_c = project(
        enc_rows, cross_kv, local, (None, CROSS_ATT + 1), t_ref
    )
    window_c = halo(pair_c)
    r9 = (window_c[0], window_c[2])
    plan4.hop(*r9)
    mixed_c, mixed_t_c, totals_c = attend_fg(query_c, window_c, both)
    mixed_c = exchange(mixed_c)
    (low_views,), (high_views,) = plan4.result()
    dec_views = ffn_views(low_views, high_views)
    summed_c, crossed, crossed_low = out_norm(
        mixed_c, cross_out_w, decoded, table, CROSS_ATT + 2
    )
    crossed_other = swap(crossed_low, "tensor", 1)
    active_d, slope_d, keep, send = ffn_up_down(
        crossed_low, crossed_other, dec_views, dec_first
    )
    came = swap(send, "tensor", 1)
    ffn_summed_d, final = add_norm([crossed, keep, came], table, DEC_FFN)

    grad_sum_d, low_d, dec_sums = norm_grad([dec_cot], ffn_summed_d, table, DEC_FFN + 1)
    other_d = swap(low_d, "tensor", 1)
    du_d, dec_first_sum, keep, send = ffn_down_up(low_d, other_d, dec_views, slope_d)
    came = swap(send, "tensor", 1)
    dec_grads = ffn_weight_grads(
        crossed_low, crossed_other, low_d, other_d, join(du_d, send), active_d, core, fsdp_size
    )
    dec_fold = Folds(dec_grads, 0)
    due(dec_fold.hop())

    grad_sum_c, low_c, sums_c, *given = norm_out_grad(
        [fg(grad_sum_d), join(keep, dec_grads), came], summed_c, table, CROSS_ATT + 3, cross_out_w
    )
    given = exchange(given)
    b2 = tuple(given[1:])
    due(dec_fold.next(*b2))
    dq_c, below, own, above = attend_back_fg(
        query_c, window_c, fg(given), mixed_t_c, totals_c, both
    )
    below = lax.ppermute(below, "fsdp", down_pairs)
    above = lax.ppermute(above, "fsdp", up_pairs)
    asked_c = exchange(by_mask(dq_c, t_ref, tensor_size))
    b3 = (below, above)
    due(dec_fold.next(*b3))
    dk_c, dv_c, columns_c, *blocks_c = input_grads(
        dq_c, fg(own), below, above, cross_kv, t_ref, tensor_size
    )
    source = Share(blocks_c, "tensor", t_up)
    due(source.hop())
    from_asked = asked_grad([join(asked_c[0], dk_c)] + asked_c[1:], cross_query)
    cross_grads = weight_grads(
        [
            [(flat_c, join(dk_c, from_asked)), (flat_c, dv_c)]
            + [(decoded_low, piece) for piece in asked_c],
            [(low_c, piece) for piece in mixed_c],
        ],
        core, fsdp_size,
    )
    cross_fold = Folds(cross_grads, 1)
    due(cross_fold.hop())

    grad_sum_s, low_s, sums_s, *given = norm_out_grad(
        [fg(join(grad_sum_c, cross_grads)), from_asked], summed_s, table, SELF_ATT + 3, self_out_w
    )
    given = exchange(given)
    b6 = tuple(given[1:])
    source.hop(*b6)
    due(cross_fold.next(*b6))
    dq_s, below, own, above = attend_back_fg(
        query_s, window_s, fg(given), mixed_t_s, totals_s, text
    )
    below = lax.ppermute(below, "fsdp", down_pairs)
    above = lax.ppermute(above, "fsdp", up_pairs)
    b7 = (below, above)
    due(cross_fold.next(*b7))
    dec_wide_share = WideShare(jnp.stack(dec_fold.result(*b7)))
    due(dec_wide_share.hop())
    grad_sum_f, low_f, enc_sums = norm_grad(
        [fg(join(enc_cot, dq_s))] + source.result(), ffn_summed_e, table, ENC_FFN + 1
    )
    other_f = swap(low_f, "tensor", 1)
    dk_s, dv_s, columns_s, *blocks_s = input_grads(
        dq_s, join(own, low_f), below, above, self_qkv, t_ref, tensor_size
    )
    b8 = dk_s
    target = Share(blocks_s, "tensor", t_up)
    due(target.hop())
    self_parts = weight_grads(
        [
            [(flat_s, join(dq_s, b8)), (flat_s, dk_s), (flat_s, dv_s)]
            + [(low_s, piece) for piece in mixed_s]
        ],
        core, fsdp_size,
    )
    self_fold = Fold(self_parts[0], self_parts[1], first_order[:-1], 1)
    due(self_fold.hop())
    du_e, enc_first_sum, keep, send = ffn_down_up(
        fg(join(low_f, self_parts)), other_f, enc_views, slope_e
    )
    came = swap(send, "tensor", 1)
    b10 = came
    due(target.hop(b10))
    due(self_fold.next(b10))
    enc_grads = ffn_weight_grads(
        hid_low, hid_other, low_f, other_f, join(du_e, send), active_e, core, fsdp_size
    )
    enc_fold = Folds(enc_grads, 0)
    due(enc_fold.hop())

    grad_sum_e, low_e, sums_e, *given = norm_out_grad(
        [grad_sum_f, fg(join(keep, enc_grads)), came], summed_e, table, ENC_ATT + 3, enc_out_w
    )
    given = exchange(given)
    b11 = tuple(given[1:])
    due(enc_fold.next(*b11))
    due(self_fold.next(*b11))
    dq_e, below, own, above = attend_back_fg(
        query_e, window_e, fg(given), mixed_t_e, totals_e, both
    )
    below = lax.ppermute(below, "fsdp", down_pairs)
    above = lax.ppermute(above, "fsdp", up_pairs)
    b12 = (below, above)
    enc_fold.next(*b12)
    cross_first, cross_outs = cross_fold.result(*b12)
    self_own = self_fold.result(*b12)
    late_share = Share(
        [
            jnp.stack([cross_first[2 + mask], cross_outs[mask], self_own[3 + mask]])
            for mask in t_masks
        ],
        "tensor", t_up,
    )
    dk_e, dv_e, columns_e, *blocks_e = input_grads(
        dq_e, fg(own), below, above, enc_qkv, t_ref, tensor_size
    )
    b13 = dk_e
    enc_share = Share(blocks_e, "tensor", t_up)
    enc_share.hop()
    small_sum = SmallSum(
        pack_grads(
            [sums_e, sums_s, sums_c, enc_sums, dec_sums], [columns_e, columns_s, columns_c],
            [enc_first_sum, dec_first_sum], t_ref, fsdp_size, wide_masks,
        )
    )
    small_sum.hop()
    enc_att = weight_grads(
        [
            [(flat_e, dq_e), (flat_e, join(dk_e, tuple(blocks_e))), (flat_e, dv_e)],
            [(low_e, piece) for piece in mixed_e],
        ],
        core, fsdp_size,
    )
    att_folds = Folds(enc_att, 1)
    att_folds.hop()

    def meet(*items):
        for item, came_ in zip(items, join([item.came for item in items])):
            item.came = came_

    meet(enc_share, small_sum, *att_folds.folds, *enc_fold.folds)
    att_folds.next()
    enc_share.hop()
    small_sum.hop()
    enc_wide_share = WideShare(jnp.stack(enc_fold.result()))
    enc_wide_share.hop()
    meet(small_sum, *att_folds.folds)
    att_folds.next()
    small_sum.hop()
    late_share.hop()
    meet(late_share, small_sum, *att_folds.folds)
    enc_att_own, enc_att_out = att_folds.result()
    out_share = Share([enc_att_out[mask] for mask in t_masks], "tensor", t_up)
    out_share.hop()
    late_share.hop()
    small_sum.hop()
    meet(out_share, late_share, small_sum)
    out_share.hop()
    small_out = unpack_grads(small_sum.result(), [item.shape for item in small])
    enc_grad = jnp.concatenate([enc_att_own, total(out_share.result())[None]])
    dec_ffn_grad = dec_wide_share.result()
    enc_ffn_grad = enc_wide_share.result()
    late = total(late_share.result())
    cross_grad = jnp.concatenate([late[0:1], cross_first[:2], late[1:2]])
    self_grad = jnp.concatenate([self_own[:3], late[2:3]])
    grad_source = total([grad_sum_e] + enc_share.result())
    grad_target = total([grad_sum_s] + target.result())

    (
        enc_bias_g, enc_norm_g, enc_vec_g, self_bias_g, self_norm_g,
        cross_bias_g, cross_norm_g, dec_vec_g, enc_b1_g, dec_b1_g,
    ) = small_out
    return (
        encoded,
        final,
        grad_source,
        grad_target,
        enc_grad,
        enc_bias_g,
        enc_norm_g,
        enc_ffn_grad,
        enc_b1_g,
        enc_vec_g,
        self_grad,
        self_bias_g,
        self_norm_g,
        cross_grad,
        cross_bias_g,
        cross_norm_g,
        dec_ffn_grad,
        dec_b1_g,
        dec_vec_g,
    )


def solution(mesh):
    rows = P(("fsdp", "tensor"), None)
    weight = P(None, "fsdp", "tensor")
    vector = P(None, "fsdp")
    att, ffn = (weight, vector, vector), (weight, vector, vector)
    in_specs = (rows,) * 4 + (P(),) * 3 + (att + ffn + att + att + ffn)
    out_specs = (rows,) * 4 + (att + ffn + att + att + ffn)
    return jax.shard_map(
        per_device, mesh=mesh, in_specs=in_specs, out_specs=out_specs, check_vma=False
    )
```

```python
import functools
import jax
import jax.numpy as jnp
from jax import lax
from jax.experimental import pallas as pl
from jax.experimental.pallas import tpu as pltpu
from jax.sharding import PartitionSpec as P

HD = 64
BF = jnp.bfloat16
F32 = jnp.float32
PACE = 30000000000


def bits_of(axis):
    count, bit, bits = lax.axis_size(axis), 1, []
    while bit < count:
        bits.append(bit)
        bit *= 2
    return bits


def swap(value, axis, mask):
    return lax.ppermute(value, axis, [(i, i ^ mask) for i in range(lax.axis_size(axis))])


def join(value, *ready):
    return lax.optimization_barrier((value, ready))[0] if ready else value


def spread(value, axis, order, gates=()):
    pieces = {0: value}
    for k, bit in enumerate(order):
        for mask in list(pieces):
            piece = pieces[mask]
            if mask and k < len(gates):
                piece = join(piece, *gates[k])
            pieces[mask | bit] = swap(piece, axis, bit)
    if len(gates) > len(order):
        return [pieces[0]] + [join(pieces[mask], *gates[-1]) for mask in sorted(pieces)[1:]]
    return [pieces[mask] for mask in sorted(pieces)]


def total(items):
    out = items[0].astype(F32)
    for item in items[1:]:
        out = out + item.astype(F32)
    return out


def plane_orders():
    bits = bits_of("fsdp")
    return bits[1:] + bits[:1], bits[1:][::-1] + bits[:1]


def placed(parts, index, splits):
    arrays = [array for array, masks in parts]
    total = sum(len(masks) for array, masks in parts)
    cols = arrays[0].shape[-1]
    shapes = [
        (width, total, arrays[0].shape[2], cols)
        if isinstance(width, int)
        else (width[0], total, width[1], cols)
        for width in splits
    ]
    moves_ = total * sum(1 if isinstance(width, int) else width[0] for width in splits)

    def kernel(index_ref, *refs):
        ins, outs, sems = refs[: len(parts)], refs[len(parts) : -1], refs[-1]
        copies = []
        for (array, masks), ref in zip(parts, ins):
            for at, mask in enumerate(masks):
                first = 0
                for out, width in zip(outs, splits):
                    if isinstance(width, int):
                        moves = [(ref.at[at, first : first + width], out.at[:, index_ref[0] ^ mask])]
                        first += width
                    else:
                        moves = []
                        for line in range(width[0]):
                            moves.append(
                                (ref.at[at, first : first + width[1]], out.at[line, index_ref[0] ^ mask])
                            )
                            first += width[1]
                    for source, target in moves:
                        copy = pltpu.make_async_copy(source, target, sems.at[len(copies)])
                        copy.start()
                        copies.append(copy)
        for copy in copies:
            copy.wait()

    outs = pl.pallas_call(
        kernel,
        out_shape=[jax.ShapeDtypeStruct(shape, arrays[0].dtype) for shape in shapes],
        in_specs=[pl.BlockSpec(memory_space=pltpu.SMEM)]
        + [pl.BlockSpec(memory_space=pl.ANY)] * len(arrays),
        out_specs=[pl.BlockSpec(memory_space=pltpu.VMEM)] * len(splits),
        scratch_shapes=[pltpu.SemaphoreType.DMA((moves_,))],
        compiler_params=pltpu.CompilerParams(vmem_limit_bytes=32 * 2**20),
        cost_estimate=pl.CostEstimate(flops=PACE, bytes_accessed=1, transcendentals=0),
        name="placed",
    )(index[None], *arrays)
    return [out.reshape(out.shape[0], -1, cols) for out in outs]


def gather_plane(shard, order, splits):
    return Gather(shard[None], order, splits).result()


def reach(value, axis, masks):
    pieces = {0: value}
    for mask in masks:
        pieces[mask] = swap(value, axis, mask)
    return [pieces[mask] for mask in sorted(pieces)]


class Gather:
    def __init__(self, held, order, splits):
        self.held, self.masks, self.order, self.splits = held, [0], list(order), splits
        self.came = None

    def take(self, gate):
        if self.came is not None:
            came = join(self.came, *gate)
            self.held = jnp.concatenate([self.held, came], 0)
            self.masks = self.masks + [mask | self.bit for mask in self.masks]

    def hop(self, *gate):
        self.take(gate)
        self.bit = self.order.pop(0)
        self.came = swap(self.held, "fsdp", self.bit)
        return self.came

    def result(self):
        while self.order:
            self.hop()
        parts = [(self.held, self.masks), (self.came, [mask | self.bit for mask in self.masks])]
        return placed(parts, lax.axis_index("fsdp"), self.splits)


class Spread:
    def __init__(self, value, axis, bits):
        self.axis, self.pieces, self.level, self.last = axis, {0: value}, 0, len(bits)
        self.masks = [m for m in range(lax.axis_size(axis)) if m & ~sum(bits) == 0]

    def hop(self, *gate):
        self.level += 1
        new = []
        for mask in self.masks[::-1]:
            if mask.bit_count() == self.level:
                low = mask & -mask
                piece = self.pieces[mask ^ low]
                if mask != low:
                    piece = join(piece, *gate)
                self.pieces[mask] = swap(piece, self.axis, low)
                new.append(self.pieces[mask])
        return new

    def result(self, *gate):
        while self.level < self.last:
            self.hop()
        return [join(self.pieces[m], *(gate if m else ())) for m in self.masks]


class Share:
    def __init__(self, pieces, axis, bits):
        self.axis, self.held, self.bits = axis, dict(enumerate(pieces)), list(bits)
        self.came, self.terms = None, [pieces[0]]

    def hop(self, *gate):
        if self.came is not None:
            came = join(self.came, *gate)
            for at, mask in enumerate(self.kept):
                if mask == 0:
                    self.terms.append(came[at])
                else:
                    self.held[mask] = self.held[mask].astype(F32) + came[at].astype(F32)
            self.came = None
        if self.bits:
            bit = self.bits.pop(0)
            sent = [mask for mask in sorted(self.held) if mask & bit]
            self.kept = [mask ^ bit for mask in sent]
            stack = jnp.stack([self.held.pop(mask).astype(BF) for mask in sent])
            self.came = swap(stack, self.axis, bit)
        return self.came

    def result(self):
        while self.bits or self.came is not None:
            self.hop()
        return self.terms


class Fold:
    def __init__(self, keep, send, order, at):
        bits = bits_of("fsdp")
        self.live, self.order, self.at = bits[1:][::-1], list(order), at
        split = keep.shape[:at] + (2,) * len(self.live) + keep.shape[at + 1 :]
        self.value, self.sent, self.bit = keep.reshape(split), send.reshape(split), bits[0]

    def hop(self, *gate):
        self.came = swap(join(self.sent, *gate), "fsdp", self.bit)
        return self.came

    def next(self, *gate):
        bit = self.order.pop(0)
        dim = self.at + self.live.index(bit)
        self.live.remove(bit)
        mine = (lax.axis_index("fsdp") // bit) % 2
        value, came = self.value, join(self.came, *gate)

        def pick(which):
            return lax.dynamic_index_in_dim(value, which, dim, False).astype(
                F32
            ) + lax.dynamic_index_in_dim(came, which, dim, False).astype(F32)

        self.value, self.sent, self.bit = pick(mine).astype(BF), pick(1 - mine).astype(BF), bit
        return self.hop()

    def result(self, *gate):
        while self.order:
            self.next(*gate)
            gate = ()
        return self.value.astype(F32) + join(self.came, *gate).astype(F32)


MIB = 2**20
HEAD_SCALE = HD ** (-0.5)


def run(kernel, scalars, arrays, outs, scratch, name, flops, grid=None, in_blocks=None, out_blocks=None):
    arrays = list(arrays)
    whole = pl.BlockSpec(memory_space=pltpu.VMEM)
    in_specs = [pl.BlockSpec(memory_space=pltpu.SMEM)] * len(scalars)
    in_specs += in_blocks if in_blocks else [whole] * len(arrays)
    extra = {"grid": grid} if grid else {}
    return pl.pallas_call(
        kernel,
        out_shape=[jax.ShapeDtypeStruct(shape, kind) for shape, kind in outs],
        in_specs=in_specs,
        out_specs=out_blocks if out_blocks else [whole] * len(outs),
        scratch_shapes=scratch,
        compiler_params=pltpu.CompilerParams(vmem_limit_bytes=40 * MIB),
        cost_estimate=pl.CostEstimate(
            flops=PACE, bytes_accessed=1, transcendentals=0
        ),
        name=name,
        **extra,
    )(*scalars, *arrays)


def dot(left, right, dims):
    return lax.dot_general(left, right, ((dims[:1], dims[1:]), ((), ())), preferred_element_type=F32)


def head_mask(rows, which, level):
    lane = lax.broadcasted_iota(jnp.int32, (rows, 128), 1)
    return jnp.where(lane // HD == which, level, 0.0).astype(BF)


def tile_allowed(meta, first, size, columns, ranges):
    place = lax.broadcasted_iota(jnp.int32, (size, columns), 0) + first
    allowed = (place >= meta[0:1]) & (place < meta[1:2])
    for k in range(1, ranges):
        allowed = allowed | ((place >= meta[2 * k : 2 * k + 1]) & (place < meta[2 * k + 1 : 2 * k + 2]))
    return allowed


def multiple(value, of):
    return pl.multiple_of(value, of)


def place_rows(ref, pieces, t_index):
    rows = pieces[0].shape[0]
    for mask, piece in enumerate(pieces):
        ref[pl.ds(multiple((t_index ^ mask) * rows, rows), rows), :] = piece[:, : ref.shape[1]]


def attend(queries, windows, meta, bounds, t_index, count, ranges):
    tokens, width = queries.shape
    heads, rows = width // HD, tokens // count
    block = min(256, tokens)
    tiles = 3 * tokens // block

    def kernel(bounds_ref, t_ref, meta_ref, q_ref, b_ref, w_ref, a_ref, *rest):
        o_refs, (ot_ref, lse_ref, keys, v_t, held, acc, nat) = rest[:count], rest[count:]
        for j, ref in enumerate((b_ref, w_ref, a_ref)):
            keys[j * tokens : (j + 1) * tokens, :] = ref[0]
            v_t[:, j * tokens : (j + 1) * tokens] = ref[1].T
        for i in range(tokens // block):
            low, high = bounds_ref[2 * i], bounds_ref[2 * i + 1]
            span = slice(i * block, (i + 1) * block)
            info = meta_ref[:, span]
            asked = []
            for h in range(heads):
                lanes = slice(h // 2 * 128, h // 2 * 128 + 128)
                asked.append(q_ref[span, lanes] * head_mask(block, h % 2, HEAD_SCALE))

            def scores(k, tops):
                first = multiple(k * block, block)
                allowed = tile_allowed(info, first, block, block, ranges)
                out = []
                for h in range(heads):
                    lanes = slice(h // 2 * 128, h // 2 * 128 + 128)
                    s = dot(keys[pl.ds(first, block), lanes], asked[h], (1, 1))
                    s = jnp.where(allowed, s, -1e30)
                    held[h, k] = s
                    out.append(jnp.maximum(tops[h], jnp.max(s, 0, keepdims=True)))
                return tuple(out)

            tops = lax.fori_loop(
                low, high, scores, tuple(jnp.full((1, block), -1e30, F32) for h in range(heads))
            )
            acc[...] = jnp.zeros_like(acc)

            def mixes(k, sums):
                first = multiple(k * block, block)
                out = []
                for h in range(heads):
                    p = jnp.exp(held[h, k] - tops[h])
                    out.append(sums[h] + jnp.sum(p, 0, keepdims=True))
                    some = slice(h * HD, (h + 1) * HD)
                    acc[some, :] += dot(v_t[some, pl.ds(first, block)], p.astype(BF), (1, 0))
                return tuple(out)

            sums = lax.fori_loop(
                low, high, mixes, tuple(jnp.zeros((1, block), F32) for h in range(heads))
            )
            for h in range(heads):
                some = slice(h * HD, (h + 1) * HD)
                acc[some, :] = acc[some, :] / sums[h]
                lse_ref[h : h + 1, span] = tops[h] + jnp.log(sums[h])
            ot_ref[:, span] = acc[...]
            nat[span, :] = acc[...].T.astype(BF)
        for mask in range(count):
            o_refs[mask][...] = nat[pl.ds(multiple((t_ref[0] ^ mask) * rows, rows), rows), :]

    out = run(
        kernel,
        [bounds, t_index],
        [meta, queries, *windows],
        [((rows, width), BF)] * count + [((width, tokens), F32), ((heads, tokens), F32)],
        [
            pltpu.VMEM((3 * tokens, width), BF),
            pltpu.VMEM((width, 3 * tokens), BF),
            pltpu.VMEM((heads, tiles, block, block), F32),
            pltpu.VMEM((width, block), F32),
            pltpu.VMEM((tokens, width), BF),
        ],
        "attend",
        4 * tokens * 3 * tokens * width * 4,
    )
    return out[:count], out[count], out[count + 1]


def attend_back(queries, windows, grads, mixed_t, totals, meta, bounds, t_index, count, ranges):
    tokens, width = queries.shape
    heads, rows = width // HD, tokens // count
    block = min(256, tokens)

    def kernel(bounds_ref, t_ref, meta_ref, q_ref, b_ref, w_ref, a_ref, ot_ref, lse_ref, *rest):
        g_refs = rest[:count]
        dq_ref, db_ref, dw_ref, da_ref, nat, keys, values, k_t, dk, dv, acc = rest[count:]
        place_rows(nat, g_refs, t_ref[0])
        for j, ref in enumerate((b_ref, w_ref, a_ref)):
            part = slice(j * tokens, (j + 1) * tokens)
            keys[part, :] = ref[0]
            values[part, :] = ref[1]
            k_t[:, part] = ref[0].T
        dk[...] = jnp.zeros_like(dk)
        dv[...] = jnp.zeros_like(dv)
        for i in range(tokens // block):
            low, high = bounds_ref[2 * i], bounds_ref[2 * i + 1]
            span = slice(i * block, (i + 1) * block)
            info = meta_ref[:, span]
            g_t = nat[span, :].astype(F32).T
            asked, given, inner = [], [], []
            for h in range(heads):
                lanes = slice(h // 2 * 128, h // 2 * 128 + 128)
                some = slice(h * HD, (h + 1) * HD)
                asked.append(q_ref[span, lanes] * head_mask(block, h % 2, HEAD_SCALE))
                given.append(nat[span, lanes] * head_mask(block, h % 2, 1.0))
                inner.append(jnp.sum(g_t[some] * ot_ref[some, span], 0, keepdims=True))
            acc[...] = jnp.zeros_like(acc)

            def step(k, carry):
                first = multiple(k * block, block)
                at = pl.ds(first, block)
                allowed = tile_allowed(info, first, block, block, ranges)
                for h in range(heads):
                    lanes = slice(h // 2 * 128, h // 2 * 128 + 128)
                    some = slice(h * HD, (h + 1) * HD)
                    s = dot(keys[at, lanes], asked[h], (1, 1))
                    p = jnp.exp(jnp.where(allowed, s, -1e30) - lse_ref[h : h + 1, span])
                    dp = dot(values[at, lanes], given[h], (1, 1))
                    ds = (p * (dp - inner[h])).astype(BF)
                    dv[at, lanes] += dot(p.astype(BF), given[h], (1, 0))
                    dk[at, lanes] += dot(ds, asked[h], (1, 0))
                    acc[some, :] += dot(k_t[some, at], ds, (1, 0))
                return carry

            lax.fori_loop(low, high, step, 0)
            dq_ref[span, :] = (acc[...] * HEAD_SCALE).T.astype(BF)
        for j, ref in enumerate((db_ref, dw_ref, da_ref)):
            part = slice(j * tokens, (j + 1) * tokens)
            ref[0] = dk[part, :].astype(ref.dtype)
            ref[1] = dv[part, :].astype(ref.dtype)

    pair = (2, tokens, width)
    return run(
        kernel,
        [bounds, t_index],
        [meta, queries, *windows, mixed_t, totals, *grads],
        [((tokens, width), BF), (pair, BF), (pair, F32), (pair, BF)],
        [
            pltpu.VMEM((tokens, width), BF),
            pltpu.VMEM((3 * tokens, width), BF),
            pltpu.VMEM((3 * tokens, width), BF),
            pltpu.VMEM((width, 3 * tokens), BF),
            pltpu.VMEM((3 * tokens, width), F32),
            pltpu.VMEM((3 * tokens, width), F32),
            pltpu.VMEM((width, block), F32),
        ],
        "attend_back",
        10 * tokens * 3 * tokens * width * 4,
    )


def project(pieces, weights, local, lines, t_index):
    count = len(pieces)
    rows, depth = pieces[0].shape[0], weights.shape[1]
    tokens, width = rows * count, weights.shape[2]
    outputs = weights.shape[0]

    def kernel(t_ref, w_ref, local_ref, *rest):
        x_ref = rest[count]
        place_rows(x_ref, rest[:count], t_ref[0])
        x = x_ref[...]
        done = []
        for k, line in enumerate(lines):
            value = dot(x, w_ref[k], (1, 0))
            if line is not None:
                value = value + local_ref[0, line : line + 1, :]
            done.append(value.astype(BF))
        if outputs == 3:
            rest[count + 2][...] = done[0]
        rest[count + 1][0] = done[-2]
        rest[count + 1][1] = done[-1]

    outs = [((tokens, depth), BF), ((2, tokens, width), BF)]
    if outputs == 3:
        outs.append(((tokens, width), BF))
    return run(
        kernel, [t_index], [weights, local, *pieces], outs, [], "project",
        2 * tokens * depth * width * outputs,
    )


def project_rows(low, weight, local, line):
    count, depth, width = weight.shape

    def kernel(x_ref, w_ref, local_ref, *outs):
        for mask in range(count):
            outs[mask][...] = (
                dot(x_ref[...], w_ref[mask], (1, 0)) + local_ref[mask, line : line + 1, :]
            ).astype(BF)

    return run(
        kernel, [], [low, weight, local], [((low.shape[0], width), BF)] * count, [],
        "project_rows", 2 * low.shape[0] * depth * width * count,
    )


def normed(total, gain, shift):
    center = total - jnp.mean(total, -1, keepdims=True)
    scale = lax.rsqrt(jnp.mean(center * center, -1, keepdims=True) + 1e-05)
    return center * scale * gain + shift


def out_norm(mixed, weight, residual, vectors, line):
    count, depth, width = weight.shape
    shape = residual.shape

    def kernel(w_ref, r_ref, v_ref, *rest):
        total = r_ref[...].astype(F32) + v_ref[line : line + 1, :]
        for mask in range(count):
            total = total + dot(rest[mask][...], w_ref[mask], (1, 1))
        sum_ref, out_ref, low_ref = rest[count:]
        sum_ref[...] = total
        out = normed(total, v_ref[line + 1 : line + 2, :], v_ref[line + 2 : line + 3, :])
        out_ref[...] = out
        low_ref[...] = out.astype(BF)

    return run(
        kernel, [], [weight, residual, vectors, *mixed], [(shape, F32), (shape, F32), (shape, BF)],
        [], "out_norm", 2 * shape[0] * depth * width * count,
    )


def add_norm(terms, vectors, line):
    shape = terms[0].shape

    def kernel(v_ref, *rest):
        total = v_ref[line : line + 1, :]
        for ref in rest[: len(terms)]:
            total = total + ref[...].astype(F32)
        sum_ref, low_ref = rest[len(terms) :]
        sum_ref[...] = total
        out = normed(total, v_ref[line + 1 : line + 2, :], v_ref[line + 2 : line + 3, :])
        low_ref[...] = out.astype(BF)

    return run(
        kernel, [], [vectors, *terms], [(shape, F32), (shape, BF)], [], "add_norm", 1e6
    )


def ffn_blocks(views, rows, depth, hidden):
    step = views[0][0].shape[2]
    row = pl.BlockSpec((rows, depth), lambda j: (0, 0))

    def weight(first):
        return pl.BlockSpec((1, depth, step), lambda j: (first + j, 0, 0))

    tall = pl.BlockSpec((len(views), 2 * rows, step), lambda j: (0, 0, j))
    line = pl.BlockSpec((len(views), 1, step), lambda j: (0, 0, j))
    specs, arrays = [], []
    for up, up_first, down, down_first in views:
        specs += [weight(up_first), weight(down_first)]
        arrays += [up, down]
    return step, row, tall, line, specs, arrays


def ffn_up_down(own, other, views, first):
    rows, depth = own.shape
    hidden = first.shape[2]
    count = len(views)
    step, row, tall, line, specs, arrays = ffn_blocks(views, rows, depth, hidden)

    def kernel(own_ref, other_ref, b_ref, *rest):
        weights, (act_ref, slope_ref, keep_ref, send_ref, pair, acc) = rest[:-6], rest[-6:]
        j = pl.program_id(0)

        @pl.when(j == 0)
        def _():
            pair[:rows, :] = own_ref[...]
            pair[rows:, :] = other_ref[...]

        total = None
        for v in range(count):
            u = dot(pair[...], weights[2 * v][0], (1, 0)) + b_ref[v]
            phi = 0.5 * (1.0 + lax.erf(u * 0.7071067811865476))
            act = (u * phi).astype(BF)
            act_ref[v] = act
            slope_ref[v] = (phi + u * 0.3989422804014327 * jnp.exp(-0.5 * u * u)).astype(BF)
            term = dot(act, weights[2 * v + 1][0], (1, 1))
            total = term if total is None else total + term

        @pl.when(j == 0)
        def _():
            acc[...] = total

        @pl.when(j > 0)
        def _():
            acc[...] += total

        @pl.when(j == hidden // step - 1)
        def _():
            keep_ref[...] = acc[:rows, :]
            send_ref[...] = acc[rows:, :].astype(BF)

    wide = (count, 2 * rows, hidden)
    return run(
        kernel, [], [own, other, first, *arrays],
        [(wide, BF), (wide, BF), ((rows, depth), F32), ((rows, depth), BF)],
        [pltpu.VMEM((2 * rows, depth), BF), pltpu.VMEM((2 * rows, depth), F32)],
        "ffn_up_down", 8 * rows * depth * hidden * count, (hidden // step,),
        [row, row, line] + specs, [tall, tall, row, row],
    )


def ffn_down_up(own, other, views, slope):
    rows, depth = own.shape
    hidden = slope.shape[2]
    count = len(views)
    step, row, tall, line, specs, arrays = ffn_blocks(views, rows, depth, hidden)

    def kernel(own_ref, other_ref, slope_ref, *rest):
        weights, (du_ref, sum_ref, keep_ref, send_ref, pair, acc) = rest[:-6], rest[-6:]
        j = pl.program_id(0)

        @pl.when(j == 0)
        def _():
            pair[:rows, :] = own_ref[...]
            pair[rows:, :] = other_ref[...]

        total = None
        for v in range(count):
            du = (dot(pair[...], weights[2 * v + 1][0], (1, 0)) * slope_ref[v].astype(F32)).astype(BF)
            du_ref[v] = du
            sum_ref[v] = jnp.sum(du.astype(F32), 0, keepdims=True)
            term = dot(du, weights[2 * v][0], (1, 1))
            total = term if total is None else total + term

        @pl.when(j == 0)
        def _():
            acc[...] = total

        @pl.when(j > 0)
        def _():
            acc[...] += total

        @pl.when(j == hidden // step - 1)
        def _():
            keep_ref[...] = acc[:rows, :]
            send_ref[...] = acc[rows:, :].astype(BF)

    return run(
        kernel, [], [own, other, slope, *arrays],
        [
            ((count, 2 * rows, hidden), BF), ((count, 1, hidden), F32),
            ((rows, depth), F32), ((rows, depth), BF),
        ],
        [pltpu.VMEM((2 * rows, depth), BF), pltpu.VMEM((2 * rows, depth), F32)],
        "ffn_down_up", 8 * rows * depth * hidden * count, (hidden // step,),
        [row, row, tall] + specs, [tall, line, row, row],
    )


def split_blocks(full, keep_ref, send_ref, at, core, blocks, size):
    for p in range(blocks // 2):
        mine = multiple((2 * p + core) * size, size)
        theirs = multiple((2 * p + 1 - core) * size, size)
        keep_ref[at + (p,)] = full[pl.ds(mine, size), :]
        send_ref[at + (p,)] = full[pl.ds(theirs, size), :]


def ffn_weight_grads(x_own, x_other, e_own, e_other, du, act, core, blocks):
    rows, depth = x_own.shape
    count, _, hidden = du.shape
    step = min(512, hidden)
    per = hidden // step
    size = depth // blocks
    split = core is not None

    def kernel(core_ref, x_ref, xo_ref, e_ref, eo_ref, du_ref, act_ref, *rest):
        outs, (xs, es, full) = rest[:-3], rest[-3:]

        @pl.when(pl.program_id(0) == 0)
        def _():
            xs[:rows, :] = x_ref[...]
            xs[rows:, :] = xo_ref[...]
            es[:rows, :] = e_ref[...]
            es[rows:, :] = eo_ref[...]

        up = dot(xs[...], du_ref[0], (0, 0)).astype(BF)
        down = dot(es[...], act_ref[0], (0, 0)).astype(BF)
        if split:
            full[...] = up
            split_blocks(full, outs[0], outs[1], (), core_ref[0], blocks, size)
            full[...] = down
            split_blocks(full, outs[2], outs[3], (), core_ref[0], blocks, size)
        else:
            outs[0][0] = up
            outs[0][1] = down

    row = pl.BlockSpec((rows, depth), lambda j: (0, 0))
    tall = pl.BlockSpec((1, 2 * rows, step), lambda j: (j // per, 0, j % per))
    if split:
        part = pl.BlockSpec((blocks // 2, size, step), lambda j: (0, 0, j))
        outs, out_blocks = [((blocks // 2, size, hidden * count), BF)] * 4, [part] * 4
    else:
        outs = [((2 * count, depth, hidden), BF)]
        out_blocks = [pl.BlockSpec((2, depth, step), lambda j: (j // per, 0, j % per))]
    return run(
        kernel, [core if split else jnp.zeros((1,), jnp.int32)],
        [x_own, x_other, e_own, e_other, du, act], outs,
        [
            pltpu.VMEM((2 * rows, depth), BF),
            pltpu.VMEM((2 * rows, depth), BF),
            pltpu.VMEM((depth, step), BF),
        ],
        "ffn_weight_grads", 8 * rows * depth * hidden * count, (count * per,),
        [row, row, row, row, tall, tall], out_blocks,
    )


def weight_grads(groups, core, blocks):
    arrays, places = [], []
    for group in groups:
        for pair in group:
            spot = []
            for array in pair:
                known = [i for i, a in enumerate(arrays) if a is array]
                if not known:
                    arrays.append(array)
                    known = [len(arrays) - 1]
                spot.append(known[0])
            places.append(spot)
    depth, width = groups[0][0][0].shape[1], groups[0][0][1].shape[1]
    size = depth // blocks
    count = len(arrays)

    def kernel(core_ref, *rest):
        outs, full = rest[count:-1], rest[-1]
        number = 0
        for g, group in enumerate(groups):
            for j in range(len(group)):
                left, right = places[number]
                value = dot(rest[left][...], rest[right][...], (0, 0)).astype(BF)
                if core is None:
                    outs[g][j] = value
                else:
                    full[...] = value
                    split_blocks(
                        full, outs[2 * g], outs[2 * g + 1], (j,), core_ref[0], blocks, size
                    )
                number += 1

    outs = []
    for group in groups:
        if core is None:
            outs.append(((len(group), depth, width), BF))
        else:
            outs += [((len(group), blocks // 2, size, width), BF)] * 2
    flops = sum(2 * left.shape[0] * depth * width for group in groups for left, right in group)
    return run(
        kernel, [jnp.zeros((1,), jnp.int32) if core is None else core], arrays, outs,
        [pltpu.VMEM((depth, width), BF)], "weight_grads", flops,
    )


def norm_grad_body(terms, summed, gain, grad_ref, low_ref, sums_ref):
    grad = terms[0][...].astype(F32)
    for ref in terms[1:]:
        grad = grad + ref[...].astype(F32)
    total = summed[...]
    center = total - jnp.mean(total, -1, keepdims=True)
    scale = lax.rsqrt(jnp.mean(center * center, -1, keepdims=True) + 1e-05)
    unit = center * scale
    inner = grad * gain
    out = scale * (
        inner - jnp.mean(inner, -1, keepdims=True) - unit * jnp.mean(inner * unit, -1, keepdims=True)
    )
    low = out.astype(BF)
    grad_ref[...] = out
    low_ref[...] = low
    sums_ref[0:1, :] = jnp.sum(low.astype(F32), 0, keepdims=True)
    sums_ref[1:2, :] = jnp.sum(grad * unit, 0, keepdims=True)
    sums_ref[2:3, :] = jnp.sum(grad, 0, keepdims=True)
    return low


def norm_grad(terms, summed, gain, line):
    shape = summed.shape

    def kernel(sum_ref, gain_ref, *rest):
        norm_grad_body(rest[: len(terms)], sum_ref, gain_ref[line : line + 1, :], *rest[len(terms) :])

    return run(
        kernel, [], [summed, gain, *terms], [(shape, F32), (shape, BF), ((3, shape[1]), F32)], [],
        "norm_grad", 1e6,
    )


def norm_out_grad(terms, summed, gain, line, weight):
    shape = summed.shape
    count, depth, width = weight.shape

    def kernel(sum_ref, gain_ref, w_ref, *rest):
        outs = rest[len(terms) :]
        low = norm_grad_body(rest[: len(terms)], sum_ref, gain_ref[line : line + 1, :], *outs[:3])
        for mask in range(count):
            outs[3 + mask][...] = dot(low, w_ref[mask], (1, 0)).astype(BF)

    return run(
        kernel, [], [summed, gain, weight, *terms],
        [(shape, F32), (shape, BF), ((3, shape[1]), F32)] + [((shape[0], width), BF)] * count, [],
        "norm_out_grad", 2 * shape[0] * depth * width * count,
    )


def input_grads(dq, own, below, above, weights, t_index, count):
    tokens, width = dq.shape
    rows, depth = tokens // count, weights.shape[1]
    ahead = weights.shape[0] - 2

    def kernel(t_ref, w_ref, dq_ref, own_ref, below_ref, above_ref, dk_ref, dv_ref, sums_ref, *rest):
        full = rest[count]
        for j, ref in enumerate((dk_ref, dv_ref)):
            ref[...] = (
                own_ref[j] + below_ref[j].astype(F32) + above_ref[j].astype(F32)
            ).astype(BF)
        sums_ref[0:1, :] = jnp.sum(dq_ref[...].astype(F32), 0, keepdims=True)
        sums_ref[1:2, :] = jnp.sum(dv_ref[...].astype(F32), 0, keepdims=True)
        total = dot(dk_ref[...], w_ref[ahead], (1, 1)) + dot(dv_ref[...], w_ref[ahead + 1], (1, 1))
        if ahead:
            total = total + dot(dq_ref[...], w_ref[0], (1, 1))
        full[...] = total
        for mask in range(count):
            part = full[pl.ds(multiple((t_ref[0] ^ mask) * rows, rows), rows), :]
            rest[mask][...] = part.astype(rest[mask].dtype)

    return run(
        kernel, [t_index], [weights, dq, own, below, above],
        [((tokens, width), BF)] * 2 + [((2, width), F32), ((rows, depth), F32)]
        + [((rows, depth), BF)] * (count - 1),
        [pltpu.VMEM((tokens, depth), F32)], "input_grads",
        2 * tokens * width * depth * weights.shape[0],
    )


def asked_grad(pieces, weight):
    count, depth, width = weight.shape
    rows = pieces[0].shape[0]

    def kernel(w_ref, *rest):
        total = dot(rest[0][...], w_ref[0], (1, 1))
        for mask in range(1, count):
            total = total + dot(rest[mask][...], w_ref[mask], (1, 1))
        rest[count][...] = total

    return run(
        kernel, [], [weight, *pieces], [((rows, depth), F32)], [], "asked_grad",
        2 * rows * depth * width * count,
    )[0]


def by_mask(values, t_index, count):
    tokens, width = values.shape
    rows = tokens // count

    def kernel(t_ref, x_ref, *outs):
        for mask in range(count):
            outs[mask][...] = x_ref[pl.ds(multiple((t_ref[0] ^ mask) * rows, rows), rows), :]

    return run(kernel, [t_index], [values], [((rows, width), BF)] * count, [], "by_mask", 1000)


def in_order(pieces, t_index):
    count = len(pieces)
    rows, width = pieces[0].shape

    def kernel(t_ref, *refs):
        place_rows(refs[count], refs[:count], t_ref[0])

    return run(
        kernel, [t_index], pieces, [((rows * count, width), BF)], [], "in_order", 1000
    )[0]


LINES = 32
ENC_ATT, ENC_FFN, SELF_ATT, CROSS_ATT, DEC_FFN, ENC_FIRST, DEC_FIRST = 0, 5, 8, 13, 18, 21, 25


def pack_small(arrays, width):
    def kernel(*refs):
        lines = []
        for ref in refs[:-1]:
            value = ref[...].astype(F32)
            if value.shape[1] > width:
                value = jnp.concatenate(
                    [value[:, i : i + width] for i in range(0, value.shape[1], width)], 0
                )
            lines.append(value)
        used = sum(value.shape[0] for value in lines)
        lines.append(jnp.zeros((LINES - used, width), F32))
        whole = jnp.concatenate(lines, 0)
        refs[-1][...] = jnp.concatenate([whole[: LINES // 2], whole[LINES // 2 :]], 1).astype(BF)

    blocks = [pl.BlockSpec(array.shape, lambda i: (0, 0)) for array in arrays]
    shape = (LINES // 2, 2 * width)
    return run(
        kernel, [], arrays, [(shape, BF)], [], "pack_small", 0, (1,), blocks,
        [pl.BlockSpec(shape, lambda i: (0, 0))],
    )[0]


def unpack_small(parts, t_index, count, features, wide_masks):
    peers, lines, width = parts.shape[0], LINES, parts.shape[2] // 2
    share_ = peers // count
    quarter = 4
    hidden = share_ * quarter * width

    def kernel(t_ref, x_ref, table, local, enc_ref, dec_ref):
        for f in range(peers):
            value = x_ref[f].astype(F32)
            span = slice(f * width, (f + 1) * width)
            table[: lines // 2, span] = value[:, :width]
            table[lines // 2 :, span] = value[:, width:]
        for mask in range(count):
            local[mask] = table[:, pl.ds(multiple((t_ref[0] ^ mask) * features, 128), features)]
        for ref, first in ((enc_ref, ENC_FIRST), (dec_ref, DEC_FIRST)):
            for v, mask in enumerate(wide_masks):
                for f in range(share_):
                    for q in range(quarter):
                        at = (f * quarter + q) * width
                        ref[v, :, at : at + width] = local[
                            mask, first + q : first + q + 1, f * width : (f + 1) * width
                        ]

    first = ((len(wide_masks), 1, hidden), F32)
    return run(
        kernel, [t_index], [parts],
        [((lines, peers * width), F32), ((count, lines, features), F32), first, first], [],
        "unpack_small", 0,
    )


def pack_grads(sums, columns, firsts, t_index, peers, wide_masks):
    depth = sums[0].shape[1]
    width = depth // peers
    features = columns[0].shape[1]
    share_ = features // width
    quarter = 4
    arrays = list(sums) + list(columns) + list(firsts)

    def kernel(t_ref, *refs):
        out, table = refs[-2:]
        table[...] = jnp.zeros_like(table)
        own = pl.ds(multiple(t_ref[0] * features, 128), features)
        att = (ENC_ATT, SELF_ATT, CROSS_ATT)
        for first, s_ref, c_ref in zip(att, refs[:3], refs[5:8]):
            table[first + 2 : first + 5, :] = s_ref[...]
            table[first : first + 2, own] = c_ref[...]
        for first, s_ref in zip((ENC_FFN, DEC_FFN), refs[3:5]):
            table[first : first + 3, :] = s_ref[...]
        for first, f_ref in zip((ENC_FIRST, DEC_FIRST), refs[8:10]):
            for v, mask in enumerate(wide_masks):
                strip = []
                for q in range(quarter):
                    pieces = []
                    for f in range(share_):
                        at = (f * quarter + q) * width
                        pieces.append(f_ref[v, :, at : at + width])
                    strip.append(jnp.concatenate(pieces, 1))
                there = pl.ds(multiple((t_ref[0] ^ mask) * features, 128), features)
                table[first : first + quarter, there] = jnp.concatenate(strip, 0)
        for f in range(peers):
            out[f] = table[:, f * width : (f + 1) * width]

    return run(
        kernel, [t_index], arrays, [((peers, LINES, width), F32)],
        [pltpu.VMEM((LINES, depth), F32)], "pack_grads", 0,
    )[0]


def unpack_grads(terms, shapes):
    def kernel(*refs):
        value = refs[0][...]
        for ref in refs[1 : len(terms)]:
            value = value + ref[...]
        width = value.shape[1]
        line = 0
        for ref in refs[len(terms) :]:
            rows, columns = ref.shape
            for r in range(rows):
                for at in range(0, columns, width):
                    ref[r : r + 1, at : at + width] = value[line : line + 1, :]
                    line += 1

    return run(kernel, [], terms, [(shape, F32) for shape in shapes], [], "unpack_grads", 0)


def token_spans(seq_lens, pic_start, pic_len, base, tokens, block):
    count, pictures = pic_start.shape
    blocks = tokens // block

    def kernel(lens, starts, extents, base_ref, both, text, both_bounds, text_bounds):
        places = lax.broadcasted_iota(jnp.int32, (1, tokens), 1) + tokens
        zero = jnp.zeros((1, tokens), jnp.int32)
        begin, end = zero, zero
        low, high = [zero] * pictures, [zero] * pictures
        edges = [
            [jnp.int32(3 * tokens), jnp.int32(0), jnp.int32(tokens + (i + 1) * block)]
            for i in range(blocks)
        ]
        start = tokens - base_ref[0]
        for s in range(count):
            stop = start + lens[s]
            inside = (places >= start) & (places < stop)
            begin = jnp.where(inside, start, begin)
            end = jnp.where(inside, stop, end)
            spans = []
            for k in range(pictures):
                first = start + starts[s, k]
                last = jnp.minimum(first + extents[s, k], stop)
                member = inside & (places >= first) & (places < last)
                low[k] = jnp.where(member, first, low[k])
                high[k] = jnp.where(member, last, high[k])
                spans.append((first, last))
            for i in range(blocks):
                from_, to = tokens + i * block, tokens + (i + 1) * block
                meets = (start < to) & (stop > from_)
                edge = edges[i]
                edge[0] = jnp.where(meets, jnp.minimum(edge[0], start), edge[0])
                edge[1] = jnp.where(meets, jnp.maximum(edge[1], stop), edge[1])
                for first, last in spans:
                    touches = (first < to) & (last > from_)
                    edge[2] = jnp.where(touches, jnp.maximum(edge[2], last), edge[2])
            start = stop
        both[...] = jnp.concatenate([begin, end] + [zero] * 6, 0)
        seen = [begin, places + 1]
        for k in range(pictures):
            seen += [low[k], high[k]]
        text[...] = jnp.concatenate(seen + [zero] * (8 - len(seen)), 0)
        for i in range(blocks):
            first = lax.div(edges[i][0], jnp.int32(block))
            both_bounds[2 * i] = first
            both_bounds[2 * i + 1] = lax.div(edges[i][1] + (block - 1), jnp.int32(block))
            text_bounds[2 * i] = first
            text_bounds[2 * i + 1] = lax.div(edges[i][2] + (block - 1), jnp.int32(block))

    whole = pl.BlockSpec(memory_space=pltpu.VMEM)
    scalars = pl.BlockSpec(memory_space=pltpu.SMEM)
    return run(
        kernel, [seq_lens, pic_start, pic_len, base], [],
        [((8, tokens), jnp.int32)] * 2 + [((2 * blocks,), jnp.int32)] * 2, [], "token_spans", 0,
        None, None, [whole, whole, scalars, scalars],
    )


def per_device(
    enc_in,
    dec_in,
    enc_cot,
    dec_cot,
    seq_lens,
    pic_start,
    pic_len,
    enc_attn_w,
    enc_attn_bias,
    enc_attn_norm,
    enc_ffn_w,
    enc_ffn_b1,
    enc_ffn_vec,
    self_attn_w,
    self_attn_bias,
    self_attn_norm,
    cross_attn_w,
    cross_attn_bias,
    cross_attn_norm,
    dec_ffn_w,
    dec_ffn_b1,
    dec_ffn_vec,
):
    rows = enc_in.shape[0]
    tensor_size = lax.axis_size("tensor")
    fsdp_size = lax.axis_size("fsdp")
    t_index = lax.axis_index("tensor")
    f_index = lax.axis_index("fsdp")
    t_ref = t_index[None].astype(jnp.int32)
    core = (f_index % 2)[None].astype(jnp.int32)
    tokens = rows * tensor_size
    features = enc_attn_w.shape[2]
    hidden = enc_ffn_w.shape[2]
    t_down = bits_of("tensor")[::-1]
    t_up = bits_of("tensor")
    wide_down = t_down[:-1]
    wide_up = t_up[1:]
    t_masks = range(tensor_size)
    wide_masks = range(0, tensor_size, 2)
    wide_count = len(wide_masks)

    small = [
        enc_attn_bias, enc_attn_norm, enc_ffn_vec, self_attn_bias, self_attn_norm,
        cross_attn_bias, cross_attn_norm, dec_ffn_vec, enc_ffn_b1, dec_ffn_b1,
    ]
    block = min(256, tokens)
    base = (f_index * tokens)[None].astype(jnp.int32)
    spans = token_spans(seq_lens, pic_start, pic_len, base, tokens, block)
    both = (spans[0], spans[2], 1)
    text = (spans[1], spans[3], 1 + pic_start.shape[1])

    first_order, second_order = plane_orders()

    def later(value, ready):
        return lax.optimization_barrier((value, ready))[0]

    class Pair:
        def __init__(self, halves, splits):
            self.plans = [
                Gather(half[None], order, split)
                for half, order, split in zip(halves, (first_order, second_order), splits)
            ]

        def hop(self, *gate):
            if self.plans[0].came is not None:
                came_ = join([plan.came for plan in self.plans], *gate)
                for plan, value in zip(self.plans, came_):
                    plan.came = value
                gate = ()
            return [plan.hop(*gate) for plan in self.plans]

        def result(self):
            return [plan.result() for plan in self.plans]

    slices = hidden // features

    def ffn_slices(shard):
        cut = shard.reshape(2, rows, slices, features)
        return jnp.moveaxis(cut, 2, 1).reshape(2 * slices, rows, features)

    def ups(shards):
        return [ffn_slices(shard)[:slices] for shard in shards]

    def downs(shards):
        return [ffn_slices(shard)[slices:] for shard in shards]

    def ffn_views(*arrays):
        views = []
        for up, down in arrays:
            for at in range(0, up.shape[0], slices):
                views.append((up, at, down, at))
        return views

    far = (wide_count - 1) * slices

    def exchange(pieces_, *hold):
        held = dict(enumerate(pieces_))
        for bit in t_up:
            moved = [mask for mask in t_masks if mask & bit]
            came_ = swap(jnp.stack([held[mask] for mask in moved]), "tensor", bit)
            if bit == 1:
                came_ = join(came_, *hold)
            for at, mask in enumerate(moved):
                held[mask] = came_[at]
        return [held[mask] for mask in t_masks]

    def doubled(value):
        held = {0: value}
        for bit in t_down:
            known = sorted(held)
            came_ = swap(jnp.stack([held[mask] for mask in known]), "tensor", bit)
            gate = yield came_
            came_ = join(came_, *(gate or ()))
            for at, mask in enumerate(known):
                held[mask | bit] = came_[at]
        yield [held[mask] for mask in t_masks]

    peers = fsdp_size
    up_pairs = [(i, i + 1) for i in range(peers - 1)]
    down_pairs = [(j, i) for i, j in up_pairs]

    def halo(pair):
        before = lax.ppermute(pair, "fsdp", up_pairs)
        after = lax.ppermute(pair, "fsdp", down_pairs)
        return before, pair, after

    def attend_fg(queries, window, mode):
        return attend(queries, window, mode[0], mode[1], t_ref, tensor_size, mode[2])

    def attend_back_fg(queries, window, grads, mixed_t, totals, mode):
        return attend_back(
            queries, window, grads, mixed_t, totals, mode[0], mode[1], t_ref, tensor_size, mode[2]
        )

    class Folds:
        def __init__(self, parts_, at):
            self.folds = [
                Fold(parts_[2 * k], parts_[2 * k + 1], order[:-1], at)
                for k, order in enumerate((first_order, second_order))
            ]

        def hop(self, *gate):
            return [fold.hop(*gate) for fold in self.folds]

        def next(self, *gate):
            came_ = join([fold.came for fold in self.folds], *gate)
            for fold, value in zip(self.folds, came_):
                fold.came = value
            return [fold.next() for fold in self.folds]

        def result(self, *gate):
            return [fold.result(*gate) for fold in self.folds]

    class SmallSum:
        def __init__(self, value):
            self.value, self.came = value, None
            self.bits = [("fsdp", bit) for bit in bits_of("fsdp")[::-1]]
            self.bits += [("tensor", bit) for bit in t_up]

        def hop(self):
            if self.came is not None:
                self.value = self.value + self.came
            axis, bit = self.bits.pop(0)
            sent = self.value
            if axis == "fsdp":
                half = self.value.shape[0] // 2
                mine = (f_index // bit) % 2
                sent = lax.dynamic_slice_in_dim(self.value, (1 - mine) * half, half, 0)
                self.value = lax.dynamic_slice_in_dim(self.value, mine * half, half, 0)
            self.came = swap(sent, axis, bit)

        def result(self):
            while self.bits:
                self.hop()
            return [self.value[0], self.came[0]]

    class WideShare:
        def __init__(self, halves):
            self.held = {
                mask: halves[:, :, j * hidden : (j + 1) * hidden]
                for j, mask in enumerate(wide_masks)
            }
            self.bits = list(wide_up)

        def hop(self):
            bit = self.bits.pop(0)
            new = []
            for mask in sorted(self.held):
                if mask not in self.held or mask & (2 * bit - 1):
                    continue
                came_ = swap(self.held.pop(mask | bit).astype(BF), "tensor", bit)
                self.held[mask] = self.held[mask] + came_.astype(F32)
                new.append(came_)
            self.came = new
            return new

        def result(self):
            while self.bits:
                self.hop()
            return self.held[0]

    pending = [[], [], [], []]

    def due(*values, lag=2):
        pending[lag - 1].extend(values)

    def fg(value):
        waits = pending.pop(0)
        pending.append([])
        return join(value, *waits)

    packed = pack_small(small, enc_attn_bias.shape[1])
    depth = enc_in.shape[1]
    enc_pieces = reach(
        jnp.concatenate([enc_in, enc_attn_w[3]], 1), "tensor", t_masks[:0:-1]
    )
    first_shard = jnp.concatenate([enc_attn_w[:3].reshape(-1, features), packed])
    qkv_plan = Gather(first_shard[None], first_order, [(3, rows), (1, packed.shape[0])])
    qkv_plan.hop()
    enc_qkv, parts = qkv_plan.result()
    table, local, enc_first, dec_first = unpack_small(
        parts.reshape(fsdp_size, -1, features), t_ref, tensor_size, features, wide_masks
    )
    plan1 = Pair(
        (
            jnp.concatenate([self_attn_w[:3]] + ups([enc_ffn_w])),
            jnp.concatenate(
                [piece[None, :, depth:] for piece in enc_pieces] + downs([enc_ffn_w])
            ),
        ),
        ([3, slices], [tensor_size, slices]),
    )
    due(plan1.hop())
    dec_steps = doubled(
        join(
            jnp.concatenate([dec_in, self_attn_w[3], cross_attn_w[3], cross_attn_w[0]], 1),
            *enc_pieces[1:],
        )
    )
    due(next(dec_steps))

    flat_e, pair_e, query_e = project(
        fg(enc_pieces), enc_qkv, local, (ENC_ATT, None, ENC_ATT + 1), t_ref
    )
    window_e = halo(pair_e)
    r1 = (window_e[0], window_e[2])
    plan1.hop(*r1)
    dec_pieces = dec_steps.send(r1)

    mixed_e, mixed_t_e, totals_e = attend_fg(fg(query_e), window_e, both)
    mixed_e = exchange(mixed_e, dec_pieces)
    r2 = tuple(mixed_e[1:])
    plan1.hop(*r2)
    (self_qkv, own_up), (enc_out_w, own_down) = plan1.result()
    enc_wide = Spread(join(enc_ffn_w, *r2), "tensor", wide_down)
    enc_wide.hop()
    for step in range(len(t_down) - 1):
        dec_pieces = dec_steps.send(r2)

    summed_e, hid, hid_low = out_norm(
        fg(mixed_e), enc_out_w, enc_in, table, ENC_ATT + 2
    )
    hid_other = swap(hid_low, "tensor", 1)
    r3 = (hid_other,)
    flat_s, pair_s, query_s = project(
        fg(join(dec_pieces, hid_low)), self_qkv, local, (SELF_ATT, None, SELF_ATT + 1), t_ref
    )
    spare = [join(piece, *r3)[:, depth:] for piece in dec_pieces]

    def spare_part(which):
        return [piece[None, :, which * features : (which + 1) * features] for piece in spare]

    others = enc_wide.result(*r3)[1:]
    plan2 = Pair(
        (
            jnp.concatenate(ups(others) + spare_part(0) + [cross_attn_w[1:3]]),
            jnp.concatenate(downs(others) + spare_part(1) + spare_part(2)),
        ),
        ([far, tensor_size, 2], [far, tensor_size, tensor_size]),
    )
    plan2.hop()
    window_s = halo(pair_s)
    r4 = (window_s[0], window_s[2])
    mixed_s, mixed_t_s, totals_s = attend_fg(fg(query_s), window_s, text)
    mixed_s = exchange(mixed_s)
    r5 = tuple(mixed_s[1:])
    plan2.hop(*r5)
    dec_wide = Spread(join(dec_ffn_w, *r5), "tensor", wide_down)
    dec_wide.hop()
    plan2.hop(*r5)
    (far_up, self_out_w, cross_kv), (far_down, cross_out_w, cross_query) = plan2.result()
    enc_views = ffn_views((own_up, own_down), (far_up, far_down))
    active_e, slope_e, keep, send = ffn_up_down(hid_low, hid_other, enc_views, enc_first)
    came = swap(send, "tensor", 1)
    r7 = (came,)
    shards = dec_wide.result(send)
    plan4 = Pair(
        (jnp.concatenate(ups(shards)), jnp.concatenate(downs(shards))),
        ([slices + far], [slices + far]),
    )
    plan4.hop()

    summed_s, decoded, decoded_low = out_norm(
        join(mixed_s, send), self_out_w, dec_in, table, SELF_ATT + 2
    )
    ffn_summed_e, encoded = add_norm(
        [hid, join(keep, decoded_low), came], table, ENC_FFN
    )
    enc_rows = spread(encoded, "tensor", t_down)
    plan4.hop(encoded)
    asked = exchange(
        project_rows(join(decoded_low, *enc_rows[1:]), cross_query, local, CROSS_ATT)
    )
    query_c = in_order(asked, t_ref)

    flat_c, pair_c = project(
        enc_rows, cross_kv, local, (None, CROSS_ATT + 1), t_ref
    )
    window_c = halo(pair_c)
    r9 = (window_c[0], window_c[2])
    plan4.hop(*r9)
    mixed_c, mixed_t_c, totals_c = attend_fg(query_c, window_c, both)
    mixed_c = exchange(mixed_c)
    dec_views = ffn_views([array for (array,) in plan4.result()])
    summed_c, crossed, crossed_low = out_norm(
        mixed_c, cross_out_w, decoded, table, CROSS_ATT + 2
    )
    crossed_other = swap(crossed_low, "tensor", 1)
    active_d, slope_d, keep, send = ffn_up_down(
        crossed_low, crossed_other, dec_views, dec_first
    )
    came = swap(send, "tensor", 1)
    ffn_summed_d, final = add_norm([crossed, keep, came], table, DEC_FFN)

    grad_sum_d, low_d, dec_sums = norm_grad([dec_cot], ffn_summed_d, table, DEC_FFN + 1)
    other_d = swap(low_d, "tensor", 1)
    du_d, dec_first_sum, keep, send = ffn_down_up(low_d, other_d, dec_views, slope_d)
    came = swap(send, "tensor", 1)
    dec_grads = ffn_weight_grads(
        crossed_low, crossed_other, low_d, other_d, join(du_d, send), active_d, core, fsdp_size
    )
    dec_fold = Folds(dec_grads, 0)
    due(dec_fold.hop())

    grad_sum_c, low_c, sums_c, *given = norm_out_grad(
        [fg(grad_sum_d), join(keep, dec_grads), came], summed_c, table, CROSS_ATT + 3, cross_out_w
    )
    given = exchange(given)
    b2 = tuple(given[1:])
    due(dec_fold.next(*b2))
    dq_c, below, own, above = attend_back_fg(
        query_c, window_c, fg(given), mixed_t_c, totals_c, both
    )
    below = lax.ppermute(below, "fsdp", down_pairs)
    above = lax.ppermute(above, "fsdp", up_pairs)
    asked_c = exchange(by_mask(dq_c, t_ref, tensor_size))
    b3 = (below, above)
    due(dec_fold.next(*b3))
    dk_c, dv_c, columns_c, *blocks_c = input_grads(
        dq_c, fg(own), below, above, cross_kv, t_ref, tensor_size
    )
    source = Share(blocks_c, "tensor", t_up)
    due(source.hop())
    from_asked = asked_grad([join(asked_c[0], dk_c)] + asked_c[1:], cross_query)
    cross_grads = weight_grads(
        [
            [(flat_c, join(dk_c, from_asked)), (flat_c, dv_c)]
            + [(decoded_low, piece) for piece in asked_c],
            [(low_c, piece) for piece in mixed_c],
        ],
        core, fsdp_size,
    )
    cross_fold = Folds(cross_grads, 1)
    due(cross_fold.hop())

    grad_sum_s, low_s, sums_s, *given = norm_out_grad(
        [fg(join(grad_sum_c, cross_grads)), from_asked], summed_s, table, SELF_ATT + 3, self_out_w
    )
    given = exchange(given)
    b6 = tuple(given[1:])
    source.hop(*b6)
    due(cross_fold.next(*b6), lag=3)
    dq_s, below, own, above = attend_back_fg(
        query_s, window_s, fg(given), mixed_t_s, totals_s, text
    )
    below = lax.ppermute(below, "fsdp", down_pairs)
    above = lax.ppermute(above, "fsdp", up_pairs)
    b7 = (below, above)
    due(cross_fold.next(*b7))
    dec_wide_share = WideShare(jnp.stack(dec_fold.result(*b7)))
    due(dec_wide_share.hop())
    grad_sum_f, low_f, enc_sums = norm_grad(
        [fg(join(enc_cot, dq_s))] + source.result(), ffn_summed_e, table, ENC_FFN + 1
    )
    other_f = swap(low_f, "tensor", 1)
    dk_s, dv_s, columns_s, *blocks_s = input_grads(
        dq_s, join(own, low_f), below, above, self_qkv, t_ref, tensor_size
    )
    b8 = dk_s
    target = Share(blocks_s, "tensor", t_up)
    due(target.hop())
    self_parts = weight_grads(
        [
            [(flat_s, join(dq_s, b8)), (flat_s, dk_s), (flat_s, dv_s)]
            + [(low_s, piece) for piece in mixed_s]
        ],
        core, fsdp_size,
    )
    self_fold = Fold(self_parts[0], self_parts[1], first_order[:-1], 1)
    due(self_fold.hop())
    du_e, enc_first_sum, keep, send = ffn_down_up(
        fg(join(low_f, self_parts)), other_f, enc_views, slope_e
    )
    came = swap(send, "tensor", 1)
    b10 = came
    due(target.hop(b10), lag=3)
    due(self_fold.next(b10), lag=3)
    enc_grads = ffn_weight_grads(
        hid_low, hid_other, low_f, other_f, join(du_e, send), active_e, core, fsdp_size
    )
    enc_fold = Folds(enc_grads, 0)
    due(enc_fold.hop())

    grad_sum_e, low_e, sums_e, *given = norm_out_grad(
        [grad_sum_f, fg(join(keep, enc_grads)), came], summed_e, table, ENC_ATT + 3, enc_out_w
    )
    given = exchange(given)
    b11 = tuple(given[1:])
    due(enc_fold.next(*b11))
    due(self_fold.next(*b11))
    dq_e, below, own, above = attend_back_fg(
        query_e, window_e, fg(given), mixed_t_e, totals_e, both
    )
    below = lax.ppermute(below, "fsdp", down_pairs)
    above = lax.ppermute(above, "fsdp", up_pairs)
    b12 = (below, above)
    enc_fold.next(*b12)
    cross_first, cross_outs = cross_fold.result(*b12)
    self_own = self_fold.result(*b12)
    late_share = Share(
        [
            jnp.stack([cross_first[2 + mask], cross_outs[mask], self_own[3 + mask]])
            for mask in t_masks
        ],
        "tensor", t_up,
    )
    dk_e, dv_e, columns_e, *blocks_e = input_grads(
        dq_e, fg(own), below, above, enc_qkv, t_ref, tensor_size
    )
    b13 = dk_e
    enc_share = Share(blocks_e, "tensor", t_up)
    enc_share.hop()
    small_sum = SmallSum(
        pack_grads(
            [sums_e, sums_s, sums_c, enc_sums, dec_sums], [columns_e, columns_s, columns_c],
            [enc_first_sum, dec_first_sum], t_ref, fsdp_size, wide_masks,
        )
    )
    small_sum.hop()
    enc_att = weight_grads(
        [
            [(flat_e, dq_e), (flat_e, join(dk_e, tuple(blocks_e))), (flat_e, dv_e)],
            [(low_e, piece) for piece in mixed_e],
        ],
        core, fsdp_size,
    )
    att_folds = Folds(enc_att, 1)
    att_folds.hop()

    def meet(*items):
        for item, came_ in zip(items, join([item.came for item in items])):
            item.came = came_

    meet(enc_share, small_sum, *att_folds.folds, *enc_fold.folds)
    att_folds.next()
    enc_share.hop()
    small_sum.hop()
    enc_wide_share = WideShare(jnp.stack(enc_fold.result()))
    enc_wide_share.hop()
    meet(small_sum, *att_folds.folds)
    att_folds.next()
    small_sum.hop()
    late_share.hop()
    meet(late_share, small_sum, *att_folds.folds)
    enc_att_own, enc_att_out = att_folds.result()
    out_share = Share([enc_att_out[mask] for mask in t_masks], "tensor", t_up)
    out_share.hop()
    late_share.hop()
    small_sum.hop()
    meet(out_share, late_share, small_sum)
    out_share.hop()
    small_out = unpack_grads(small_sum.result(), [item.shape for item in small])
    enc_grad = jnp.concatenate([enc_att_own, total(out_share.result())[None]])
    dec_ffn_grad = dec_wide_share.result()
    enc_ffn_grad = enc_wide_share.result()
    late = total(late_share.result())
    cross_grad = jnp.concatenate([late[0:1], cross_first[:2], late[1:2]])
    self_grad = jnp.concatenate([self_own[:3], late[2:3]])
    grad_source = total([grad_sum_e] + enc_share.result())
    grad_target = total([grad_sum_s] + target.result())

    (
        enc_bias_g, enc_norm_g, enc_vec_g, self_bias_g, self_norm_g,
        cross_bias_g, cross_norm_g, dec_vec_g, enc_b1_g, dec_b1_g,
    ) = small_out
    return (
        encoded,
        final,
        grad_source,
        grad_target,
        enc_grad,
        enc_bias_g,
        enc_norm_g,
        enc_ffn_grad,
        enc_b1_g,
        enc_vec_g,
        self_grad,
        self_bias_g,
        self_norm_g,
        cross_grad,
        cross_bias_g,
        cross_norm_g,
        dec_ffn_grad,
        dec_b1_g,
        dec_vec_g,
    )


def solution(mesh):
    rows = P(("fsdp", "tensor"), None)
    weight = P(None, "fsdp", "tensor")
    vector = P(None, "fsdp")
    att, ffn = (weight, vector, vector), (weight, vector, vector)
    in_specs = (rows,) * 4 + (P(),) * 3 + (att + ffn + att + att + ffn)
    out_specs = (rows,) * 4 + (att + ffn + att + att + ffn)
    return jax.shard_map(
        per_device, mesh=mesh, in_specs=in_specs, out_specs=out_specs, check_vma=False
    )
```

```python
import functools
import jax
import jax.numpy as jnp
from jax import lax
from jax.experimental import pallas as pl
from jax.experimental.pallas import tpu as pltpu
from jax.sharding import PartitionSpec as P

HD = 64
BF = jnp.bfloat16
F32 = jnp.float32
PACE = 30000000000


def bits_of(axis):
    count, bit, bits = lax.axis_size(axis), 1, []
    while bit < count:
        bits.append(bit)
        bit *= 2
    return bits


def swap(value, axis, mask):
    return lax.ppermute(value, axis, [(i, i ^ mask) for i in range(lax.axis_size(axis))])


def join(value, *ready):
    return lax.optimization_barrier((value, ready))[0] if ready else value


def spread(value, axis, order, gates=()):
    pieces = {0: value}
    for k, bit in enumerate(order):
        for mask in list(pieces):
            piece = pieces[mask]
            if mask and k < len(gates):
                piece = join(piece, *gates[k])
            pieces[mask | bit] = swap(piece, axis, bit)
    if len(gates) > len(order):
        return [pieces[0]] + [join(pieces[mask], *gates[-1]) for mask in sorted(pieces)[1:]]
    return [pieces[mask] for mask in sorted(pieces)]


def total(items):
    out = items[0].astype(F32)
    for item in items[1:]:
        out = out + item.astype(F32)
    return out


def plane_orders():
    bits = bits_of("fsdp")
    return bits[1:] + bits[:1], bits[1:][::-1] + bits[:1]


def placed(parts, index, splits):
    arrays = [array for array, masks in parts]
    total = sum(len(masks) for array, masks in parts)
    cols = arrays[0].shape[-1]
    shapes = [
        (width, total, arrays[0].shape[2], cols)
        if isinstance(width, int)
        else (width[0], total, width[1], cols)
        for width in splits
    ]
    moves_ = total * sum(1 if isinstance(width, int) else width[0] for width in splits)

    def kernel(index_ref, *refs):
        ins, outs, sems = refs[: len(parts)], refs[len(parts) : -1], refs[-1]
        copies = []
        for (array, masks), ref in zip(parts, ins):
            for at, mask in enumerate(masks):
                first = 0
                for out, width in zip(outs, splits):
                    if isinstance(width, int):
                        moves = [(ref.at[at, first : first + width], out.at[:, index_ref[0] ^ mask])]
                        first += width
                    else:
                        moves = []
                        for line in range(width[0]):
                            moves.append(
                                (ref.at[at, first : first + width[1]], out.at[line, index_ref[0] ^ mask])
                            )
                            first += width[1]
                    for source, target in moves:
                        copy = pltpu.make_async_copy(source, target, sems.at[len(copies)])
                        copy.start()
                        copies.append(copy)
        for copy in copies:
            copy.wait()

    outs = pl.pallas_call(
        kernel,
        out_shape=[jax.ShapeDtypeStruct(shape, arrays[0].dtype) for shape in shapes],
        in_specs=[pl.BlockSpec(memory_space=pltpu.SMEM)]
        + [pl.BlockSpec(memory_space=pl.ANY)] * len(arrays),
        out_specs=[pl.BlockSpec(memory_space=pltpu.VMEM)] * len(splits),
        scratch_shapes=[pltpu.SemaphoreType.DMA((moves_,))],
        compiler_params=pltpu.CompilerParams(vmem_limit_bytes=32 * 2**20),
        cost_estimate=pl.CostEstimate(flops=PACE, bytes_accessed=1, transcendentals=0),
        name="placed",
    )(index[None], *arrays)
    return [out.reshape(out.shape[0], -1, cols) for out in outs]


def gather_plane(shard, order, splits):
    return Gather(shard[None], order, splits).result()


def reach(value, axis, masks):
    pieces = {0: value}
    for mask in masks:
        pieces[mask] = swap(value, axis, mask)
    return [pieces[mask] for mask in sorted(pieces)]


class Gather:
    def __init__(self, held, order, splits):
        self.held, self.masks, self.order, self.splits = held, [0], list(order), splits
        self.came = None

    def take(self, gate):
        if self.came is not None:
            came = join(self.came, *gate)
            self.held = jnp.concatenate([self.held, came], 0)
            self.masks = self.masks + [mask | self.bit for mask in self.masks]

    def hop(self, *gate):
        self.take(gate)
        self.bit = self.order.pop(0)
        self.came = swap(self.held, "fsdp", self.bit)
        return self.came

    def result(self):
        while self.order:
            self.hop()
        parts = [(self.held, self.masks), (self.came, [mask | self.bit for mask in self.masks])]
        return placed(parts, lax.axis_index("fsdp"), self.splits)


class Spread:
    def __init__(self, value, axis, bits):
        self.axis, self.pieces, self.level, self.last = axis, {0: value}, 0, len(bits)
        self.masks = [m for m in range(lax.axis_size(axis)) if m & ~sum(bits) == 0]

    def hop(self, *gate):
        self.level += 1
        new = []
        for mask in self.masks[::-1]:
            if mask.bit_count() == self.level:
                low = mask & -mask
                piece = self.pieces[mask ^ low]
                if mask != low:
                    piece = join(piece, *gate)
                self.pieces[mask] = swap(piece, self.axis, low)
                new.append(self.pieces[mask])
        return new

    def result(self, *gate):
        while self.level < self.last:
            self.hop()
        return [join(self.pieces[m], *(gate if m else ())) for m in self.masks]


class Share:
    def __init__(self, pieces, axis, bits):
        self.axis, self.held, self.bits = axis, dict(enumerate(pieces)), list(bits)
        self.came, self.terms = None, [pieces[0]]

    def hop(self, *gate):
        if self.came is not None:
            came = join(self.came, *gate)
            for at, mask in enumerate(self.kept):
                if mask == 0:
                    self.terms.append(came[at])
                else:
                    self.held[mask] = self.held[mask].astype(F32) + came[at].astype(F32)
            self.came = None
        if self.bits:
            bit = self.bits.pop(0)
            sent = [mask for mask in sorted(self.held) if mask & bit]
            self.kept = [mask ^ bit for mask in sent]
            stack = jnp.stack([self.held.pop(mask).astype(BF) for mask in sent])
            self.came = swap(stack, self.axis, bit)
        return self.came

    def result(self):
        while self.bits or self.came is not None:
            self.hop()
        return self.terms


def halve_all(folds, *gate):
    came = join([fold.came for fold in folds], *gate)
    index = lax.axis_index("fsdp")
    arrays, shapes, bits = [], [], []
    for fold, new in zip(folds, came):
        dim, bit = fold.cut()
        shape = fold.value.shape
        lead = 1
        for extent in shape[:dim]:
            lead *= extent
        rest = 1
        for extent in shape[dim + 1 : -2]:
            rest *= extent
        flat = (lead, 2, rest) + shape[-2:]
        arrays += [fold.value.reshape(flat), new.reshape(flat)]
        shapes.append((shape[:dim] + shape[dim + 1 :], (lead, rest) + shape[-2:]))
        bits.append(bit)
    mine = jnp.stack([(index // bit) % 2 for bit in bits]).astype(jnp.int32)

    def kernel(mine_ref, *refs):
        ins, outs = refs[: len(arrays)], refs[len(arrays) :]
        for n in range(len(folds)):
            value, new = ins[2 * n : 2 * n + 2]
            here = mine_ref[n]
            lead, unused, rest = value.shape[:3]
            for out, which in zip(outs[2 * n : 2 * n + 2], (here, 1 - here)):

                @pl.loop(0, lead)
                def _(i):
                    for j in range(rest):
                        out[i, j] = (
                            value[i, which, j].astype(F32) + new[i, which, j].astype(F32)
                        ).astype(BF)

    outs = []
    for full, flat in shapes:
        outs += [(flat, BF)] * 2
    done = run(kernel, [mine], arrays, outs, [], "halve", 0)
    sent = []
    for n, fold in enumerate(folds):
        fold.value = done[2 * n].reshape(shapes[n][0])
        fold.sent = done[2 * n + 1].reshape(shapes[n][0])
        fold.bit = bits[n]
        sent.append(fold.hop())
    return sent


class Fold:
    def __init__(self, keep, send, order, at):
        bits = bits_of("fsdp")
        self.live, self.order, self.at = bits[1:][::-1], list(order), at
        split = keep.shape[:at] + (2,) * len(self.live) + keep.shape[at + 1 :]
        self.value, self.sent, self.bit = keep.reshape(split), send.reshape(split), bits[0]

    def hop(self, *gate):
        self.came = swap(join(self.sent, *gate), "fsdp", self.bit)
        return self.came

    def cut(self):
        bit = self.order.pop(0)
        dim = self.at + self.live.index(bit)
        self.live.remove(bit)
        return dim, bit

    def next(self, *gate):
        return halve_all([self], *gate)[0]

    def result(self, *gate):
        while self.order:
            self.next(*gate)
            gate = ()
        return self.value.astype(F32) + join(self.came, *gate).astype(F32)


MIB = 2**20
QUICK = ("halve",)
HEAD_SCALE = HD ** (-0.5)


def run(kernel, scalars, arrays, outs, scratch, name, flops, grid=None, in_blocks=None, out_blocks=None):
    arrays = list(arrays)
    whole = pl.BlockSpec(memory_space=pltpu.VMEM)
    in_specs = [pl.BlockSpec(memory_space=pltpu.SMEM)] * len(scalars)
    in_specs += in_blocks if in_blocks else [whole] * len(arrays)
    extra = {"grid": grid} if grid else {}
    return pl.pallas_call(
        kernel,
        out_shape=[jax.ShapeDtypeStruct(shape, kind) for shape, kind in outs],
        in_specs=in_specs,
        out_specs=out_blocks if out_blocks else [whole] * len(outs),
        scratch_shapes=scratch,
        compiler_params=pltpu.CompilerParams(vmem_limit_bytes=40 * MIB),
        cost_estimate=pl.CostEstimate(
            flops=1 if name in QUICK else PACE, bytes_accessed=1, transcendentals=0
        ),
        name=name,
        **extra,
    )(*scalars, *arrays)


def dot(left, right, dims):
    return lax.dot_general(left, right, ((dims[:1], dims[1:]), ((), ())), preferred_element_type=F32)


def head_mask(rows, which, level):
    lane = lax.broadcasted_iota(jnp.int32, (rows, 128), 1)
    return jnp.where(lane // HD == which, level, 0.0).astype(BF)


def tile_allowed(meta, first, size, columns, ranges):
    place = lax.broadcasted_iota(jnp.int32, (size, columns), 0) + first
    allowed = (place >= meta[0:1]) & (place < meta[1:2])
    for k in range(1, ranges):
        allowed = allowed | ((place >= meta[2 * k : 2 * k + 1]) & (place < meta[2 * k + 1 : 2 * k + 2]))
    return allowed


def multiple(value, of):
    return pl.multiple_of(value, of)


def place_rows(ref, pieces, t_index):
    rows = pieces[0].shape[0]
    for mask, piece in enumerate(pieces):
        ref[pl.ds(multiple((t_index ^ mask) * rows, rows), rows), :] = piece[:, : ref.shape[1]]


def attend(queries, windows, meta, bounds, t_index, count, ranges):
    tokens, width = queries.shape
    heads, rows = width // HD, tokens // count
    block = min(256, tokens)
    tiles = 3 * tokens // block

    def kernel(bounds_ref, t_ref, meta_ref, q_ref, b_ref, w_ref, a_ref, *rest):
        o_refs, (ot_ref, lse_ref, keys, v_t, held, acc, nat) = rest[:count], rest[count:]
        for j, ref in enumerate((b_ref, w_ref, a_ref)):
            keys[j * tokens : (j + 1) * tokens, :] = ref[0]
            v_t[:, j * tokens : (j + 1) * tokens] = ref[1].T
        for i in range(tokens // block):
            low, high = bounds_ref[2 * i], bounds_ref[2 * i + 1]
            span = slice(i * block, (i + 1) * block)
            info = meta_ref[:, span]
            asked = []
            for h in range(heads):
                lanes = slice(h // 2 * 128, h // 2 * 128 + 128)
                asked.append(q_ref[span, lanes] * head_mask(block, h % 2, HEAD_SCALE))

            def scores(k, tops):
                first = multiple(k * block, block)
                allowed = tile_allowed(info, first, block, block, ranges)
                out = []
                for h in range(heads):
                    lanes = slice(h // 2 * 128, h // 2 * 128 + 128)
                    s = dot(keys[pl.ds(first, block), lanes], asked[h], (1, 1))
                    s = jnp.where(allowed, s, -1e30)
                    held[h, k] = s
                    out.append(jnp.maximum(tops[h], jnp.max(s, 0, keepdims=True)))
                return tuple(out)

            tops = lax.fori_loop(
                low, high, scores, tuple(jnp.full((1, block), -1e30, F32) for h in range(heads))
            )
            acc[...] = jnp.zeros_like(acc)

            def mixes(k, sums):
                first = multiple(k * block, block)
                out = []
                for h in range(heads):
                    p = jnp.exp(held[h, k] - tops[h])
                    out.append(sums[h] + jnp.sum(p, 0, keepdims=True))
                    some = slice(h * HD, (h + 1) * HD)
                    acc[some, :] += dot(v_t[some, pl.ds(first, block)], p.astype(BF), (1, 0))
                return tuple(out)

            sums = lax.fori_loop(
                low, high, mixes, tuple(jnp.zeros((1, block), F32) for h in range(heads))
            )
            for h in range(heads):
                some = slice(h * HD, (h + 1) * HD)
                acc[some, :] = acc[some, :] / sums[h]
                lse_ref[h : h + 1, span] = tops[h] + jnp.log(sums[h])
            ot_ref[:, span] = acc[...]
            nat[span, :] = acc[...].T.astype(BF)
        for mask in range(count):
            o_refs[mask][...] = nat[pl.ds(multiple((t_ref[0] ^ mask) * rows, rows), rows), :]

    out = run(
        kernel,
        [bounds, t_index],
        [meta, queries, *windows],
        [((rows, width), BF)] * count + [((width, tokens), F32), ((heads, tokens), F32)],
        [
            pltpu.VMEM((3 * tokens, width), BF),
            pltpu.VMEM((width, 3 * tokens), BF),
            pltpu.VMEM((heads, tiles, block, block), F32),
            pltpu.VMEM((width, block), F32),
            pltpu.VMEM((tokens, width), BF),
        ],
        "attend",
        4 * tokens * 3 * tokens * width * 4,
    )
    return out[:count], out[count], out[count + 1]


def attend_back(queries, windows, grads, mixed_t, totals, meta, bounds, t_index, count, ranges):
    tokens, width = queries.shape
    heads, rows = width // HD, tokens // count
    block = min(256, tokens)

    def kernel(bounds_ref, t_ref, meta_ref, q_ref, b_ref, w_ref, a_ref, ot_ref, lse_ref, *rest):
        g_refs = rest[:count]
        dq_ref, db_ref, dw_ref, da_ref, nat, keys, values, k_t, dk, dv, acc = rest[count:]
        place_rows(nat, g_refs, t_ref[0])
        for j, ref in enumerate((b_ref, w_ref, a_ref)):
            part = slice(j * tokens, (j + 1) * tokens)
            keys[part, :] = ref[0]
            values[part, :] = ref[1]
            k_t[:, part] = ref[0].T
        dk[...] = jnp.zeros_like(dk)
        dv[...] = jnp.zeros_like(dv)
        for i in range(tokens // block):
            low, high = bounds_ref[2 * i], bounds_ref[2 * i + 1]
            span = slice(i * block, (i + 1) * block)
            info = meta_ref[:, span]
            g_t = nat[span, :].astype(F32).T
            asked, given, inner = [], [], []
            for h in range(heads):
                lanes = slice(h // 2 * 128, h // 2 * 128 + 128)
                some = slice(h * HD, (h + 1) * HD)
                asked.append(q_ref[span, lanes] * head_mask(block, h % 2, HEAD_SCALE))
                given.append(nat[span, lanes] * head_mask(block, h % 2, 1.0))
                inner.append(jnp.sum(g_t[some] * ot_ref[some, span], 0, keepdims=True))
            acc[...] = jnp.zeros_like(acc)

            def step(k, carry):
                first = multiple(k * block, block)
                at = pl.ds(first, block)
                allowed = tile_allowed(info, first, block, block, ranges)
                for h in range(heads):
                    lanes = slice(h // 2 * 128, h // 2 * 128 + 128)
                    some = slice(h * HD, (h + 1) * HD)
                    s = dot(keys[at, lanes], asked[h], (1, 1))
                    p = jnp.exp(jnp.where(allowed, s, -1e30) - lse_ref[h : h + 1, span])
                    dp = dot(values[at, lanes], given[h], (1, 1))
                    ds = (p * (dp - inner[h])).astype(BF)
                    dv[at, lanes] += dot(p.astype(BF), given[h], (1, 0))
                    dk[at, lanes] += dot(ds, asked[h], (1, 0))
                    acc[some, :] += dot(k_t[some, at], ds, (1, 0))
                return carry

            lax.fori_loop(low, high, step, 0)
            dq_ref[span, :] = (acc[...] * HEAD_SCALE).T.astype(BF)
        for j, ref in enumerate((db_ref, dw_ref, da_ref)):
            part = slice(j * tokens, (j + 1) * tokens)
            ref[0] = dk[part, :].astype(ref.dtype)
            ref[1] = dv[part, :].astype(ref.dtype)

    pair = (2, tokens, width)
    return run(
        kernel,
        [bounds, t_index],
        [meta, queries, *windows, mixed_t, totals, *grads],
        [((tokens, width), BF), (pair, BF), (pair, F32), (pair, BF)],
        [
            pltpu.VMEM((tokens, width), BF),
            pltpu.VMEM((3 * tokens, width), BF),
            pltpu.VMEM((3 * tokens, width), BF),
            pltpu.VMEM((width, 3 * tokens), BF),
            pltpu.VMEM((3 * tokens, width), F32),
            pltpu.VMEM((3 * tokens, width), F32),
            pltpu.VMEM((width, block), F32),
        ],
        "attend_back",
        10 * tokens * 3 * tokens * width * 4,
    )


def project(pieces, weights, local, lines, t_index):
    count = len(pieces)
    rows, depth = pieces[0].shape[0], weights.shape[1]
    tokens, width = rows * count, weights.shape[2]
    outputs = weights.shape[0]

    def kernel(t_ref, w_ref, local_ref, *rest):
        x_ref = rest[count]
        place_rows(x_ref, rest[:count], t_ref[0])
        x = x_ref[...]
        done = []
        for k, line in enumerate(lines):
            value = dot(x, w_ref[k], (1, 0))
            if line is not None:
                value = value + local_ref[0, line : line + 1, :]
            done.append(value.astype(BF))
        if outputs == 3:
            rest[count + 2][...] = done[0]
        rest[count + 1][0] = done[-2]
        rest[count + 1][1] = done[-1]

    outs = [((tokens, depth), BF), ((2, tokens, width), BF)]
    if outputs == 3:
        outs.append(((tokens, width), BF))
    return run(
        kernel, [t_index], [weights, local, *pieces], outs, [], "project",
        2 * tokens * depth * width * outputs,
    )


def project_rows(low, weight, local, line):
    count, depth, width = weight.shape

    def kernel(x_ref, w_ref, local_ref, *outs):
        for mask in range(count):
            outs[mask][...] = (
                dot(x_ref[...], w_ref[mask], (1, 0)) + local_ref[mask, line : line + 1, :]
            ).astype(BF)

    return run(
        kernel, [], [low, weight, local], [((low.shape[0], width), BF)] * count, [],
        "project_rows", 2 * low.shape[0] * depth * width * count,
    )


def normed(total, gain, shift):
    center = total - jnp.mean(total, -1, keepdims=True)
    scale = lax.rsqrt(jnp.mean(center * center, -1, keepdims=True) + 1e-05)
    return center * scale * gain + shift


def out_norm(mixed, weight, residual, vectors, line):
    count, depth, width = weight.shape
    shape = residual.shape

    def kernel(w_ref, r_ref, v_ref, *rest):
        total = r_ref[...].astype(F32) + v_ref[line : line + 1, :]
        for mask in range(count):
            total = total + dot(rest[mask][...], w_ref[mask], (1, 1))
        sum_ref, out_ref, low_ref = rest[count:]
        sum_ref[...] = total
        out = normed(total, v_ref[line + 1 : line + 2, :], v_ref[line + 2 : line + 3, :])
        out_ref[...] = out
        low_ref[...] = out.astype(BF)

    return run(
        kernel, [], [weight, residual, vectors, *mixed], [(shape, F32), (shape, F32), (shape, BF)],
        [], "out_norm", 2 * shape[0] * depth * width * count,
    )


def add_norm(terms, vectors, line):
    shape = terms[0].shape

    def kernel(v_ref, *rest):
        total = v_ref[line : line + 1, :]
        for ref in rest[: len(terms)]:
            total = total + ref[...].astype(F32)
        sum_ref, low_ref = rest[len(terms) :]
        sum_ref[...] = total
        out = normed(total, v_ref[line + 1 : line + 2, :], v_ref[line + 2 : line + 3, :])
        low_ref[...] = out.astype(BF)

    return run(
        kernel, [], [vectors, *terms], [(shape, F32), (shape, BF)], [], "add_norm", 1e6
    )


def ffn_blocks(views, rows, depth, hidden):
    step = views[0][0].shape[2]
    row = pl.BlockSpec((rows, depth), lambda j: (0, 0))

    def weight(first):
        return pl.BlockSpec((1, depth, step), lambda j: (first + j, 0, 0))

    tall = pl.BlockSpec((len(views), 2 * rows, step), lambda j: (0, 0, j))
    line = pl.BlockSpec((len(views), 1, step), lambda j: (0, 0, j))
    specs, arrays = [], []
    for up, up_first, down, down_first in views:
        specs += [weight(up_first), weight(down_first)]
        arrays += [up, down]
    return step, row, tall, line, specs, arrays


def ffn_up_down(own, other, views, first):
    rows, depth = own.shape
    hidden = first.shape[2]
    count = len(views)
    step, row, tall, line, specs, arrays = ffn_blocks(views, rows, depth, hidden)

    def kernel(own_ref, other_ref, b_ref, *rest):
        weights, (act_ref, slope_ref, keep_ref, send_ref, pair, acc) = rest[:-6], rest[-6:]
        j = pl.program_id(0)

        @pl.when(j == 0)
        def _():
            pair[:rows, :] = own_ref[...]
            pair[rows:, :] = other_ref[...]

        total = None
        for v in range(count):
            u = dot(pair[...], weights[2 * v][0], (1, 0)) + b_ref[v]
            phi = 0.5 * (1.0 + lax.erf(u * 0.7071067811865476))
            act = (u * phi).astype(BF)
            act_ref[v] = act
            slope_ref[v] = (phi + u * 0.3989422804014327 * jnp.exp(-0.5 * u * u)).astype(BF)
            term = dot(act, weights[2 * v + 1][0], (1, 1))
            total = term if total is None else total + term

        @pl.when(j == 0)
        def _():
            acc[...] = total

        @pl.when(j > 0)
        def _():
            acc[...] += total

        @pl.when(j == hidden // step - 1)
        def _():
            keep_ref[...] = acc[:rows, :]
            send_ref[...] = acc[rows:, :].astype(BF)

    wide = (count, 2 * rows, hidden)
    return run(
        kernel, [], [own, other, first, *arrays],
        [(wide, BF), (wide, BF), ((rows, depth), F32), ((rows, depth), BF)],
        [pltpu.VMEM((2 * rows, depth), BF), pltpu.VMEM((2 * rows, depth), F32)],
        "ffn_up_down", 8 * rows * depth * hidden * count, (hidden // step,),
        [row, row, line] + specs, [tall, tall, row, row],
    )


def ffn_down_up(own, other, views, slope):
    rows, depth = own.shape
    hidden = slope.shape[2]
    count = len(views)
    step, row, tall, line, specs, arrays = ffn_blocks(views, rows, depth, hidden)

    def kernel(own_ref, other_ref, slope_ref, *rest):
        weights, (du_ref, sum_ref, keep_ref, send_ref, pair, acc) = rest[:-6], rest[-6:]
        j = pl.program_id(0)

        @pl.when(j == 0)
        def _():
            pair[:rows, :] = own_ref[...]
            pair[rows:, :] = other_ref[...]

        total = None
        for v in range(count):
            du = (dot(pair[...], weights[2 * v + 1][0], (1, 0)) * slope_ref[v].astype(F32)).astype(BF)
            du_ref[v] = du
            sum_ref[v] = jnp.sum(du.astype(F32), 0, keepdims=True)
            term = dot(du, weights[2 * v][0], (1, 1))
            total = term if total is None else total + term

        @pl.when(j == 0)
        def _():
            acc[...] = total

        @pl.when(j > 0)
        def _():
            acc[...] += total

        @pl.when(j == hidden // step - 1)
        def _():
            keep_ref[...] = acc[:rows, :]
            send_ref[...] = acc[rows:, :].astype(BF)

    return run(
        kernel, [], [own, other, slope, *arrays],
        [
            ((count, 2 * rows, hidden), BF), ((count, 1, hidden), F32),
            ((rows, depth), F32), ((rows, depth), BF),
        ],
        [pltpu.VMEM((2 * rows, depth), BF), pltpu.VMEM((2 * rows, depth), F32)],
        "ffn_down_up", 8 * rows * depth * hidden * count, (hidden // step,),
        [row, row, tall] + specs, [tall, line, row, row],
    )


def split_blocks(full, keep_ref, send_ref, at, core, blocks, size):
    for p in range(blocks // 2):
        mine = multiple((2 * p + core) * size, size)
        theirs = multiple((2 * p + 1 - core) * size, size)
        keep_ref[at + (p,)] = full[pl.ds(mine, size), :]
        send_ref[at + (p,)] = full[pl.ds(theirs, size), :]


def ffn_weight_grads(x_own, x_other, e_own, e_other, du, act, core, blocks):
    rows, depth = x_own.shape
    count, _, hidden = du.shape
    step = min(512, hidden)
    per = hidden // step
    size = depth // blocks
    split = core is not None

    def kernel(core_ref, x_ref, xo_ref, e_ref, eo_ref, du_ref, act_ref, *rest):
        outs, (xs, es, full) = rest[:-3], rest[-3:]

        @pl.when(pl.program_id(0) == 0)
        def _():
            xs[:rows, :] = x_ref[...]
            xs[rows:, :] = xo_ref[...]
            es[:rows, :] = e_ref[...]
            es[rows:, :] = eo_ref[...]

        up = dot(xs[...], du_ref[0], (0, 0)).astype(BF)
        down = dot(es[...], act_ref[0], (0, 0)).astype(BF)
        if split:
            full[...] = up
            split_blocks(full, outs[0], outs[1], (), core_ref[0], blocks, size)
            full[...] = down
            split_blocks(full, outs[2], outs[3], (), core_ref[0], blocks, size)
        else:
            outs[0][0] = up
            outs[0][1] = down

    row = pl.BlockSpec((rows, depth), lambda j: (0, 0))
    tall = pl.BlockSpec((1, 2 * rows, step), lambda j: (j // per, 0, j % per))
    if split:
        part = pl.BlockSpec((blocks // 2, size, step), lambda j: (0, 0, j))
        outs, out_blocks = [((blocks // 2, size, hidden * count), BF)] * 4, [part] * 4
    else:
        outs = [((2 * count, depth, hidden), BF)]
        out_blocks = [pl.BlockSpec((2, depth, step), lambda j: (j // per, 0, j % per))]
    return run(
        kernel, [core if split else jnp.zeros((1,), jnp.int32)],
        [x_own, x_other, e_own, e_other, du, act], outs,
        [
            pltpu.VMEM((2 * rows, depth), BF),
            pltpu.VMEM((2 * rows, depth), BF),
            pltpu.VMEM((depth, step), BF),
        ],
        "ffn_weight_grads", 8 * rows * depth * hidden * count, (count * per,),
        [row, row, row, row, tall, tall], out_blocks,
    )


def weight_grads(groups, core, blocks):
    arrays, places = [], []
    for group in groups:
        for pair in group:
            spot = []
            for array in pair:
                known = [i for i, a in enumerate(arrays) if a is array]
                if not known:
                    arrays.append(array)
                    known = [len(arrays) - 1]
                spot.append(known[0])
            places.append(spot)
    depth, width = groups[0][0][0].shape[1], groups[0][0][1].shape[1]
    size = depth // blocks
    count = len(arrays)

    def kernel(core_ref, *rest):
        outs, full = rest[count:-1], rest[-1]
        number = 0
        for g, group in enumerate(groups):
            for j in range(len(group)):
                left, right = places[number]
                value = dot(rest[left][...], rest[right][...], (0, 0)).astype(BF)
                if core is None:
                    outs[g][j] = value
                else:
                    full[...] = value
                    split_blocks(
                        full, outs[2 * g], outs[2 * g + 1], (j,), core_ref[0], blocks, size
                    )
                number += 1

    outs = []
    for group in groups:
        if core is None:
            outs.append(((len(group), depth, width), BF))
        else:
            outs += [((len(group), blocks // 2, size, width), BF)] * 2
    flops = sum(2 * left.shape[0] * depth * width for group in groups for left, right in group)
    return run(
        kernel, [jnp.zeros((1,), jnp.int32) if core is None else core], arrays, outs,
        [pltpu.VMEM((depth, width), BF)], "weight_grads", flops,
    )


def norm_grad_body(terms, summed, gain, grad_ref, low_ref, sums_ref):
    grad = terms[0][...].astype(F32)
    for ref in terms[1:]:
        grad = grad + ref[...].astype(F32)
    total = summed[...]
    center = total - jnp.mean(total, -1, keepdims=True)
    scale = lax.rsqrt(jnp.mean(center * center, -1, keepdims=True) + 1e-05)
    unit = center * scale
    inner = grad * gain
    out = scale * (
        inner - jnp.mean(inner, -1, keepdims=True) - unit * jnp.mean(inner * unit, -1, keepdims=True)
    )
    low = out.astype(BF)
    grad_ref[...] = out
    low_ref[...] = low
    sums_ref[0:1, :] = jnp.sum(low.astype(F32), 0, keepdims=True)
    sums_ref[1:2, :] = jnp.sum(grad * unit, 0, keepdims=True)
    sums_ref[2:3, :] = jnp.sum(grad, 0, keepdims=True)
    return low


def norm_grad(terms, summed, gain, line):
    shape = summed.shape

    def kernel(sum_ref, gain_ref, *rest):
        norm_grad_body(rest[: len(terms)], sum_ref, gain_ref[line : line + 1, :], *rest[len(terms) :])

    return run(
        kernel, [], [summed, gain, *terms], [(shape, F32), (shape, BF), ((3, shape[1]), F32)], [],
        "norm_grad", 1e6,
    )


def norm_out_grad(terms, summed, gain, line, weight):
    shape = summed.shape
    count, depth, width = weight.shape

    def kernel(sum_ref, gain_ref, w_ref, *rest):
        outs = rest[len(terms) :]
        low = norm_grad_body(rest[: len(terms)], sum_ref, gain_ref[line : line + 1, :], *outs[:3])
        for mask in range(count):
            outs[3 + mask][...] = dot(low, w_ref[mask], (1, 0)).astype(BF)

    return run(
        kernel, [], [summed, gain, weight, *terms],
        [(shape, F32), (shape, BF), ((3, shape[1]), F32)] + [((shape[0], width), BF)] * count, [],
        "norm_out_grad", 2 * shape[0] * depth * width * count,
    )


def input_grads(dq, own, below, above, weights, t_index, count):
    tokens, width = dq.shape
    rows, depth = tokens // count, weights.shape[1]
    ahead = weights.shape[0] - 2

    def kernel(t_ref, w_ref, dq_ref, own_ref, below_ref, above_ref, dk_ref, dv_ref, sums_ref, *rest):
        full = rest[count]
        for j, ref in enumerate((dk_ref, dv_ref)):
            ref[...] = (
                own_ref[j] + below_ref[j].astype(F32) + above_ref[j].astype(F32)
            ).astype(BF)
        sums_ref[0:1, :] = jnp.sum(dq_ref[...].astype(F32), 0, keepdims=True)
        sums_ref[1:2, :] = jnp.sum(dv_ref[...].astype(F32), 0, keepdims=True)
        total = dot(dk_ref[...], w_ref[ahead], (1, 1)) + dot(dv_ref[...], w_ref[ahead + 1], (1, 1))
        if ahead:
            total = total + dot(dq_ref[...], w_ref[0], (1, 1))
        full[...] = total
        for mask in range(count):
            part = full[pl.ds(multiple((t_ref[0] ^ mask) * rows, rows), rows), :]
            rest[mask][...] = part.astype(rest[mask].dtype)

    return run(
        kernel, [t_index], [weights, dq, own, below, above],
        [((tokens, width), BF)] * 2 + [((2, width), F32), ((rows, depth), F32)]
        + [((rows, depth), BF)] * (count - 1),
        [pltpu.VMEM((tokens, depth), F32)], "input_grads",
        2 * tokens * width * depth * weights.shape[0],
    )


def asked_grad(pieces, weight):
    count, depth, width = weight.shape
    rows = pieces[0].shape[0]

    def kernel(w_ref, *rest):
        total = dot(rest[0][...], w_ref[0], (1, 1))
        for mask in range(1, count):
            total = total + dot(rest[mask][...], w_ref[mask], (1, 1))
        rest[count][...] = total

    return run(
        kernel, [], [weight, *pieces], [((rows, depth), F32)], [], "asked_grad",
        2 * rows * depth * width * count,
    )[0]


def by_mask(values, t_index, count):
    tokens, width = values.shape
    rows = tokens // count

    def kernel(t_ref, x_ref, *outs):
        for mask in range(count):
            outs[mask][...] = x_ref[pl.ds(multiple((t_ref[0] ^ mask) * rows, rows), rows), :]

    return run(kernel, [t_index], [values], [((rows, width), BF)] * count, [], "by_mask", 1000)


def in_order(pieces, t_index):
    count = len(pieces)
    rows, width = pieces[0].shape

    def kernel(t_ref, *refs):
        place_rows(refs[count], refs[:count], t_ref[0])

    return run(
        kernel, [t_index], pieces, [((rows * count, width), BF)], [], "in_order", 1000
    )[0]


LINES = 32
ENC_ATT, ENC_FFN, SELF_ATT, CROSS_ATT, DEC_FFN, ENC_FIRST, DEC_FIRST = 0, 5, 8, 13, 18, 21, 25


def pack_small(arrays, width):
    def kernel(*refs):
        lines = []
        for ref in refs[:-1]:
            value = ref[...].astype(F32)
            if value.shape[1] > width:
                value = jnp.concatenate(
                    [value[:, i : i + width] for i in range(0, value.shape[1], width)], 0
                )
            lines.append(value)
        used = sum(value.shape[0] for value in lines)
        lines.append(jnp.zeros((LINES - used, width), F32))
        whole = jnp.concatenate(lines, 0)
        refs[-1][...] = jnp.concatenate([whole[: LINES // 2], whole[LINES // 2 :]], 1).astype(BF)

    blocks = [pl.BlockSpec(array.shape, lambda i: (0, 0)) for array in arrays]
    shape = (LINES // 2, 2 * width)
    return run(
        kernel, [], arrays, [(shape, BF)], [], "pack_small", 0, (1,), blocks,
        [pl.BlockSpec(shape, lambda i: (0, 0))],
    )[0]


def unpack_small(parts, t_index, count, features, wide_masks):
    peers, lines, width = parts.shape[0], LINES, parts.shape[2] // 2
    share_ = peers // count
    quarter = 4
    hidden = share_ * quarter * width

    def kernel(t_ref, x_ref, table, local, enc_ref, dec_ref):
        for f in range(peers):
            value = x_ref[f].astype(F32)
            span = slice(f * width, (f + 1) * width)
            table[: lines // 2, span] = value[:, :width]
            table[lines // 2 :, span] = value[:, width:]
        for mask in range(count):
            local[mask] = table[:, pl.ds(multiple((t_ref[0] ^ mask) * features, 128), features)]
        for ref, first in ((enc_ref, ENC_FIRST), (dec_ref, DEC_FIRST)):
            for v, mask in enumerate(wide_masks):
                for f in range(share_):
                    for q in range(quarter):
                        at = (f * quarter + q) * width
                        ref[v, :, at : at + width] = local[
                            mask, first + q : first + q + 1, f * width : (f + 1) * width
                        ]

    first = ((len(wide_masks), 1, hidden), F32)
    return run(
        kernel, [t_index], [parts],
        [((lines, peers * width), F32), ((count, lines, features), F32), first, first], [],
        "unpack_small", 0,
    )


def pack_grads(sums, columns, firsts, t_index, peers, wide_masks):
    depth = sums[0].shape[1]
    width = depth // peers
    features = columns[0].shape[1]
    share_ = features // width
    quarter = 4
    arrays = list(sums) + list(columns) + list(firsts)

    def kernel(t_ref, *refs):
        out, table = refs[-2:]
        table[...] = jnp.zeros_like(table)
        own = pl.ds(multiple(t_ref[0] * features, 128), features)
        att = (ENC_ATT, SELF_ATT, CROSS_ATT)
        for first, s_ref, c_ref in zip(att, refs[:3], refs[5:8]):
            table[first + 2 : first + 5, :] = s_ref[...]
            table[first : first + 2, own] = c_ref[...]
        for first, s_ref in zip((ENC_FFN, DEC_FFN), refs[3:5]):
            table[first : first + 3, :] = s_ref[...]
        for first, f_ref in zip((ENC_FIRST, DEC_FIRST), refs[8:10]):
            for v, mask in enumerate(wide_masks):
                strip = []
                for q in range(quarter):
                    pieces = []
                    for f in range(share_):
                        at = (f * quarter + q) * width
                        pieces.append(f_ref[v, :, at : at + width])
                    strip.append(jnp.concatenate(pieces, 1))
                there = pl.ds(multiple((t_ref[0] ^ mask) * features, 128), features)
                table[first : first + quarter, there] = jnp.concatenate(strip, 0)
        for f in range(peers):
            out[f] = table[:, f * width : (f + 1) * width]

    return run(
        kernel, [t_index], arrays, [((peers, LINES, width), F32)],
        [pltpu.VMEM((LINES, depth), F32)], "pack_grads", 0,
    )[0]


def unpack_grads(terms, shapes):
    def kernel(*refs):
        value = refs[0][...]
        for ref in refs[1 : len(terms)]:
            value = value + ref[...]
        width = value.shape[1]
        line = 0
        for ref in refs[len(terms) :]:
            rows, columns = ref.shape
            for r in range(rows):
                for at in range(0, columns, width):
                    ref[r : r + 1, at : at + width] = value[line : line + 1, :]
                    line += 1

    return run(kernel, [], terms, [(shape, F32) for shape in shapes], [], "unpack_grads", 0)


def token_spans(seq_lens, pic_start, pic_len, base, tokens, block):
    count, pictures = pic_start.shape
    blocks = tokens // block

    def kernel(lens, starts, extents, base_ref, both, text, both_bounds, text_bounds):
        places = lax.broadcasted_iota(jnp.int32, (1, tokens), 1) + tokens
        zero = jnp.zeros((1, tokens), jnp.int32)
        begin, end = zero, zero
        low, high = [zero] * pictures, [zero] * pictures
        edges = [
            [jnp.int32(3 * tokens), jnp.int32(0), jnp.int32(tokens + (i + 1) * block)]
            for i in range(blocks)
        ]
        start = tokens - base_ref[0]
        for s in range(count):
            stop = start + lens[s]
            inside = (places >= start) & (places < stop)
            begin = jnp.where(inside, start, begin)
            end = jnp.where(inside, stop, end)
            spans = []
            for k in range(pictures):
                first = start + starts[s, k]
                last = jnp.minimum(first + extents[s, k], stop)
                member = inside & (places >= first) & (places < last)
                low[k] = jnp.where(member, first, low[k])
                high[k] = jnp.where(member, last, high[k])
                spans.append((first, last))
            for i in range(blocks):
                from_, to = tokens + i * block, tokens + (i + 1) * block
                meets = (start < to) & (stop > from_)
                edge = edges[i]
                edge[0] = jnp.where(meets, jnp.minimum(edge[0], start), edge[0])
                edge[1] = jnp.where(meets, jnp.maximum(edge[1], stop), edge[1])
                for first, last in spans:
                    touches = (first < to) & (last > from_)
                    edge[2] = jnp.where(touches, jnp.maximum(edge[2], last), edge[2])
            start = stop
        both[...] = jnp.concatenate([begin, end] + [zero] * 6, 0)
        seen = [begin, places + 1]
        for k in range(pictures):
            seen += [low[k], high[k]]
        text[...] = jnp.concatenate(seen + [zero] * (8 - len(seen)), 0)
        for i in range(blocks):
            first = lax.div(edges[i][0], jnp.int32(block))
            both_bounds[2 * i] = first
            both_bounds[2 * i + 1] = lax.div(edges[i][1] + (block - 1), jnp.int32(block))
            text_bounds[2 * i] = first
            text_bounds[2 * i + 1] = lax.div(edges[i][2] + (block - 1), jnp.int32(block))

    whole = pl.BlockSpec(memory_space=pltpu.VMEM)
    scalars = pl.BlockSpec(memory_space=pltpu.SMEM)
    return run(
        kernel, [seq_lens, pic_start, pic_len, base], [],
        [((8, tokens), jnp.int32)] * 2 + [((2 * blocks,), jnp.int32)] * 2, [], "token_spans", 0,
        None, None, [whole, whole, scalars, scalars],
    )


def per_device(
    enc_in,
    dec_in,
    enc_cot,
    dec_cot,
    seq_lens,
    pic_start,
    pic_len,
    enc_attn_w,
    enc_attn_bias,
    enc_attn_norm,
    enc_ffn_w,
    enc_ffn_b1,
    enc_ffn_vec,
    self_attn_w,
    self_attn_bias,
    self_attn_norm,
    cross_attn_w,
    cross_attn_bias,
    cross_attn_norm,
    dec_ffn_w,
    dec_ffn_b1,
    dec_ffn_vec,
):
    rows = enc_in.shape[0]
    tensor_size = lax.axis_size("tensor")
    fsdp_size = lax.axis_size("fsdp")
    t_index = lax.axis_index("tensor")
    f_index = lax.axis_index("fsdp")
    t_ref = t_index[None].astype(jnp.int32)
    core = (f_index % 2)[None].astype(jnp.int32)
    tokens = rows * tensor_size
    features = enc_attn_w.shape[2]
    hidden = enc_ffn_w.shape[2]
    t_down = bits_of("tensor")[::-1]
    t_up = bits_of("tensor")
    wide_down = t_down[:-1]
    wide_up = t_up[1:]
    t_masks = range(tensor_size)
    wide_masks = range(0, tensor_size, 2)
    wide_count = len(wide_masks)

    small = [
        enc_attn_bias, enc_attn_norm, enc_ffn_vec, self_attn_bias, self_attn_norm,
        cross_attn_bias, cross_attn_norm, dec_ffn_vec, enc_ffn_b1, dec_ffn_b1,
    ]
    block = min(256, tokens)
    base = (f_index * tokens)[None].astype(jnp.int32)
    spans = token_spans(seq_lens, pic_start, pic_len, base, tokens, block)
    both = (spans[0], spans[2], 1)
    text = (spans[1], spans[3], 1 + pic_start.shape[1])

    first_order, second_order = plane_orders()

    def later(value, ready):
        return lax.optimization_barrier((value, ready))[0]

    class Pair:
        def __init__(self, halves, splits):
            self.plans = [
                Gather(half[None], order, split)
                for half, order, split in zip(halves, (first_order, second_order), splits)
            ]

        def hop(self, *gate):
            if self.plans[0].came is not None:
                came_ = join([plan.came for plan in self.plans], *gate)
                for plan, value in zip(self.plans, came_):
                    plan.came = value
                gate = ()
            return [plan.hop(*gate) for plan in self.plans]

        def result(self):
            return [plan.result() for plan in self.plans]

    slices = hidden // features

    def ffn_slices(shard):
        cut = shard.reshape(2, rows, slices, features)
        return jnp.moveaxis(cut, 2, 1).reshape(2 * slices, rows, features)

    def ups(shards):
        return [ffn_slices(shard)[:slices] for shard in shards]

    def downs(shards):
        return [ffn_slices(shard)[slices:] for shard in shards]

    def ffn_views(*arrays):
        views = []
        for up, down in arrays:
            for at in range(0, up.shape[0], slices):
                views.append((up, at, down, at))
        return views

    far = (wide_count - 1) * slices

    def exchange(pieces_, *hold):
        held = dict(enumerate(pieces_))
        for bit in t_up:
            moved = [mask for mask in t_masks if mask & bit]
            came_ = swap(jnp.stack([held[mask] for mask in moved]), "tensor", bit)
            if bit == 1:
                came_ = join(came_, *hold)
            for at, mask in enumerate(moved):
                held[mask] = came_[at]
        return [held[mask] for mask in t_masks]

    def doubled(value):
        held = {0: value}
        for bit in t_down:
            known = sorted(held)
            came_ = swap(jnp.stack([held[mask] for mask in known]), "tensor", bit)
            gate = yield came_
            came_ = join(came_, *(gate or ()))
            for at, mask in enumerate(known):
                held[mask | bit] = came_[at]
        yield [held[mask] for mask in t_masks]

    peers = fsdp_size
    up_pairs = [(i, i + 1) for i in range(peers - 1)]
    down_pairs = [(j, i) for i, j in up_pairs]

    def halo(pair):
        before = lax.ppermute(pair, "fsdp", up_pairs)
        after = lax.ppermute(pair, "fsdp", down_pairs)
        return before, pair, after

    def attend_fg(queries, window, mode):
        return attend(queries, window, mode[0], mode[1], t_ref, tensor_size, mode[2])

    def attend_back_fg(queries, window, grads, mixed_t, totals, mode):
        return attend_back(
            queries, window, grads, mixed_t, totals, mode[0], mode[1], t_ref, tensor_size, mode[2]
        )

    class Folds:
        def __init__(self, parts_, at):
            self.folds = [
                Fold(parts_[2 * k], parts_[2 * k + 1], order[:-1], at)
                for k, order in enumerate((first_order, second_order))
            ]

        def hop(self, *gate):
            return [fold.hop(*gate) for fold in self.folds]

        def next(self, *gate):
            return halve_all(self.folds, *gate)

        def result(self, *gate):
            return [fold.result(*gate) for fold in self.folds]

    class SmallSum:
        def __init__(self, value):
            self.value, self.came = value, None
            self.bits = [("fsdp", bit) for bit in bits_of("fsdp")[::-1]]
            self.bits += [("tensor", bit) for bit in t_up]

        def hop(self):
            if self.came is not None:
                self.value = self.value + self.came
            axis, bit = self.bits.pop(0)
            sent = self.value
            if axis == "fsdp":
                half = self.value.shape[0] // 2
                mine = (f_index // bit) % 2
                sent = lax.dynamic_slice_in_dim(self.value, (1 - mine) * half, half, 0)
                self.value = lax.dynamic_slice_in_dim(self.value, mine * half, half, 0)
            self.came = swap(sent, axis, bit)

        def result(self):
            while self.bits:
                self.hop()
            return [self.value[0], self.came[0]]

    class WideShare:
        def __init__(self, halves):
            self.held = {
                mask: halves[:, :, j * hidden : (j + 1) * hidden]
                for j, mask in enumerate(wide_masks)
            }
            self.bits = list(wide_up)

        def hop(self):
            bit = self.bits.pop(0)
            new = []
            for mask in sorted(self.held):
                if mask not in self.held or mask & (2 * bit - 1):
                    continue
                came_ = swap(self.held.pop(mask | bit).astype(BF), "tensor", bit)
                self.held[mask] = self.held[mask] + came_.astype(F32)
                new.append(came_)
            self.came = new
            return new

        def result(self):
            while self.bits:
                self.hop()
            return self.held[0]

    pending = [[], [], [], []]

    def due(*values, lag=2):
        pending[lag - 1].extend(values)

    def fg(value):
        waits = pending.pop(0)
        pending.append([])
        return join(value, *waits)

    packed = pack_small(small, enc_attn_bias.shape[1])
    depth = enc_in.shape[1]
    enc_pieces = reach(
        jnp.concatenate([enc_in, enc_attn_w[3]], 1), "tensor", t_masks[:0:-1]
    )
    first_shard = jnp.concatenate([enc_attn_w[:3].reshape(-1, features), packed])
    qkv_plan = Gather(first_shard[None], first_order, [(3, rows), (1, packed.shape[0])])
    qkv_plan.hop()
    enc_qkv, parts = qkv_plan.result()
    table, local, enc_first, dec_first = unpack_small(
        parts.reshape(fsdp_size, -1, features), t_ref, tensor_size, features, wide_masks
    )
    plan1 = Pair(
        (
            jnp.concatenate([self_attn_w[:3]] + ups([enc_ffn_w])),
            jnp.concatenate(
                [piece[None, :, depth:] for piece in enc_pieces] + downs([enc_ffn_w])
            ),
        ),
        ([3, slices], [tensor_size, slices]),
    )
    due(plan1.hop())
    dec_steps = doubled(
        join(
            jnp.concatenate([dec_in, self_attn_w[3], cross_attn_w[3], cross_attn_w[0]], 1),
            *enc_pieces[1:],
        )
    )
    due(next(dec_steps))

    flat_e, pair_e, query_e = project(
        fg(enc_pieces), enc_qkv, local, (ENC_ATT, None, ENC_ATT + 1), t_ref
    )
    window_e = halo(pair_e)
    r1 = (window_e[0], window_e[2])
    plan1.hop(*r1)
    dec_pieces = dec_steps.send(r1)

    mixed_e, mixed_t_e, totals_e = attend_fg(fg(query_e), window_e, both)
    mixed_e = exchange(mixed_e, dec_pieces)
    r2 = tuple(mixed_e[1:])
    plan1.hop(*r2)
    (self_qkv, own_up), (enc_out_w, own_down) = plan1.result()
    enc_wide = Spread(join(enc_ffn_w, *r2), "tensor", wide_down)
    enc_wide.hop()
    for step in range(len(t_down) - 1):
        dec_pieces = dec_steps.send(r2)

    summed_e, hid, hid_low = out_norm(
        fg(mixed_e), enc_out_w, enc_in, table, ENC_ATT + 2
    )
    hid_other = swap(hid_low, "tensor", 1)
    r3 = (hid_other,)
    flat_s, pair_s, query_s = project(
        fg(join(dec_pieces, hid_low)), self_qkv, local, (SELF_ATT, None, SELF_ATT + 1), t_ref
    )
    spare = [join(piece, *r3)[:, depth:] for piece in dec_pieces]

    def spare_part(which):
        return [piece[None, :, which * features : (which + 1) * features] for piece in spare]

    others = enc_wide.result(*r3)[1:]
    plan2 = Pair(
        (
            jnp.concatenate(ups(others) + spare_part(0) + [cross_attn_w[1:3]]),
            jnp.concatenate(downs(others) + spare_part(1) + spare_part(2)),
        ),
        ([far, tensor_size, 2], [far, tensor_size, tensor_size]),
    )
    plan2.hop()
    window_s = halo(pair_s)
    r4 = (window_s[0], window_s[2])
    mixed_s, mixed_t_s, totals_s = attend_fg(fg(query_s), window_s, text)
    mixed_s = exchange(mixed_s)
    r5 = tuple(mixed_s[1:])
    plan2.hop(*r5)
    dec_wide = Spread(join(dec_ffn_w, *r5), "tensor", wide_down)
    dec_wide.hop()
    plan2.hop(*r5)
    (far_up, self_out_w, cross_kv), (far_down, cross_out_w, cross_query) = plan2.result()
    enc_views = ffn_views((own_up, own_down), (far_up, far_down))
    active_e, slope_e, keep, send = ffn_up_down(hid_low, hid_other, enc_views, enc_first)
    came = swap(send, "tensor", 1)
    r7 = (came,)
    shards = dec_wide.result(send)
    plan4 = Pair(
        (jnp.concatenate(ups(shards)), jnp.concatenate(downs(shards))),
        ([slices + far], [slices + far]),
    )
    plan4.hop()

    summed_s, decoded, decoded_low = out_norm(
        join(mixed_s, send), self_out_w, dec_in, table, SELF_ATT + 2
    )
    ffn_summed_e, encoded = add_norm(
        [hid, join(keep, decoded_low), came], table, ENC_FFN
    )
    enc_rows = spread(encoded, "tensor", t_down)
    plan4.hop(encoded)
    asked = exchange(
        project_rows(join(decoded_low, *enc_rows[1:]), cross_query, local, CROSS_ATT)
    )
    query_c = in_order(asked, t_ref)

    flat_c, pair_c = project(
        enc_rows, cross_kv, local, (None, CROSS_ATT + 1), t_ref
    )
    window_c = halo(pair_c)
    r9 = (window_c[0], window_c[2])
    plan4.hop(*r9)
    mixed_c, mixed_t_c, totals_c = attend_fg(query_c, window_c, both)
    mixed_c = exchange(mixed_c)
    dec_views = ffn_views([array for (array,) in plan4.result()])
    summed_c, crossed, crossed_low = out_norm(
        mixed_c, cross_out_w, decoded, table, CROSS_ATT + 2
    )
    crossed_other = swap(crossed_low, "tensor", 1)
    active_d, slope_d, keep, send = ffn_up_down(
        crossed_low, crossed_other, dec_views, dec_first
    )
    came = swap(send, "tensor", 1)
    ffn_summed_d, final = add_norm([crossed, keep, came], table, DEC_FFN)

    grad_sum_d, low_d, dec_sums = norm_grad([dec_cot], ffn_summed_d, table, DEC_FFN + 1)
    other_d = swap(low_d, "tensor", 1)
    du_d, dec_first_sum, keep, send = ffn_down_up(low_d, other_d, dec_views, slope_d)
    came = swap(send, "tensor", 1)
    dec_grads = ffn_weight_grads(
        crossed_low, crossed_other, low_d, other_d, join(du_d, send), active_d, core, fsdp_size
    )
    dec_fold = Folds(dec_grads, 0)
    due(dec_fold.hop())

    grad_sum_c, low_c, sums_c, *given = norm_out_grad(
        [fg(grad_sum_d), join(keep, dec_grads), came], summed_c, table, CROSS_ATT + 3, cross_out_w
    )
    given = exchange(given)
    b2 = tuple(given[1:])
    due(dec_fold.next(*b2))
    dq_c, below, own, above = attend_back_fg(
        query_c, window_c, fg(given), mixed_t_c, totals_c, both
    )
    below = lax.ppermute(below, "fsdp", down_pairs)
    above = lax.ppermute(above, "fsdp", up_pairs)
    asked_c = exchange(by_mask(dq_c, t_ref, tensor_size))
    b3 = (below, above)
    due(dec_fold.next(*b3))
    dk_c, dv_c, columns_c, *blocks_c = input_grads(
        dq_c, fg(own), below, above, cross_kv, t_ref, tensor_size
    )
    source = Share(blocks_c, "tensor", t_up)
    due(source.hop())
    from_asked = asked_grad([join(asked_c[0], dk_c)] + asked_c[1:], cross_query)
    cross_grads = weight_grads(
        [
            [(flat_c, join(dk_c, from_asked)), (flat_c, dv_c)]
            + [(decoded_low, piece) for piece in asked_c],
            [(low_c, piece) for piece in mixed_c],
        ],
        core, fsdp_size,
    )
    cross_fold = Folds(cross_grads, 1)
    due(cross_fold.hop())

    grad_sum_s, low_s, sums_s, *given = norm_out_grad(
        [fg(join(grad_sum_c, cross_grads)), from_asked], summed_s, table, SELF_ATT + 3, self_out_w
    )
    given = exchange(given)
    b6 = tuple(given[1:])
    source.hop(*b6)
    due(cross_fold.next(*b6), lag=3)
    dq_s, below, own, above = attend_back_fg(
        query_s, window_s, fg(given), mixed_t_s, totals_s, text
    )
    below = lax.ppermute(below, "fsdp", down_pairs)
    above = lax.ppermute(above, "fsdp", up_pairs)
    b7 = (below, above)
    due(cross_fold.next(*b7))
    dec_wide_share = WideShare(jnp.stack(dec_fold.result(*b7)))
    due(dec_wide_share.hop())
    grad_sum_f, low_f, enc_sums = norm_grad(
        [fg(join(enc_cot, dq_s))] + source.result(), ffn_summed_e, table, ENC_FFN + 1
    )
    other_f = swap(low_f, "tensor", 1)
    dk_s, dv_s, columns_s, *blocks_s = input_grads(
        dq_s, join(own, low_f), below, above, self_qkv, t_ref, tensor_size
    )
    b8 = dk_s
    target = Share(blocks_s, "tensor", t_up)
    due(target.hop())
    self_parts = weight_grads(
        [
            [(flat_s, join(dq_s, b8)), (flat_s, dk_s), (flat_s, dv_s)]
            + [(low_s, piece) for piece in mixed_s]
        ],
        core, fsdp_size,
    )
    self_fold = Fold(self_parts[0], self_parts[1], first_order[:-1], 1)
    due(self_fold.hop())
    du_e, enc_first_sum, keep, send = ffn_down_up(
        fg(join(low_f, self_parts)), other_f, enc_views, slope_e
    )
    came = swap(send, "tensor", 1)
    b10 = came
    due(target.hop(b10), lag=3)
    due(self_fold.next(b10), lag=3)
    enc_grads = ffn_weight_grads(
        hid_low, hid_other, low_f, other_f, join(du_e, send), active_e, core, fsdp_size
    )
    enc_fold = Folds(enc_grads, 0)
    due(enc_fold.hop())

    grad_sum_e, low_e, sums_e, *given = norm_out_grad(
        [grad_sum_f, fg(join(keep, enc_grads)), came], summed_e, table, ENC_ATT + 3, enc_out_w
    )
    given = exchange(given)
    b11 = tuple(given[1:])
    due(enc_fold.next(*b11))
    due(self_fold.next(*b11))
    dq_e, below, own, above = attend_back_fg(
        query_e, window_e, fg(given), mixed_t_e, totals_e, both
    )
    below = lax.ppermute(below, "fsdp", down_pairs)
    above = lax.ppermute(above, "fsdp", up_pairs)
    b12 = (below, above)
    enc_fold.next(*b12)
    cross_first, cross_outs = cross_fold.result(*b12)
    self_own = self_fold.result(*b12)
    late_share = Share(
        [
            jnp.stack([cross_first[2 + mask], cross_outs[mask], self_own[3 + mask]])
            for mask in t_masks
        ],
        "tensor", t_up,
    )
    dk_e, dv_e, columns_e, *blocks_e = input_grads(
        dq_e, fg(own), below, above, enc_qkv, t_ref, tensor_size
    )
    b13 = dk_e
    enc_share = Share(blocks_e, "tensor", t_up)
    enc_share.hop()
    small_sum = SmallSum(
        pack_grads(
            [sums_e, sums_s, sums_c, enc_sums, dec_sums], [columns_e, columns_s, columns_c],
            [enc_first_sum, dec_first_sum], t_ref, fsdp_size, wide_masks,
        )
    )
    small_sum.hop()
    enc_att = weight_grads(
        [
            [(flat_e, dq_e), (flat_e, join(dk_e, tuple(blocks_e))), (flat_e, dv_e)],
            [(low_e, piece) for piece in mixed_e],
        ],
        core, fsdp_size,
    )
    att_folds = Folds(enc_att, 1)
    att_folds.hop()

    def meet(*items):
        for item, came_ in zip(items, join([item.came for item in items])):
            item.came = came_

    meet(enc_share, small_sum, *att_folds.folds, *enc_fold.folds)
    att_folds.next()
    enc_share.hop()
    small_sum.hop()
    enc_wide_share = WideShare(jnp.stack(enc_fold.result()))
    enc_wide_share.hop()
    meet(small_sum, *att_folds.folds)
    att_folds.next()
    small_sum.hop()
    late_share.hop()
    meet(late_share, small_sum, *att_folds.folds)
    enc_att_own, enc_att_out = att_folds.result()
    out_share = Share([enc_att_out[mask] for mask in t_masks], "tensor", t_up)
    out_share.hop()
    late_share.hop()
    small_sum.hop()
    meet(out_share, late_share, small_sum)
    out_share.hop()
    small_out = unpack_grads(small_sum.result(), [item.shape for item in small])
    enc_grad = jnp.concatenate([enc_att_own, total(out_share.result())[None]])
    dec_ffn_grad = dec_wide_share.result()
    enc_ffn_grad = enc_wide_share.result()
    late = total(late_share.result())
    cross_grad = jnp.concatenate([late[0:1], cross_first[:2], late[1:2]])
    self_grad = jnp.concatenate([self_own[:3], late[2:3]])
    grad_source = total([grad_sum_e] + enc_share.result())
    grad_target = total([grad_sum_s] + target.result())

    (
        enc_bias_g, enc_norm_g, enc_vec_g, self_bias_g, self_norm_g,
        cross_bias_g, cross_norm_g, dec_vec_g, enc_b1_g, dec_b1_g,
    ) = small_out
    return (
        encoded,
        final,
        grad_source,
        grad_target,
        enc_grad,
        enc_bias_g,
        enc_norm_g,
        enc_ffn_grad,
        enc_b1_g,
        enc_vec_g,
        self_grad,
        self_bias_g,
        self_norm_g,
        cross_grad,
        cross_bias_g,
        cross_norm_g,
        dec_ffn_grad,
        dec_b1_g,
        dec_vec_g,
    )


def solution(mesh):
    rows = P(("fsdp", "tensor"), None)
    weight = P(None, "fsdp", "tensor")
    vector = P(None, "fsdp")
    att, ffn = (weight, vector, vector), (weight, vector, vector)
    in_specs = (rows,) * 4 + (P(),) * 3 + (att + ffn + att + att + ffn)
    out_specs = (rows,) * 4 + (att + ffn + att + att + ffn)
    return jax.shard_map(
        per_device, mesh=mesh, in_specs=in_specs, out_specs=out_specs, check_vma=False
    )
```

```python
import functools
import jax
import jax.numpy as jnp
from jax import lax
from jax.experimental import pallas as pl
from jax.experimental.pallas import tpu as pltpu
from jax.sharding import PartitionSpec as P

HD = 64
BF = jnp.bfloat16
F32 = jnp.float32
PACE = 30000000000


def bits_of(axis):
    count, bit, bits = lax.axis_size(axis), 1, []
    while bit < count:
        bits.append(bit)
        bit *= 2
    return bits


def swap(value, axis, mask):
    return lax.ppermute(value, axis, [(i, i ^ mask) for i in range(lax.axis_size(axis))])


def join(value, *ready):
    return lax.optimization_barrier((value, ready))[0] if ready else value


def spread(value, axis, order, gates=()):
    pieces = {0: value}
    for k, bit in enumerate(order):
        for mask in list(pieces):
            piece = pieces[mask]
            if mask and k < len(gates):
                piece = join(piece, *gates[k])
            pieces[mask | bit] = swap(piece, axis, bit)
    if len(gates) > len(order):
        return [pieces[0]] + [join(pieces[mask], *gates[-1]) for mask in sorted(pieces)[1:]]
    return [pieces[mask] for mask in sorted(pieces)]


def total(items):
    out = items[0].astype(F32)
    for item in items[1:]:
        out = out + item.astype(F32)
    return out


def plane_orders():
    bits = bits_of("fsdp")
    return bits[1:] + bits[:1], bits[1:][::-1] + bits[:1]


def placed(parts, index, splits):
    arrays = [array for array, masks in parts]
    total = sum(len(masks) for array, masks in parts)
    cols = arrays[0].shape[-1]
    shapes = [
        (width, total, arrays[0].shape[2], cols)
        if isinstance(width, int)
        else (width[0], total, width[1], cols)
        for width in splits
    ]
    moves_ = total * sum(1 if isinstance(width, int) else width[0] for width in splits)

    def kernel(index_ref, *refs):
        ins, outs, sems = refs[: len(parts)], refs[len(parts) : -1], refs[-1]
        copies = []
        for (array, masks), ref in zip(parts, ins):
            for at, mask in enumerate(masks):
                first = 0
                for out, width in zip(outs, splits):
                    if isinstance(width, int):
                        moves = [(ref.at[at, first : first + width], out.at[:, index_ref[0] ^ mask])]
                        first += width
                    else:
                        moves = []
                        for line in range(width[0]):
                            moves.append(
                                (ref.at[at, first : first + width[1]], out.at[line, index_ref[0] ^ mask])
                            )
                            first += width[1]
                    for source, target in moves:
                        copy = pltpu.make_async_copy(source, target, sems.at[len(copies)])
                        copy.start()
                        copies.append(copy)
        for copy in copies:
            copy.wait()

    outs = pl.pallas_call(
        kernel,
        out_shape=[jax.ShapeDtypeStruct(shape, arrays[0].dtype) for shape in shapes],
        in_specs=[pl.BlockSpec(memory_space=pltpu.SMEM)]
        + [pl.BlockSpec(memory_space=pl.ANY)] * len(arrays),
        out_specs=[pl.BlockSpec(memory_space=pltpu.VMEM)] * len(splits),
        scratch_shapes=[pltpu.SemaphoreType.DMA((moves_,))],
        compiler_params=pltpu.CompilerParams(vmem_limit_bytes=32 * 2**20),
        cost_estimate=pl.CostEstimate(flops=PACE, bytes_accessed=1, transcendentals=0),
        name="placed",
    )(index[None], *arrays)
    return [out.reshape(out.shape[0], -1, cols) for out in outs]


def gather_plane(shard, order, splits):
    return Gather(shard[None], order, splits).result()


def reach(value, axis, masks):
    pieces = {0: value}
    for mask in masks:
        pieces[mask] = swap(value, axis, mask)
    return [pieces[mask] for mask in sorted(pieces)]


class Gather:
    def __init__(self, held, order, splits):
        self.held, self.masks, self.order, self.splits = held, [0], list(order), splits
        self.came = None

    def take(self, gate):
        if self.came is not None:
            came = join(self.came, *gate)
            self.held = jnp.concatenate([self.held, came], 0)
            self.masks = self.masks + [mask | self.bit for mask in self.masks]

    def hop(self, *gate):
        self.take(gate)
        self.bit = self.order.pop(0)
        self.came = swap(self.held, "fsdp", self.bit)
        return self.came

    def result(self):
        while self.order:
            self.hop()
        parts = [(self.held, self.masks), (self.came, [mask | self.bit for mask in self.masks])]
        return placed(parts, lax.axis_index("fsdp"), self.splits)


class Spread:
    def __init__(self, value, axis, bits):
        self.axis, self.pieces, self.level, self.last = axis, {0: value}, 0, len(bits)
        self.masks = [m for m in range(lax.axis_size(axis)) if m & ~sum(bits) == 0]

    def hop(self, *gate):
        self.level += 1
        new = []
        for mask in self.masks[::-1]:
            if mask.bit_count() == self.level:
                low = mask & -mask
                piece = self.pieces[mask ^ low]
                if mask != low:
                    piece = join(piece, *gate)
                self.pieces[mask] = swap(piece, self.axis, low)
                new.append(self.pieces[mask])
        return new

    def result(self, *gate):
        while self.level < self.last:
            self.hop()
        return [join(self.pieces[m], *(gate if m else ())) for m in self.masks]


class Share:
    def __init__(self, pieces, axis, bits):
        self.axis, self.held, self.bits = axis, dict(enumerate(pieces)), list(bits)
        self.came, self.terms = None, [pieces[0]]

    def hop(self, *gate):
        if self.came is not None:
            came = join(self.came, *gate)
            for at, mask in enumerate(self.kept):
                if mask == 0:
                    self.terms.append(came[at])
                else:
                    self.held[mask] = self.held[mask].astype(F32) + came[at].astype(F32)
            self.came = None
        if self.bits:
            bit = self.bits.pop(0)
            sent = [mask for mask in sorted(self.held) if mask & bit]
            self.kept = [mask ^ bit for mask in sent]
            stack = jnp.stack([self.held.pop(mask).astype(BF) for mask in sent])
            self.came = swap(stack, self.axis, bit)
        return self.came

    def result(self):
        while self.bits or self.came is not None:
            self.hop()
        return self.terms


def halve_all(folds, *gate):
    came = join([fold.came for fold in folds], *gate)
    index = lax.axis_index("fsdp")
    arrays, shapes, bits = [], [], []
    for fold, new in zip(folds, came):
        dim, bit = fold.cut()
        shape = fold.value.shape
        lead = 1
        for extent in shape[:dim]:
            lead *= extent
        rest = 1
        for extent in shape[dim + 1 : -2]:
            rest *= extent
        flat = (lead, 2, rest) + shape[-2:]
        arrays += [fold.value.reshape(flat), new.reshape(flat)]
        shapes.append((shape[:dim] + shape[dim + 1 :], (lead, rest) + shape[-2:]))
        bits.append(bit)
    mine = jnp.stack([(index // bit) % 2 for bit in bits]).astype(jnp.int32)

    def kernel(mine_ref, *refs):
        ins, outs = refs[: len(arrays)], refs[len(arrays) :]
        for n in range(len(folds)):
            value, new = ins[2 * n : 2 * n + 2]
            here = mine_ref[n]
            lead, unused, rest = value.shape[:3]
            for out, which in zip(outs[2 * n : 2 * n + 2], (here, 1 - here)):

                @pl.loop(0, lead)
                def _(i):
                    for j in range(rest):
                        out[i, j] = (
                            value[i, which, j].astype(F32) + new[i, which, j].astype(F32)
                        ).astype(BF)

    outs = []
    for full, flat in shapes:
        outs += [(flat, BF)] * 2
    done = run(kernel, [mine], arrays, outs, [], "halve", 0)
    sent = []
    for n, fold in enumerate(folds):
        fold.value = done[2 * n].reshape(shapes[n][0])
        fold.sent = done[2 * n + 1].reshape(shapes[n][0])
        fold.bit = bits[n]
        sent.append(fold.hop())
    return sent


class Fold:
    def __init__(self, keep, send, order, at):
        bits = bits_of("fsdp")
        self.live, self.order, self.at = bits[1:][::-1], list(order), at
        split = keep.shape[:at] + (2,) * len(self.live) + keep.shape[at + 1 :]
        self.value, self.sent, self.bit = keep.reshape(split), send.reshape(split), bits[0]

    def hop(self, *gate):
        self.came = swap(join(self.sent, *gate), "fsdp", self.bit)
        return self.came

    def cut(self):
        bit = self.order.pop(0)
        dim = self.at + self.live.index(bit)
        self.live.remove(bit)
        return dim, bit

    def next(self, *gate):
        return halve_all([self], *gate)[0]

    def result(self, *gate):
        while self.order:
            self.next(*gate)
            gate = ()
        return self.value.astype(F32) + join(self.came, *gate).astype(F32)


MIB = 2**20
QUICK = ("halve",)
HEAD_SCALE = HD ** (-0.5)


def run(kernel, scalars, arrays, outs, scratch, name, flops, grid=None, in_blocks=None, out_blocks=None):
    arrays = list(arrays)
    whole = pl.BlockSpec(memory_space=pltpu.VMEM)
    in_specs = [pl.BlockSpec(memory_space=pltpu.SMEM)] * len(scalars)
    in_specs += in_blocks if in_blocks else [whole] * len(arrays)
    extra = {"grid": grid} if grid else {}
    return pl.pallas_call(
        kernel,
        out_shape=[jax.ShapeDtypeStruct(shape, kind) for shape, kind in outs],
        in_specs=in_specs,
        out_specs=out_blocks if out_blocks else [whole] * len(outs),
        scratch_shapes=scratch,
        compiler_params=pltpu.CompilerParams(vmem_limit_bytes=40 * MIB),
        cost_estimate=pl.CostEstimate(
            flops=1 if name in QUICK else PACE, bytes_accessed=1, transcendentals=0
        ),
        name=name,
        **extra,
    )(*scalars, *arrays)


def dot(left, right, dims):
    return lax.dot_general(left, right, ((dims[:1], dims[1:]), ((), ())), preferred_element_type=F32)


def head_mask(rows, which, level):
    lane = lax.broadcasted_iota(jnp.int32, (rows, 128), 1)
    return jnp.where(lane // HD == which, level, 0.0).astype(BF)


def tile_allowed(meta, first, size, columns, ranges):
    place = lax.broadcasted_iota(jnp.int32, (size, columns), 0) + first
    allowed = (place >= meta[0:1]) & (place < meta[1:2])
    for k in range(1, ranges):
        allowed = allowed | ((place >= meta[2 * k : 2 * k + 1]) & (place < meta[2 * k + 1 : 2 * k + 2]))
    return allowed


def multiple(value, of):
    return pl.multiple_of(value, of)


def place_rows(ref, pieces, t_index):
    rows = pieces[0].shape[0]
    for mask, piece in enumerate(pieces):
        ref[pl.ds(multiple((t_index ^ mask) * rows, rows), rows), :] = piece[:, : ref.shape[1]]


def attend(queries, windows, meta, bounds, t_index, count, ranges):
    tokens, width = queries.shape
    heads, rows = width // HD, tokens // count
    block = min(256, tokens)
    tiles = 3 * tokens // block

    def kernel(bounds_ref, t_ref, meta_ref, q_ref, b_ref, w_ref, a_ref, *rest):
        o_refs, (ot_ref, lse_ref, keys, v_t, held, acc, nat) = rest[:count], rest[count:]
        for j, ref in enumerate((b_ref, w_ref, a_ref)):
            keys[j * tokens : (j + 1) * tokens, :] = ref[0]
            v_t[:, j * tokens : (j + 1) * tokens] = ref[1].T
        for i in range(tokens // block):
            low, high = bounds_ref[2 * i], bounds_ref[2 * i + 1]
            span = slice(i * block, (i + 1) * block)
            info = meta_ref[:, span]
            asked = []
            for h in range(heads):
                lanes = slice(h // 2 * 128, h // 2 * 128 + 128)
                asked.append(q_ref[span, lanes] * head_mask(block, h % 2, HEAD_SCALE))

            def scores(k, tops):
                first = multiple(k * block, block)
                allowed = tile_allowed(info, first, block, block, ranges)
                out = []
                for h in range(heads):
                    lanes = slice(h // 2 * 128, h // 2 * 128 + 128)
                    s = dot(keys[pl.ds(first, block), lanes], asked[h], (1, 1))
                    s = jnp.where(allowed, s, -1e30)
                    held[h, k] = s
                    out.append(jnp.maximum(tops[h], jnp.max(s, 0, keepdims=True)))
                return tuple(out)

            tops = lax.fori_loop(
                low, high, scores, tuple(jnp.full((1, block), -1e30, F32) for h in range(heads))
            )
            acc[...] = jnp.zeros_like(acc)

            def mixes(k, sums):
                first = multiple(k * block, block)
                out = []
                for h in range(heads):
                    p = jnp.exp(held[h, k] - tops[h])
                    out.append(sums[h] + jnp.sum(p, 0, keepdims=True))
                    some = slice(h * HD, (h + 1) * HD)
                    acc[some, :] += dot(v_t[some, pl.ds(first, block)], p.astype(BF), (1, 0))
                return tuple(out)

            sums = lax.fori_loop(
                low, high, mixes, tuple(jnp.zeros((1, block), F32) for h in range(heads))
            )
            for h in range(heads):
                some = slice(h * HD, (h + 1) * HD)
                acc[some, :] = acc[some, :] / sums[h]
                lse_ref[h : h + 1, span] = tops[h] + jnp.log(sums[h])
            ot_ref[:, span] = acc[...]
            nat[span, :] = acc[...].T.astype(BF)
        for mask in range(count):
            o_refs[mask][...] = nat[pl.ds(multiple((t_ref[0] ^ mask) * rows, rows), rows), :]

    out = run(
        kernel,
        [bounds, t_index],
        [meta, queries, *windows],
        [((rows, width), BF)] * count + [((width, tokens), F32), ((heads, tokens), F32)],
        [
            pltpu.VMEM((3 * tokens, width), BF),
            pltpu.VMEM((width, 3 * tokens), BF),
            pltpu.VMEM((heads, tiles, block, block), F32),
            pltpu.VMEM((width, block), F32),
            pltpu.VMEM((tokens, width), BF),
        ],
        "attend",
        4 * tokens * 3 * tokens * width * 4,
    )
    return out[:count], out[count], out[count + 1]


def attend_back(queries, windows, grads, mixed_t, totals, meta, bounds, t_index, count, ranges):
    tokens, width = queries.shape
    heads, rows = width // HD, tokens // count
    block = min(256, tokens)

    def kernel(bounds_ref, t_ref, meta_ref, q_ref, b_ref, w_ref, a_ref, ot_ref, lse_ref, *rest):
        g_refs = rest[:count]
        dq_ref, db_ref, dw_ref, da_ref, nat, keys, values, k_t, dk, dv, acc = rest[count:]
        place_rows(nat, g_refs, t_ref[0])
        for j, ref in enumerate((b_ref, w_ref, a_ref)):
            part = slice(j * tokens, (j + 1) * tokens)
            keys[part, :] = ref[0]
            values[part, :] = ref[1]
            k_t[:, part] = ref[0].T
        dk[...] = jnp.zeros_like(dk)
        dv[...] = jnp.zeros_like(dv)
        for i in range(tokens // block):
            low, high = bounds_ref[2 * i], bounds_ref[2 * i + 1]
            span = slice(i * block, (i + 1) * block)
            info = meta_ref[:, span]
            g_t = nat[span, :].astype(F32).T
            asked, given, inner = [], [], []
            for h in range(heads):
                lanes = slice(h // 2 * 128, h // 2 * 128 + 128)
                some = slice(h * HD, (h + 1) * HD)
                asked.append(q_ref[span, lanes] * head_mask(block, h % 2, HEAD_SCALE))
                given.append(nat[span, lanes] * head_mask(block, h % 2, 1.0))
                inner.append(jnp.sum(g_t[some] * ot_ref[some, span], 0, keepdims=True))
            acc[...] = jnp.zeros_like(acc)

            def step(k, carry):
                first = multiple(k * block, block)
                at = pl.ds(first, block)
                allowed = tile_allowed(info, first, block, block, ranges)
                for h in range(heads):
                    lanes = slice(h // 2 * 128, h // 2 * 128 + 128)
                    some = slice(h * HD, (h + 1) * HD)
                    s = dot(keys[at, lanes], asked[h], (1, 1))
                    p = jnp.exp(jnp.where(allowed, s, -1e30) - lse_ref[h : h + 1, span])
                    dp = dot(values[at, lanes], given[h], (1, 1))
                    ds = (p * (dp - inner[h])).astype(BF)
                    dv[at, lanes] += dot(p.astype(BF), given[h], (1, 0))
                    dk[at, lanes] += dot(ds, asked[h], (1, 0))
                    acc[some, :] += dot(k_t[some, at], ds, (1, 0))
                return carry

            lax.fori_loop(low, high, step, 0)
            dq_ref[span, :] = (acc[...] * HEAD_SCALE).T.astype(BF)
        for j, ref in enumerate((db_ref, dw_ref, da_ref)):
            part = slice(j * tokens, (j + 1) * tokens)
            ref[0] = dk[part, :].astype(ref.dtype)
            ref[1] = dv[part, :].astype(ref.dtype)

    pair = (2, tokens, width)
    return run(
        kernel,
        [bounds, t_index],
        [meta, queries, *windows, mixed_t, totals, *grads],
        [((tokens, width), BF), (pair, BF), (pair, F32), (pair, BF)],
        [
            pltpu.VMEM((tokens, width), BF),
            pltpu.VMEM((3 * tokens, width), BF),
            pltpu.VMEM((3 * tokens, width), BF),
            pltpu.VMEM((width, 3 * tokens), BF),
            pltpu.VMEM((3 * tokens, width), F32),
            pltpu.VMEM((3 * tokens, width), F32),
            pltpu.VMEM((width, block), F32),
        ],
        "attend_back",
        10 * tokens * 3 * tokens * width * 4,
    )


def project(pieces, weights, local, lines, t_index):
    count = len(pieces)
    rows, depth = pieces[0].shape[0], weights.shape[1]
    tokens, width = rows * count, weights.shape[2]
    outputs = weights.shape[0]

    def kernel(t_ref, w_ref, local_ref, *rest):
        x_ref = rest[count]
        place_rows(x_ref, rest[:count], t_ref[0])
        x = x_ref[...]
        done = []
        for k, line in enumerate(lines):
            value = dot(x, w_ref[k], (1, 0))
            if line is not None:
                value = value + local_ref[0, line : line + 1, :]
            done.append(value.astype(BF))
        if outputs == 3:
            rest[count + 2][...] = done[0]
        rest[count + 1][0] = done[-2]
        rest[count + 1][1] = done[-1]

    outs = [((tokens, depth), BF), ((2, tokens, width), BF)]
    if outputs == 3:
        outs.append(((tokens, width), BF))
    return run(
        kernel, [t_index], [weights, local, *pieces], outs, [], "project",
        2 * tokens * depth * width * outputs,
    )


def project_rows(low, weight, local, line):
    count, depth, width = weight.shape

    def kernel(x_ref, w_ref, local_ref, *outs):
        for mask in range(count):
            outs[mask][...] = (
                dot(x_ref[...], w_ref[mask], (1, 0)) + local_ref[mask, line : line + 1, :]
            ).astype(BF)

    return run(
        kernel, [], [low, weight, local], [((low.shape[0], width), BF)] * count, [],
        "project_rows", 2 * low.shape[0] * depth * width * count,
    )


def normed(total, gain, shift):
    center = total - jnp.mean(total, -1, keepdims=True)
    scale = lax.rsqrt(jnp.mean(center * center, -1, keepdims=True) + 1e-05)
    return center * scale * gain + shift


def out_norm(mixed, weight, residual, vectors, line):
    count, depth, width = weight.shape
    shape = residual.shape

    def kernel(w_ref, r_ref, v_ref, *rest):
        total = r_ref[...].astype(F32) + v_ref[line : line + 1, :]
        for mask in range(count):
            total = total + dot(rest[mask][...], w_ref[mask], (1, 1))
        sum_ref, out_ref, low_ref = rest[count:]
        sum_ref[...] = total
        out = normed(total, v_ref[line + 1 : line + 2, :], v_ref[line + 2 : line + 3, :])
        out_ref[...] = out
        low_ref[...] = out.astype(BF)

    return run(
        kernel, [], [weight, residual, vectors, *mixed], [(shape, F32), (shape, F32), (shape, BF)],
        [], "out_norm", 2 * shape[0] * depth * width * count,
    )


def add_norm(terms, vectors, line):
    shape = terms[0].shape

    def kernel(v_ref, *rest):
        total = v_ref[line : line + 1, :]
        for ref in rest[: len(terms)]:
            total = total + ref[...].astype(F32)
        sum_ref, low_ref = rest[len(terms) :]
        sum_ref[...] = total
        out = normed(total, v_ref[line + 1 : line + 2, :], v_ref[line + 2 : line + 3, :])
        low_ref[...] = out.astype(BF)

    return run(
        kernel, [], [vectors, *terms], [(shape, F32), (shape, BF)], [], "add_norm", 1e6
    )


def ffn_blocks(views, rows, depth, hidden):
    step = views[0][0].shape[2]
    row = pl.BlockSpec((rows, depth), lambda j: (0, 0))

    def weight(first):
        return pl.BlockSpec((1, depth, step), lambda j: (first + j, 0, 0))

    tall = pl.BlockSpec((len(views), 2 * rows, step), lambda j: (0, 0, j))
    line = pl.BlockSpec((len(views), 1, step), lambda j: (0, 0, j))
    specs, arrays = [], []
    for up, up_first, down, down_first in views:
        specs += [weight(up_first), weight(down_first)]
        arrays += [up, down]
    return step, row, tall, line, specs, arrays


def ffn_up_down(own, other, views, first):
    rows, depth = own.shape
    hidden = first.shape[2]
    count = len(views)
    step, row, tall, line, specs, arrays = ffn_blocks(views, rows, depth, hidden)

    def kernel(own_ref, other_ref, b_ref, *rest):
        weights, (act_ref, slope_ref, keep_ref, send_ref, pair, acc) = rest[:-6], rest[-6:]
        j = pl.program_id(0)

        @pl.when(j == 0)
        def _():
            pair[:rows, :] = own_ref[...]
            pair[rows:, :] = other_ref[...]

        total = None
        for v in range(count):
            u = dot(pair[...], weights[2 * v][0], (1, 0)) + b_ref[v]
            phi = 0.5 * (1.0 + lax.erf(u * 0.7071067811865476))
            act = (u * phi).astype(BF)
            act_ref[v] = act
            slope_ref[v] = (phi + u * 0.3989422804014327 * jnp.exp(-0.5 * u * u)).astype(BF)
            term = dot(act, weights[2 * v + 1][0], (1, 1))
            total = term if total is None else total + term

        @pl.when(j == 0)
        def _():
            acc[...] = total

        @pl.when(j > 0)
        def _():
            acc[...] += total

        @pl.when(j == hidden // step - 1)
        def _():
            keep_ref[...] = acc[:rows, :]
            send_ref[...] = acc[rows:, :].astype(BF)

    wide = (count, 2 * rows, hidden)
    return run(
        kernel, [], [own, other, first, *arrays],
        [(wide, BF), (wide, BF), ((rows, depth), F32), ((rows, depth), BF)],
        [pltpu.VMEM((2 * rows, depth), BF), pltpu.VMEM((2 * rows, depth), F32)],
        "ffn_up_down", 8 * rows * depth * hidden * count, (hidden // step,),
        [row, row, line] + specs, [tall, tall, row, row],
    )


def ffn_down_up(own, other, views, slope):
    rows, depth = own.shape
    hidden = slope.shape[2]
    count = len(views)
    step, row, tall, line, specs, arrays = ffn_blocks(views, rows, depth, hidden)

    def kernel(own_ref, other_ref, slope_ref, *rest):
        weights, (du_ref, sum_ref, keep_ref, send_ref, pair, acc) = rest[:-6], rest[-6:]
        j = pl.program_id(0)

        @pl.when(j == 0)
        def _():
            pair[:rows, :] = own_ref[...]
            pair[rows:, :] = other_ref[...]

        total = None
        for v in range(count):
            du = (dot(pair[...], weights[2 * v + 1][0], (1, 0)) * slope_ref[v].astype(F32)).astype(BF)
            du_ref[v] = du
            sum_ref[v] = jnp.sum(du.astype(F32), 0, keepdims=True)
            term = dot(du, weights[2 * v][0], (1, 1))
            total = term if total is None else total + term

        @pl.when(j == 0)
        def _():
            acc[...] = total

        @pl.when(j > 0)
        def _():
            acc[...] += total

        @pl.when(j == hidden // step - 1)
        def _():
            keep_ref[...] = acc[:rows, :]
            send_ref[...] = acc[rows:, :].astype(BF)

    return run(
        kernel, [], [own, other, slope, *arrays],
        [
            ((count, 2 * rows, hidden), BF), ((count, 1, hidden), F32),
            ((rows, depth), F32), ((rows, depth), BF),
        ],
        [pltpu.VMEM((2 * rows, depth), BF), pltpu.VMEM((2 * rows, depth), F32)],
        "ffn_down_up", 8 * rows * depth * hidden * count, (hidden // step,),
        [row, row, tall] + specs, [tall, line, row, row],
    )


def split_blocks(full, keep_ref, send_ref, at, core, blocks, size):
    for p in range(blocks // 2):
        mine = multiple((2 * p + core) * size, size)
        theirs = multiple((2 * p + 1 - core) * size, size)
        keep_ref[at + (p,)] = full[pl.ds(mine, size), :]
        send_ref[at + (p,)] = full[pl.ds(theirs, size), :]


def ffn_weight_grads(x_own, x_other, e_own, e_other, du, act, core, blocks):
    rows, depth = x_own.shape
    count, _, hidden = du.shape
    step = min(512, hidden)
    per = hidden // step
    size = depth // blocks
    split = core is not None

    def kernel(core_ref, x_ref, xo_ref, e_ref, eo_ref, du_ref, act_ref, *rest):
        outs, (xs, es, full) = rest[:-3], rest[-3:]

        @pl.when(pl.program_id(0) == 0)
        def _():
            xs[:rows, :] = x_ref[...]
            xs[rows:, :] = xo_ref[...]
            es[:rows, :] = e_ref[...]
            es[rows:, :] = eo_ref[...]

        up = dot(xs[...], du_ref[0], (0, 0)).astype(BF)
        down = dot(es[...], act_ref[0], (0, 0)).astype(BF)
        if split:
            full[...] = up
            split_blocks(full, outs[0], outs[1], (), core_ref[0], blocks, size)
            full[...] = down
            split_blocks(full, outs[2], outs[3], (), core_ref[0], blocks, size)
        else:
            outs[0][0] = up
            outs[0][1] = down

    row = pl.BlockSpec((rows, depth), lambda j: (0, 0))
    tall = pl.BlockSpec((1, 2 * rows, step), lambda j: (j // per, 0, j % per))
    if split:
        part = pl.BlockSpec((blocks // 2, size, step), lambda j: (0, 0, j))
        outs, out_blocks = [((blocks // 2, size, hidden * count), BF)] * 4, [part] * 4
    else:
        outs = [((2 * count, depth, hidden), BF)]
        out_blocks = [pl.BlockSpec((2, depth, step), lambda j: (j // per, 0, j % per))]
    return run(
        kernel, [core if split else jnp.zeros((1,), jnp.int32)],
        [x_own, x_other, e_own, e_other, du, act], outs,
        [
            pltpu.VMEM((2 * rows, depth), BF),
            pltpu.VMEM((2 * rows, depth), BF),
            pltpu.VMEM((depth, step), BF),
        ],
        "ffn_weight_grads", 8 * rows * depth * hidden * count, (count * per,),
        [row, row, row, row, tall, tall], out_blocks,
    )


def weight_grads(groups, core, blocks):
    arrays, places = [], []
    for group in groups:
        for pair in group:
            spot = []
            for array in pair:
                known = [i for i, a in enumerate(arrays) if a is array]
                if not known:
                    arrays.append(array)
                    known = [len(arrays) - 1]
                spot.append(known[0])
            places.append(spot)
    depth, width = groups[0][0][0].shape[1], groups[0][0][1].shape[1]
    size = depth // blocks
    count = len(arrays)

    def kernel(core_ref, *rest):
        outs, full = rest[count:-1], rest[-1]
        number = 0
        for g, group in enumerate(groups):
            for j in range(len(group)):
                left, right = places[number]
                value = dot(rest[left][...], rest[right][...], (0, 0)).astype(BF)
                if core is None:
                    outs[g][j] = value
                else:
                    full[...] = value
                    split_blocks(
                        full, outs[2 * g], outs[2 * g + 1], (j,), core_ref[0], blocks, size
                    )
                number += 1

    outs = []
    for group in groups:
        if core is None:
            outs.append(((len(group), depth, width), BF))
        else:
            outs += [((len(group), blocks // 2, size, width), BF)] * 2
    flops = sum(2 * left.shape[0] * depth * width for group in groups for left, right in group)
    return run(
        kernel, [jnp.zeros((1,), jnp.int32) if core is None else core], arrays, outs,
        [pltpu.VMEM((depth, width), BF)], "weight_grads", flops,
    )


def norm_grad_body(terms, summed, gain, grad_ref, low_ref, sums_ref):
    grad = terms[0][...].astype(F32)
    for ref in terms[1:]:
        grad = grad + ref[...].astype(F32)
    total = summed[...]
    center = total - jnp.mean(total, -1, keepdims=True)
    scale = lax.rsqrt(jnp.mean(center * center, -1, keepdims=True) + 1e-05)
    unit = center * scale
    inner = grad * gain
    out = scale * (
        inner - jnp.mean(inner, -1, keepdims=True) - unit * jnp.mean(inner * unit, -1, keepdims=True)
    )
    low = out.astype(BF)
    grad_ref[...] = out
    low_ref[...] = low
    sums_ref[0:1, :] = jnp.sum(low.astype(F32), 0, keepdims=True)
    sums_ref[1:2, :] = jnp.sum(grad * unit, 0, keepdims=True)
    sums_ref[2:3, :] = jnp.sum(grad, 0, keepdims=True)
    return low


def norm_grad(terms, summed, gain, line):
    shape = summed.shape

    def kernel(sum_ref, gain_ref, *rest):
        norm_grad_body(rest[: len(terms)], sum_ref, gain_ref[line : line + 1, :], *rest[len(terms) :])

    return run(
        kernel, [], [summed, gain, *terms], [(shape, F32), (shape, BF), ((3, shape[1]), F32)], [],
        "norm_grad", 1e6,
    )


def norm_out_grad(terms, summed, gain, line, weight):
    shape = summed.shape
    count, depth, width = weight.shape

    def kernel(sum_ref, gain_ref, w_ref, *rest):
        outs = rest[len(terms) :]
        low = norm_grad_body(rest[: len(terms)], sum_ref, gain_ref[line : line + 1, :], *outs[:3])
        for mask in range(count):
            outs[3 + mask][...] = dot(low, w_ref[mask], (1, 0)).astype(BF)

    return run(
        kernel, [], [summed, gain, weight, *terms],
        [(shape, F32), (shape, BF), ((3, shape[1]), F32)] + [((shape[0], width), BF)] * count, [],
        "norm_out_grad", 2 * shape[0] * depth * width * count,
    )


def input_grads(dq, own, below, above, weights, t_index, count):
    tokens, width = dq.shape
    rows, depth = tokens // count, weights.shape[1]
    ahead = weights.shape[0] - 2

    def kernel(t_ref, w_ref, dq_ref, own_ref, below_ref, above_ref, dk_ref, dv_ref, sums_ref, *rest):
        full = rest[count]
        for j, ref in enumerate((dk_ref, dv_ref)):
            ref[...] = (
                own_ref[j] + below_ref[j].astype(F32) + above_ref[j].astype(F32)
            ).astype(BF)
        sums_ref[0:1, :] = jnp.sum(dq_ref[...].astype(F32), 0, keepdims=True)
        sums_ref[1:2, :] = jnp.sum(dv_ref[...].astype(F32), 0, keepdims=True)
        total = dot(dk_ref[...], w_ref[ahead], (1, 1)) + dot(dv_ref[...], w_ref[ahead + 1], (1, 1))
        if ahead:
            total = total + dot(dq_ref[...], w_ref[0], (1, 1))
        full[...] = total
        for mask in range(count):
            part = full[pl.ds(multiple((t_ref[0] ^ mask) * rows, rows), rows), :]
            rest[mask][...] = part.astype(rest[mask].dtype)

    return run(
        kernel, [t_index], [weights, dq, own, below, above],
        [((tokens, width), BF)] * 2 + [((2, width), F32), ((rows, depth), F32)]
        + [((rows, depth), BF)] * (count - 1),
        [pltpu.VMEM((tokens, depth), F32)], "input_grads",
        2 * tokens * width * depth * weights.shape[0],
    )


def asked_grad(pieces, weight):
    count, depth, width = weight.shape
    rows = pieces[0].shape[0]

    def kernel(w_ref, *rest):
        total = dot(rest[0][...], w_ref[0], (1, 1))
        for mask in range(1, count):
            total = total + dot(rest[mask][...], w_ref[mask], (1, 1))
        rest[count][...] = total

    return run(
        kernel, [], [weight, *pieces], [((rows, depth), F32)], [], "asked_grad",
        2 * rows * depth * width * count,
    )[0]


def by_mask(values, t_index, count):
    tokens, width = values.shape
    rows = tokens // count

    def kernel(t_ref, x_ref, *outs):
        for mask in range(count):
            outs[mask][...] = x_ref[pl.ds(multiple((t_ref[0] ^ mask) * rows, rows), rows), :]

    return run(kernel, [t_index], [values], [((rows, width), BF)] * count, [], "by_mask", 1000)


def in_order(pieces, t_index):
    count = len(pieces)
    rows, width = pieces[0].shape

    def kernel(t_ref, *refs):
        place_rows(refs[count], refs[:count], t_ref[0])

    return run(
        kernel, [t_index], pieces, [((rows * count, width), BF)], [], "in_order", 1000
    )[0]


LINES = 32
ENC_ATT, ENC_FFN, SELF_ATT, CROSS_ATT, DEC_FFN, ENC_FIRST, DEC_FIRST = 0, 5, 8, 13, 18, 21, 25


def pack_small(arrays, width):
    def kernel(*refs):
        lines = []
        for ref in refs[:-1]:
            value = ref[...].astype(F32)
            if value.shape[1] > width:
                value = jnp.concatenate(
                    [value[:, i : i + width] for i in range(0, value.shape[1], width)], 0
                )
            lines.append(value)
        used = sum(value.shape[0] for value in lines)
        lines.append(jnp.zeros((LINES - used, width), F32))
        whole = jnp.concatenate(lines, 0)
        refs[-1][...] = jnp.concatenate([whole[: LINES // 2], whole[LINES // 2 :]], 1).astype(BF)

    blocks = [pl.BlockSpec(array.shape, lambda i: (0, 0)) for array in arrays]
    shape = (LINES // 2, 2 * width)
    return run(
        kernel, [], arrays, [(shape, BF)], [], "pack_small", 0, (1,), blocks,
        [pl.BlockSpec(shape, lambda i: (0, 0))],
    )[0]


def unpack_small(parts, t_index, count, features, wide_masks):
    peers, lines, width = parts.shape[0], LINES, parts.shape[2] // 2
    share_ = peers // count
    quarter = 4
    hidden = share_ * quarter * width

    def kernel(t_ref, x_ref, table, local, enc_ref, dec_ref):
        for f in range(peers):
            value = x_ref[f].astype(F32)
            span = slice(f * width, (f + 1) * width)
            table[: lines // 2, span] = value[:, :width]
            table[lines // 2 :, span] = value[:, width:]
        for mask in range(count):
            local[mask] = table[:, pl.ds(multiple((t_ref[0] ^ mask) * features, 128), features)]
        for ref, first in ((enc_ref, ENC_FIRST), (dec_ref, DEC_FIRST)):
            for v, mask in enumerate(wide_masks):
                for f in range(share_):
                    for q in range(quarter):
                        at = (f * quarter + q) * width
                        ref[v, :, at : at + width] = local[
                            mask, first + q : first + q + 1, f * width : (f + 1) * width
                        ]

    first = ((len(wide_masks), 1, hidden), F32)
    return run(
        kernel, [t_index], [parts],
        [((lines, peers * width), F32), ((count, lines, features), F32), first, first], [],
        "unpack_small", 0,
    )


def pack_grads(sums, columns, firsts, t_index, peers, wide_masks):
    depth = sums[0].shape[1]
    width = depth // peers
    features = columns[0].shape[1]
    share_ = features // width
    quarter = 4
    arrays = list(sums) + list(columns) + list(firsts)

    def kernel(t_ref, *refs):
        out, table = refs[-2:]
        table[...] = jnp.zeros_like(table)
        own = pl.ds(multiple(t_ref[0] * features, 128), features)
        att = (ENC_ATT, SELF_ATT, CROSS_ATT)
        for first, s_ref, c_ref in zip(att, refs[:3], refs[5:8]):
            table[first + 2 : first + 5, :] = s_ref[...]
            table[first : first + 2, own] = c_ref[...]
        for first, s_ref in zip((ENC_FFN, DEC_FFN), refs[3:5]):
            table[first : first + 3, :] = s_ref[...]
        for first, f_ref in zip((ENC_FIRST, DEC_FIRST), refs[8:10]):
            for v, mask in enumerate(wide_masks):
                strip = []
                for q in range(quarter):
                    pieces = []
                    for f in range(share_):
                        at = (f * quarter + q) * width
                        pieces.append(f_ref[v, :, at : at + width])
                    strip.append(jnp.concatenate(pieces, 1))
                there = pl.ds(multiple((t_ref[0] ^ mask) * features, 128), features)
                table[first : first + quarter, there] = jnp.concatenate(strip, 0)
        for f in range(peers):
            out[f] = table[:, f * width : (f + 1) * width]

    return run(
        kernel, [t_index], arrays, [((peers, LINES, width), F32)],
        [pltpu.VMEM((LINES, depth), F32)], "pack_grads", 0,
    )[0]


def unpack_grads(terms, shapes):
    def kernel(*refs):
        value = refs[0][...]
        for ref in refs[1 : len(terms)]:
            value = value + ref[...]
        width = value.shape[1]
        line = 0
        for ref in refs[len(terms) :]:
            rows, columns = ref.shape
            for r in range(rows):
                for at in range(0, columns, width):
                    ref[r : r + 1, at : at + width] = value[line : line + 1, :]
                    line += 1

    return run(kernel, [], terms, [(shape, F32) for shape in shapes], [], "unpack_grads", 0)


def token_spans(seq_lens, pic_start, pic_len, base, tokens, block):
    count, pictures = pic_start.shape
    blocks = tokens // block

    def kernel(lens, starts, extents, base_ref, both, text, both_bounds, text_bounds):
        places = lax.broadcasted_iota(jnp.int32, (1, tokens), 1) + tokens
        zero = jnp.zeros((1, tokens), jnp.int32)
        begin, end = zero, zero
        low, high = [zero] * pictures, [zero] * pictures
        edges = [
            [jnp.int32(3 * tokens), jnp.int32(0), jnp.int32(tokens + (i + 1) * block)]
            for i in range(blocks)
        ]
        start = tokens - base_ref[0]
        for s in range(count):
            stop = start + lens[s]
            inside = (places >= start) & (places < stop)
            begin = jnp.where(inside, start, begin)
            end = jnp.where(inside, stop, end)
            spans = []
            for k in range(pictures):
                first = start + starts[s, k]
                last = jnp.minimum(first + extents[s, k], stop)
                member = inside & (places >= first) & (places < last)
                low[k] = jnp.where(member, first, low[k])
                high[k] = jnp.where(member, last, high[k])
                spans.append((first, last))
            for i in range(blocks):
                from_, to = tokens + i * block, tokens + (i + 1) * block
                meets = (start < to) & (stop > from_)
                edge = edges[i]
                edge[0] = jnp.where(meets, jnp.minimum(edge[0], start), edge[0])
                edge[1] = jnp.where(meets, jnp.maximum(edge[1], stop), edge[1])
                for first, last in spans:
                    touches = (first < to) & (last > from_)
                    edge[2] = jnp.where(touches, jnp.maximum(edge[2], last), edge[2])
            start = stop
        both[...] = jnp.concatenate([begin, end] + [zero] * 6, 0)
        seen = [begin, places + 1]
        for k in range(pictures):
            seen += [low[k], high[k]]
        text[...] = jnp.concatenate(seen + [zero] * (8 - len(seen)), 0)
        for i in range(blocks):
            first = lax.div(edges[i][0], jnp.int32(block))
            both_bounds[2 * i] = first
            both_bounds[2 * i + 1] = lax.div(edges[i][1] + (block - 1), jnp.int32(block))
            text_bounds[2 * i] = first
            text_bounds[2 * i + 1] = lax.div(edges[i][2] + (block - 1), jnp.int32(block))

    whole = pl.BlockSpec(memory_space=pltpu.VMEM)
    scalars = pl.BlockSpec(memory_space=pltpu.SMEM)
    return run(
        kernel, [seq_lens, pic_start, pic_len, base], [],
        [((8, tokens), jnp.int32)] * 2 + [((2 * blocks,), jnp.int32)] * 2, [], "token_spans", 0,
        None, None, [whole, whole, scalars, scalars],
    )


def per_device(
    enc_in,
    dec_in,
    enc_cot,
    dec_cot,
    seq_lens,
    pic_start,
    pic_len,
    enc_attn_w,
    enc_attn_bias,
    enc_attn_norm,
    enc_ffn_w,
    enc_ffn_b1,
    enc_ffn_vec,
    self_attn_w,
    self_attn_bias,
    self_attn_norm,
    cross_attn_w,
    cross_attn_bias,
    cross_attn_norm,
    dec_ffn_w,
    dec_ffn_b1,
    dec_ffn_vec,
):
    rows = enc_in.shape[0]
    tensor_size = lax.axis_size("tensor")
    fsdp_size = lax.axis_size("fsdp")
    t_index = lax.axis_index("tensor")
    f_index = lax.axis_index("fsdp")
    t_ref = t_index[None].astype(jnp.int32)
    core = (f_index % 2)[None].astype(jnp.int32)
    tokens = rows * tensor_size
    features = enc_attn_w.shape[2]
    hidden = enc_ffn_w.shape[2]
    t_down = bits_of("tensor")[::-1]
    t_up = bits_of("tensor")
    wide_down = t_down[:-1]
    wide_up = t_up[1:]
    t_masks = range(tensor_size)
    wide_masks = range(0, tensor_size, 2)
    wide_count = len(wide_masks)

    small = [
        enc_attn_bias, enc_attn_norm, enc_ffn_vec, self_attn_bias, self_attn_norm,
        cross_attn_bias, cross_attn_norm, dec_ffn_vec, enc_ffn_b1, dec_ffn_b1,
    ]
    block = min(256, tokens)
    base = (f_index * tokens)[None].astype(jnp.int32)
    spans = token_spans(seq_lens, pic_start, pic_len, base, tokens, block)
    both = (spans[0], spans[2], 1)
    text = (spans[1], spans[3], 1 + pic_start.shape[1])

    first_order, second_order = plane_orders()

    def later(value, ready):
        return lax.optimization_barrier((value, ready))[0]

    class Pair:
        def __init__(self, halves, splits):
            self.plans = [
                Gather(half[None], order, split)
                for half, order, split in zip(halves, (first_order, second_order), splits)
            ]

        def hop(self, *gate):
            if self.plans[0].came is not None:
                came_ = join([plan.came for plan in self.plans], *gate)
                for plan, value in zip(self.plans, came_):
                    plan.came = value
                gate = ()
            return [plan.hop(*gate) for plan in self.plans]

        def result(self):
            return [plan.result() for plan in self.plans]

    slices = hidden // features

    def ffn_slices(shard):
        cut = shard.reshape(2, rows, slices, features)
        return jnp.moveaxis(cut, 2, 1).reshape(2 * slices, rows, features)

    def ups(shards):
        return [ffn_slices(shard)[:slices] for shard in shards]

    def downs(shards):
        return [ffn_slices(shard)[slices:] for shard in shards]

    def ffn_views(*arrays):
        views = []
        for up, down in arrays:
            for at in range(0, up.shape[0], slices):
                views.append((up, at, down, at))
        return views

    far = (wide_count - 1) * slices

    def exchange(pieces_, *hold):
        held = dict(enumerate(pieces_))
        for bit in t_up:
            moved = [mask for mask in t_masks if mask & bit]
            came_ = swap(jnp.stack([held[mask] for mask in moved]), "tensor", bit)
            if bit == 1:
                came_ = join(came_, *hold)
            for at, mask in enumerate(moved):
                held[mask] = came_[at]
        return [held[mask] for mask in t_masks]

    def doubled(value):
        held = {0: value}
        for bit in t_down:
            known = sorted(held)
            came_ = swap(jnp.stack([held[mask] for mask in known]), "tensor", bit)
            gate = yield came_
            came_ = join(came_, *(gate or ()))
            for at, mask in enumerate(known):
                held[mask | bit] = came_[at]
        yield [held[mask] for mask in t_masks]

    peers = fsdp_size
    up_pairs = [(i, i + 1) for i in range(peers - 1)]
    down_pairs = [(j, i) for i, j in up_pairs]

    def halo(pair):
        before = lax.ppermute(pair, "fsdp", up_pairs)
        after = lax.ppermute(pair, "fsdp", down_pairs)
        return before, pair, after

    def attend_fg(queries, window, mode):
        return attend(queries, window, mode[0], mode[1], t_ref, tensor_size, mode[2])

    def attend_back_fg(queries, window, grads, mixed_t, totals, mode):
        return attend_back(
            queries, window, grads, mixed_t, totals, mode[0], mode[1], t_ref, tensor_size, mode[2]
        )

    class Folds:
        def __init__(self, parts_, at):
            self.folds = [
                Fold(parts_[2 * k], parts_[2 * k + 1], order[:-1], at)
                for k, order in enumerate((first_order, second_order))
            ]

        def hop(self, *gate):
            return [fold.hop(*gate) for fold in self.folds]

        def next(self, *gate):
            return halve_all(self.folds, *gate)

        def result(self, *gate):
            return [fold.result(*gate) for fold in self.folds]

    class SmallSum:
        def __init__(self, value):
            self.value, self.came = value, None
            self.bits = [("fsdp", bit) for bit in bits_of("fsdp")[::-1]]
            self.bits += [("tensor", bit) for bit in t_up]

        def hop(self):
            if self.came is not None:
                self.value = self.value + self.came
            axis, bit = self.bits.pop(0)
            sent = self.value
            if axis == "fsdp":
                half = self.value.shape[0] // 2
                mine = (f_index // bit) % 2
                sent = lax.dynamic_slice_in_dim(self.value, (1 - mine) * half, half, 0)
                self.value = lax.dynamic_slice_in_dim(self.value, mine * half, half, 0)
            self.came = swap(sent, axis, bit)

        def result(self):
            while self.bits:
                self.hop()
            return [self.value[0], self.came[0]]

    class WideShare:
        def __init__(self, halves):
            self.held = {
                mask: halves[:, :, j * hidden : (j + 1) * hidden]
                for j, mask in enumerate(wide_masks)
            }
            self.bits = list(wide_up)

        def hop(self):
            bit = self.bits.pop(0)
            new = []
            for mask in sorted(self.held):
                if mask not in self.held or mask & (2 * bit - 1):
                    continue
                came_ = swap(self.held.pop(mask | bit).astype(BF), "tensor", bit)
                self.held[mask] = self.held[mask] + came_.astype(F32)
                new.append(came_)
            self.came = new
            return new

        def result(self):
            while self.bits:
                self.hop()
            return self.held[0]

    pending = [[], [], [], []]

    def due(*values, lag=2):
        pending[lag - 1].extend(values)

    def fg(value):
        waits = pending.pop(0)
        pending.append([])
        return join(value, *waits)

    packed = pack_small(small, enc_attn_bias.shape[1])
    depth = enc_in.shape[1]
    enc_pieces = reach(
        jnp.concatenate([enc_in, enc_attn_w[3]], 1), "tensor", t_masks[:0:-1]
    )
    first_shard = jnp.concatenate([enc_attn_w[:3].reshape(-1, features), packed])
    qkv_plan = Gather(first_shard[None], first_order, [(3, rows), (1, packed.shape[0])])
    qkv_plan.hop()
    enc_qkv, parts = qkv_plan.result()
    table, local, enc_first, dec_first = unpack_small(
        parts.reshape(fsdp_size, -1, features), t_ref, tensor_size, features, wide_masks
    )
    plan1 = Pair(
        (
            jnp.concatenate([self_attn_w[:3]] + ups([enc_ffn_w])),
            jnp.concatenate(
                [piece[None, :, depth:] for piece in enc_pieces] + downs([enc_ffn_w])
            ),
        ),
        ([3, slices], [tensor_size, slices]),
    )
    due(plan1.hop())
    dec_steps = doubled(
        join(
            jnp.concatenate([dec_in, self_attn_w[3], cross_attn_w[3], cross_attn_w[0]], 1),
            *enc_pieces[1:],
        )
    )
    due(next(dec_steps))

    flat_e, pair_e, query_e = project(
        fg(enc_pieces), enc_qkv, local, (ENC_ATT, None, ENC_ATT + 1), t_ref
    )
    window_e = halo(pair_e)
    r1 = (window_e[0], window_e[2])
    plan1.hop(*r1)
    dec_pieces = dec_steps.send(r1)

    mixed_e, mixed_t_e, totals_e = attend_fg(fg(query_e), window_e, both)
    mixed_e = exchange(mixed_e, dec_pieces)
    r2 = tuple(mixed_e[1:])
    plan1.hop(*r2)
    (self_qkv, own_up), (enc_out_w, own_down) = plan1.result()
    enc_wide = Spread(join(enc_ffn_w, *r2), "tensor", wide_down)
    enc_wide.hop()
    dec_own = join(dec_ffn_w, *r2)
    plan0 = Pair(
        (jnp.concatenate(ups([dec_own])), jnp.concatenate(downs([dec_own]))),
        ([slices], [slices]),
    )
    due(plan0.hop())
    for step in range(len(t_down) - 1):
        dec_pieces = dec_steps.send(r2)

    summed_e, hid, hid_low = out_norm(
        fg(mixed_e), enc_out_w, enc_in, table, ENC_ATT + 2
    )
    hid_other = swap(hid_low, "tensor", 1)
    r3 = (hid_other,)
    second_hop = plan0.hop(hid_low)
    flat_s, pair_s, query_s = project(
        fg(join(dec_pieces, hid_low)), self_qkv, local, (SELF_ATT, None, SELF_ATT + 1), t_ref
    )
    spare = [join(piece, *r3)[:, depth:] for piece in dec_pieces]

    def spare_part(which):
        return [piece[None, :, which * features : (which + 1) * features] for piece in spare]

    others = enc_wide.result(*r3)[1:]
    plan2 = Pair(
        (
            jnp.concatenate(ups(others) + spare_part(0) + [cross_attn_w[1:3]]),
            jnp.concatenate(downs(others) + spare_part(1) + spare_part(2)),
        ),
        ([far, tensor_size, 2], [far, tensor_size, tensor_size]),
    )
    plan2.hop()
    window_s = halo(pair_s)
    r4 = (window_s[0], window_s[2])
    plan0.hop(*r4)
    mixed_s, mixed_t_s, totals_s = attend_fg(fg(join(query_s, second_hop)), window_s, text)
    mixed_s = exchange(mixed_s)
    r5 = tuple(mixed_s[1:])
    plan2.hop(*r5)
    dec_wide = Spread(join(dec_ffn_w, *r5), "tensor", wide_down)
    dec_wide.hop()
    plan2.hop(*r5)
    (far_up, self_out_w, cross_kv), (far_down, cross_out_w, cross_query) = plan2.result()
    enc_views = ffn_views((own_up, own_down), (far_up, far_down))
    active_e, slope_e, keep, send = ffn_up_down(hid_low, hid_other, enc_views, enc_first)
    came = swap(send, "tensor", 1)
    r7 = (came,)
    shards = dec_wide.result(send)[1:]
    plan4 = Pair(
        (jnp.concatenate(ups(shards)), jnp.concatenate(downs(shards))), ([far], [far])
    )
    plan4.hop()

    summed_s, decoded, decoded_low = out_norm(
        join(mixed_s, send), self_out_w, dec_in, table, SELF_ATT + 2
    )
    ffn_summed_e, encoded = add_norm(
        [hid, join(keep, decoded_low), came], table, ENC_FFN
    )
    enc_rows = spread(encoded, "tensor", t_down)
    plan4.hop(encoded)
    asked = exchange(
        project_rows(join(decoded_low, *enc_rows[1:]), cross_query, local, CROSS_ATT)
    )
    query_c = in_order(asked, t_ref)

    flat_c, pair_c = project(
        enc_rows, cross_kv, local, (None, CROSS_ATT + 1), t_ref
    )
    window_c = halo(pair_c)
    r9 = (window_c[0], window_c[2])
    plan4.hop(*r9)
    mixed_c, mixed_t_c, totals_c = attend_fg(query_c, window_c, both)
    mixed_c = exchange(mixed_c)
    dec_views = ffn_views(
        [array for (array,) in plan0.result()], [array for (array,) in plan4.result()]
    )
    summed_c, crossed, crossed_low = out_norm(
        mixed_c, cross_out_w, decoded, table, CROSS_ATT + 2
    )
    crossed_other = swap(crossed_low, "tensor", 1)
    active_d, slope_d, keep, send = ffn_up_down(
        crossed_low, crossed_other, dec_views, dec_first
    )
    came = swap(send, "tensor", 1)
    ffn_summed_d, final = add_norm([crossed, keep, came], table, DEC_FFN)

    grad_sum_d, low_d, dec_sums = norm_grad([dec_cot], ffn_summed_d, table, DEC_FFN + 1)
    other_d = swap(low_d, "tensor", 1)
    du_d, dec_first_sum, keep, send = ffn_down_up(low_d, other_d, dec_views, slope_d)
    came = swap(send, "tensor", 1)
    dec_grads = ffn_weight_grads(
        crossed_low, crossed_other, low_d, other_d, join(du_d, send), active_d, core, fsdp_size
    )
    dec_fold = Folds(dec_grads, 0)
    due(dec_fold.hop())

    grad_sum_c, low_c, sums_c, *given = norm_out_grad(
        [fg(grad_sum_d), join(keep, dec_grads), came], summed_c, table, CROSS_ATT + 3, cross_out_w
    )
    given = exchange(given)
    b2 = tuple(given[1:])
    due(dec_fold.next(*b2))
    dq_c, below, own, above = attend_back_fg(
        query_c, window_c, fg(given), mixed_t_c, totals_c, both
    )
    below = lax.ppermute(below, "fsdp", down_pairs)
    above = lax.ppermute(above, "fsdp", up_pairs)
    asked_c = exchange(by_mask(dq_c, t_ref, tensor_size))
    b3 = (below, above)
    due(dec_fold.next(*b3))
    dk_c, dv_c, columns_c, *blocks_c = input_grads(
        dq_c, fg(own), below, above, cross_kv, t_ref, tensor_size
    )
    source = Share(blocks_c, "tensor", t_up)
    due(source.hop())
    from_asked = asked_grad([join(asked_c[0], dk_c)] + asked_c[1:], cross_query)
    cross_grads = weight_grads(
        [
            [(flat_c, join(dk_c, from_asked)), (flat_c, dv_c)]
            + [(decoded_low, piece) for piece in asked_c],
            [(low_c, piece) for piece in mixed_c],
        ],
        core, fsdp_size,
    )
    cross_fold = Folds(cross_grads, 1)
    due(cross_fold.hop())

    grad_sum_s, low_s, sums_s, *given = norm_out_grad(
        [fg(join(grad_sum_c, cross_grads)), from_asked], summed_s, table, SELF_ATT + 3, self_out_w
    )
    given = exchange(given)
    b6 = tuple(given[1:])
    source.hop(*b6)
    due(cross_fold.next(*b6), lag=3)
    dq_s, below, own, above = attend_back_fg(
        query_s, window_s, fg(given), mixed_t_s, totals_s, text
    )
    below = lax.ppermute(below, "fsdp", down_pairs)
    above = lax.ppermute(above, "fsdp", up_pairs)
    b7 = (below, above)
    due(cross_fold.next(*b7))
    dec_wide_share = WideShare(jnp.stack(dec_fold.result(*b7)))
    due(dec_wide_share.hop())
    grad_sum_f, low_f, enc_sums = norm_grad(
        [fg(join(enc_cot, dq_s))] + source.result(), ffn_summed_e, table, ENC_FFN + 1
    )
    other_f = swap(low_f, "tensor", 1)
    dk_s, dv_s, columns_s, *blocks_s = input_grads(
        dq_s, join(own, low_f), below, above, self_qkv, t_ref, tensor_size
    )
    b8 = dk_s
    target = Share(blocks_s, "tensor", t_up)
    due(target.hop())
    self_parts = weight_grads(
        [
            [(flat_s, join(dq_s, b8)), (flat_s, dk_s), (flat_s, dv_s)]
            + [(low_s, piece) for piece in mixed_s]
        ],
        core, fsdp_size,
    )
    self_fold = Fold(self_parts[0], self_parts[1], first_order[:-1], 1)
    due(self_fold.hop())
    du_e, enc_first_sum, keep, send = ffn_down_up(
        fg(join(low_f, self_parts)), other_f, enc_views, slope_e
    )
    came = swap(send, "tensor", 1)
    b10 = came
    due(target.hop(b10), lag=3)
    due(self_fold.next(b10), lag=3)
    enc_grads = ffn_weight_grads(
        hid_low, hid_other, low_f, other_f, join(du_e, send), active_e, core, fsdp_size
    )
    enc_fold = Folds(enc_grads, 0)
    due(enc_fold.hop())

    grad_sum_e, low_e, sums_e, *given = norm_out_grad(
        [grad_sum_f, fg(join(keep, enc_grads)), came], summed_e, table, ENC_ATT + 3, enc_out_w
    )
    given = exchange(given)
    b11 = tuple(given[1:])
    due(enc_fold.next(*b11))
    due(self_fold.next(*b11))
    dq_e, below, own, above = attend_back_fg(
        query_e, window_e, fg(given), mixed_t_e, totals_e, both
    )
    below = lax.ppermute(below, "fsdp", down_pairs)
    above = lax.ppermute(above, "fsdp", up_pairs)
    b12 = (below, above)
    enc_fold.next(*b12)
    cross_first, cross_outs = cross_fold.result(*b12)
    self_own = self_fold.result(*b12)
    late_share = Share(
        [
            jnp.stack([cross_first[2 + mask], cross_outs[mask], self_own[3 + mask]])
            for mask in t_masks
        ],
        "tensor", t_up,
    )
    dk_e, dv_e, columns_e, *blocks_e = input_grads(
        dq_e, fg(own), below, above, enc_qkv, t_ref, tensor_size
    )
    b13 = dk_e
    enc_share = Share(blocks_e, "tensor", t_up)
    enc_share.hop()
    small_sum = SmallSum(
        pack_grads(
            [sums_e, sums_s, sums_c, enc_sums, dec_sums], [columns_e, columns_s, columns_c],
            [enc_first_sum, dec_first_sum], t_ref, fsdp_size, wide_masks,
        )
    )
    small_sum.hop()
    enc_att = weight_grads(
        [
            [(flat_e, dq_e), (flat_e, join(dk_e, tuple(blocks_e))), (flat_e, dv_e)],
            [(low_e, piece) for piece in mixed_e],
        ],
        core, fsdp_size,
    )
    att_folds = Folds(enc_att, 1)
    att_folds.hop()

    def meet(*items):
        for item, came_ in zip(items, join([item.came for item in items])):
            item.came = came_

    meet(enc_share, small_sum, *att_folds.folds, *enc_fold.folds)
    att_folds.next()
    enc_share.hop()
    small_sum.hop()
    enc_wide_share = WideShare(jnp.stack(enc_fold.result()))
    enc_wide_share.hop()
    meet(small_sum, *att_folds.folds)
    att_folds.next()
    small_sum.hop()
    late_share.hop()
    meet(late_share, small_sum, *att_folds.folds)
    enc_att_own, enc_att_out = att_folds.result()
    out_share = Share([enc_att_out[mask] for mask in t_masks], "tensor", t_up)
    out_share.hop()
    late_share.hop()
    small_sum.hop()
    meet(out_share, late_share, small_sum)
    out_share.hop()
    small_out = unpack_grads(small_sum.result(), [item.shape for item in small])
    enc_grad = jnp.concatenate([enc_att_own, total(out_share.result())[None]])
    dec_ffn_grad = dec_wide_share.result()
    enc_ffn_grad = enc_wide_share.result()
    late = total(late_share.result())
    cross_grad = jnp.concatenate([late[0:1], cross_first[:2], late[1:2]])
    self_grad = jnp.concatenate([self_own[:3], late[2:3]])
    grad_source = total([grad_sum_e] + enc_share.result())
    grad_target = total([grad_sum_s] + target.result())

    (
        enc_bias_g, enc_norm_g, enc_vec_g, self_bias_g, self_norm_g,
        cross_bias_g, cross_norm_g, dec_vec_g, enc_b1_g, dec_b1_g,
    ) = small_out
    return (
        encoded,
        final,
        grad_source,
        grad_target,
        enc_grad,
        enc_bias_g,
        enc_norm_g,
        enc_ffn_grad,
        enc_b1_g,
        enc_vec_g,
        self_grad,
        self_bias_g,
        self_norm_g,
        cross_grad,
        cross_bias_g,
        cross_norm_g,
        dec_ffn_grad,
        dec_b1_g,
        dec_vec_g,
    )


def solution(mesh):
    rows = P(("fsdp", "tensor"), None)
    weight = P(None, "fsdp", "tensor")
    vector = P(None, "fsdp")
    att, ffn = (weight, vector, vector), (weight, vector, vector)
    in_specs = (rows,) * 4 + (P(),) * 3 + (att + ffn + att + att + ffn)
    out_specs = (rows,) * 4 + (att + ffn + att + att + ffn)
    return jax.shard_map(
        per_device, mesh=mesh, in_specs=in_specs, out_specs=out_specs, check_vma=False
    )
```
